32 devices in a mesh: slab: 4 (over z), filt: 8 (over y, x, core).
Axes of the slice: x: 2, y: 2, z: 4, core: 2. Of those that a mesh axis runs over, the one named last changes fastest.
Arguments:
- features: bfloat16 [16, 256, 64, 128], P('slab', 'filt'), may hold values from -6 to 6
- kernel: bfloat16 [3, 3, 3, 256, 256], P(None, None, None, 'filt'), may hold values from -0.078125 to 0.078125
- bias_vector: float32 [256], replicated, may hold values from -0.6 to 0.6
Outputs:
- activated: bfloat16 [16, 256, 64, 128], P('slab', 'filt')
The draws below stay inside these ranges and needn't reach their ends.
All inputs are finite; a program needn't handle non-finite values.
Results may differ from the reference program's by a relative error of at most 0.005.
Values may be sent and summed in bfloat16 or wider, within the bound.
No kernel may reach another device: no remote copies, remote signals or barrier semaphores. Data moves between devices by JAX's collectives and lax.ppermute only.
A program may use at most 256 MiB of HBM per device.

```python
import jax
import jax.numpy as jnp
from jax import lax

CIN = 256
COUT = 256
Y = 64
X = 128
Z = 16


def block_levels(key, extent, pieces, low, largest):
    factor_of = 1.0
    for dim, blocks in pieces:
        draws = jax.random.uniform(jax.random.fold_in(jax.random.fold_in(key, 6), dim), (blocks,), jnp.float32, low / len(pieces), largest / len(pieces))
        factor_of = factor_of * jnp.repeat(jnp.exp(draws), extent[dim] // blocks).reshape((-1,) + (1,) * (len(extent) - 1 - dim))
    return factor_of


def centred(key, extent, scale, limit, pieces=(), kind=jnp.bfloat16):
    loudness = block_levels(key, extent, pieces, -0.22, 0.18) if pieces else 1.0
    entries = jax.random.normal(key, extent, jnp.float32) * scale * loudness
    return jnp.minimum(jnp.maximum(entries, -limit), limit).astype(kind)


def setup_inputs(seed: int = 0) -> dict:
    key_list = jax.random.split(jax.random.key(seed), 4)
    features = centred(key_list[0], (Z, CIN, Y, X), 1.0, 6.0, ((0, 4), (1, 8)))
    kernel = centred(key_list[1], (3, 3, 3, COUT, CIN), (27 * CIN) ** -0.5, 0.078125, ((3, 8),))
    bias_vector = jnp.clip(jax.random.uniform(key_list[2], (COUT,), jnp.float32, -0.6, 0.6), -0.6, 0.6)
    return dict(features=features, kernel=kernel, bias_vector=bias_vector)


def reference(features, kernel, bias_vector):
    volume = features.astype(jnp.float32).transpose(1, 0, 2, 3)[None]
    filters = kernel.astype(jnp.float32).transpose(3, 4, 0, 1, 2)
    convolved = lax.conv_general_dilated(volume, filters, (1, 1, 1), ((1, 1), (1, 1), (1, 1)), dimension_numbers=("NCDHW", "OIDHW", "NCDHW"), precision=lax.Precision.HIGHEST)
    shifted = convolved[0].transpose(1, 0, 2, 3) + bias_vector[None, :, None, None]
    return jnp.where(shifted > 0, shifted, 0.3 * shifted).astype(jnp.bfloat16)
```

```python
import functools

import jax
import jax.numpy as jnp
from jax import lax
from jax.experimental import pallas as pl
from jax.experimental.pallas import tpu as pltpu
from jax.sharding import PartitionSpec as P

slope = 0.3
PAIR = 2


def neighbour_planes(first, last, axis):
    devices = lax.axis_size(axis)
    up = [(i, i + 1) for i in range(devices - 1)]
    down = [(j, i) for i, j in up]
    return lax.ppermute(last, axis, up), lax.ppermute(first, axis, down)


def conv_kernel(vol_in, before_in, after_in, taps_in, bias_ref, out_ref, vol, taps, vol_sem, edge_sem, taps_sem):
    sources, planes, rows_in, chan, cols = vol_in.shape
    out_sources, out_chan = taps_in.shape[0], taps_in.shape[4]
    rows = rows_in - 2
    total_out = out_sources * out_chan
    copies = []
    for s in range(sources):
        part = pl.ds(s * chan, chan)
        copies.append(pltpu.make_async_copy(vol_in.at[s], vol.at[pl.ds(1, planes), :, part, :], vol_sem.at[s]))
        copies.append(pltpu.make_async_copy(before_in.at[s], vol.at[0, :, part, :], edge_sem.at[0, s]))
        copies.append(pltpu.make_async_copy(after_in.at[s], vol.at[planes + 1, :, part, :], edge_sem.at[1, s]))
    for s in range(out_sources):
        part = pl.ds(s * out_chan, out_chan)
        copies.append(pltpu.make_async_copy(taps_in.at[s], taps.at[:, :, :, part, :], taps_sem.at[s]))
    for copy in copies:
        copy.start()
    for copy in copies:
        copy.wait()

    lane = lax.broadcasted_iota(jnp.int32, (total_out, cols), 1)

    def tile(step, carry):
        plane = step // (rows // PAIR)
        row = (step % (rows // PAIR)) * PAIR
        total = jnp.zeros((3 * total_out, PAIR * cols), jnp.float32)
        for a in range(3):
            for b in range(3):
                piece = jnp.concatenate([vol[plane + a, row + b + r] for r in range(PAIR)], axis=1)
                total = total + jnp.dot(
                    taps[a, b].reshape(3 * total_out, -1), piece, preferred_element_type=jnp.float32
                )
        for r in range(PAIR):
            part = total[:, r * cols : (r + 1) * cols].reshape(3, total_out, cols)
            left = jnp.where(lane == 0, 0.0, pltpu.roll(part[0], 1, 1))
            right = jnp.where(lane == cols - 1, 0.0, pltpu.roll(part[2], cols - 1, 1))
            shifted = part[1] + left + right + bias_ref[...]
            done = jnp.where(shifted > 0, shifted, slope * shifted).astype(jnp.bfloat16)
            out_ref[:, plane, row + r] = done.reshape(out_sources, out_chan, cols)
        return carry

    lax.fori_loop(0, planes * (rows // PAIR), tile, 0)


def convolve(volume, before, after, taps, bias):
    sources, planes, rows_in, chan, cols = volume.shape
    out_sources, out_chan, in_chan = taps.shape[0], taps.shape[4], taps.shape[5]
    total_out = out_sources * out_chan
    rows = rows_in - 2
    wide_bias = jnp.broadcast_to(bias[:, None], (total_out, cols))
    macs = 27 * total_out * in_chan * planes * rows * cols
    any_space = pl.BlockSpec(memory_space=pl.ANY)
    in_vmem = pl.BlockSpec(memory_space=pltpu.VMEM)
    return pl.pallas_call(
        conv_kernel,
        out_shape=jax.ShapeDtypeStruct((out_sources, planes, rows, out_chan, cols), jnp.bfloat16),
        in_specs=[any_space] * 4 + [in_vmem],
        out_specs=in_vmem,
        scratch_shapes=[
            pltpu.VMEM((planes + 2, rows_in, sources * chan, cols), jnp.bfloat16),
            pltpu.VMEM((3, 3, 3, total_out, in_chan), jnp.bfloat16),
            pltpu.SemaphoreType.DMA((sources,)),
            pltpu.SemaphoreType.DMA((2, sources)),
            pltpu.SemaphoreType.DMA((out_sources,)),
        ],
        cost_estimate=pl.CostEstimate(flops=2 * macs, bytes_accessed=10_000_000, transcendentals=0),
        compiler_params=pltpu.CompilerParams(vmem_limit_bytes=48 * 2**20),
    )(volume, before, after, taps, wide_bias)


def body(features, kernel, bias_vector):
    planes, chan, y_cells, cols = features.shape
    out_chan = kernel.shape[3]
    parts = lax.axis_size("filt")
    me = lax.axis_index("filt")
    rows = y_cells // parts
    taps = lax.all_gather(kernel, "filt", axis=0)
    by_row = jnp.pad(features.transpose(0, 2, 1, 3), ((0, 0), (1, 1), (0, 0), (0, 0)))
    blocks = jnp.stack([by_row[:, j * rows : (j + 1) * rows + 2] for j in range(parts)])
    volume = lax.all_to_all(blocks, "filt", 0, 0)
    before, after = neighbour_planes(volume[:, 0], volume[:, -1], "slab")
    if chan % 16:
        volume = volume.transpose(1, 2, 0, 3, 4).reshape(1, planes, rows + 2, parts * chan, cols)
        before = before.transpose(1, 0, 2, 3).reshape(1, rows + 2, parts * chan, cols)
        after = after.transpose(1, 0, 2, 3).reshape(1, rows + 2, parts * chan, cols)
    if out_chan % 16:
        taps = taps.transpose(1, 2, 3, 0, 4, 5).reshape(1, 3, 3, 3, parts * out_chan, -1)
    result = convolve(volume, before, after, taps, bias_vector)
    if out_chan % 16:
        result = result.reshape(planes, rows, parts, out_chan, cols).transpose(2, 0, 1, 3, 4)
    final = jnp.zeros((planes, y_cells, out_chan, cols), jnp.bfloat16)
    for k in range(parts):
        other = me ^ k
        block = lax.dynamic_index_in_dim(result, other, 0, keepdims=False)
        if k:
            block = lax.ppermute(block, "filt", [(i, i ^ k) for i in range(parts)])
        final = lax.dynamic_update_slice_in_dim(final, block, other * rows, 1)
    return final.transpose(0, 2, 1, 3)


def solution(mesh):
    placed = (P("slab", "filt", None, None), P(None, None, None, "filt", None), P())
    return jax.shard_map(
        body, mesh=mesh, in_specs=placed, out_specs=P("slab", "filt", None, None), check_vma=False
    )
```

```python
import functools

import jax
import jax.numpy as jnp
from jax import lax
from jax.experimental import pallas as pl
from jax.experimental.pallas import tpu as pltpu
from jax.sharding import PartitionSpec as P

slope = 0.3
PAIR = 2


def conv_kernel(out_planes, planes, chips, middle_planes, with_edges, *refs):
    refs = list(refs)
    chip_ref = refs.pop(0)
    outer = [refs.pop(0) for _ in range(chips)]
    inner = [refs.pop(0) for _ in range(chips)]
    edges = [refs.pop(0) for _ in range(2)] if with_edges else []
    taps_in, bias_ref, out_ref, vol, taps, vol_sem, edge_sem, taps_sem = refs
    rows_in, chan, cols = outer[0].shape[1:]
    halves, blocks, out_chan = taps_in.shape[0], taps_in.shape[1], taps_in.shape[5]
    total_out = halves * blocks * out_chan
    rows = rows_in - 2
    chip = chip_ref[0]
    copies = []
    for s in range(halves):
        for g in range(blocks):
            part = pl.ds((g * halves + s) * out_chan, out_chan)
            copies.append(pltpu.make_async_copy(taps_in.at[s, g], taps.at[:, :, :, part, :], taps_sem.at[s, g]))
    for k in range(chips):
        part = pl.ds(pl.multiple_of((chip ^ k) * chan, chan), chan)
        copies.append(pltpu.make_async_copy(outer[k].at[0], vol.at[1, :, part, :], vol_sem.at[0, k]))
        copies.append(pltpu.make_async_copy(outer[k].at[1], vol.at[planes, :, part, :], vol_sem.at[1, k]))
        copies.append(pltpu.make_async_copy(inner[k], vol.at[pl.ds(2, middle_planes), :, part, :], vol_sem.at[2, k]))
        for side, edge in enumerate(edges):
            place = (planes + 1) * side
            copies.append(pltpu.make_async_copy(edge.at[k], vol.at[place, :, part, :], edge_sem.at[side, k]))
    for copy in copies:
        copy.start()
    for copy in copies:
        copy.wait()

    lane = lax.broadcasted_iota(jnp.int32, (total_out, cols), 1)
    per_plane = rows // PAIR
    first, stride = out_planes[0], (out_planes[1] - out_planes[0] if len(out_planes) > 1 else 0)

    def tile(step, carry):
        slot = step // per_plane
        plane = first + slot * stride
        row = (step % per_plane) * PAIR
        total = jnp.zeros((3 * total_out, PAIR * cols), jnp.float32)
        for a in range(3):
            for b in range(3):
                piece = jnp.concatenate([vol[plane + a, row + b + r] for r in range(PAIR)], axis=1)
                total = total + jnp.dot(
                    taps[a, b].reshape(3 * total_out, -1), piece, preferred_element_type=jnp.float32
                )
        for r in range(PAIR):
            part = total[:, r * cols : (r + 1) * cols].reshape(3, total_out, cols)
            left = jnp.where(lane == 0, 0.0, pltpu.roll(part[0], 1, 1))
            right = jnp.where(lane == cols - 1, 0.0, pltpu.roll(part[2], cols - 1, 1))
            shifted = part[1] + left + right + bias_ref[...]
            done = jnp.where(shifted > 0, shifted, slope * shifted).astype(jnp.bfloat16)
            out_ref[:, slot, row + r] = done.reshape(out_ref.shape[0], out_ref.shape[3], cols)
        return carry

    lax.fori_loop(0, len(out_planes) * per_plane, tile, 0)


def convolve(out_planes, planes, chip, outer, inner, edges, taps, bias):
    chips = len(outer)
    middle_planes, rows_in, chan, cols = inner[0].shape
    halves, blocks, out_chan, in_chan = taps.shape[0], taps.shape[1], taps.shape[5], taps.shape[6]
    total_out = halves * blocks * out_chan
    rows = rows_in - 2
    wide_bias = jnp.broadcast_to(bias[:, None], (total_out, cols))
    macs = 27 * total_out * in_chan * len(out_planes) * rows * cols
    any_space = pl.BlockSpec(memory_space=pl.ANY)
    in_vmem = pl.BlockSpec(memory_space=pltpu.VMEM)
    in_smem = pl.BlockSpec(memory_space=pltpu.SMEM)
    arrays = [*outer, *inner, *edges, taps]
    return pl.pallas_call(
        functools.partial(conv_kernel, out_planes, planes, chips, middle_planes, bool(edges)),
        out_shape=jax.ShapeDtypeStruct((chips, len(out_planes), rows, total_out // chips, cols), jnp.bfloat16),
        in_specs=[in_smem] + [any_space] * len(arrays) + [in_vmem],
        out_specs=in_vmem,
        scratch_shapes=[
            pltpu.VMEM((planes + 2, rows_in, chips * chan, cols), jnp.bfloat16),
            pltpu.VMEM((3, 3, 3, total_out, in_chan), jnp.bfloat16),
            pltpu.SemaphoreType.DMA((3, chips)),
            pltpu.SemaphoreType.DMA((2, chips)),
            pltpu.SemaphoreType.DMA((halves, blocks)),
        ],
        cost_estimate=pl.CostEstimate(flops=2 * macs, bytes_accessed=10_000_000, transcendentals=0),
        compiler_params=pltpu.CompilerParams(vmem_limit_bytes=48 * 2**20),
    )(chip, *arrays, wide_bias)


def body(features, kernel, bias_vector):
    planes, chan, y_cells, cols = features.shape
    out_chan = kernel.shape[3]
    parts = lax.axis_size("filt")
    slabs = lax.axis_size("slab")
    me = lax.axis_index("filt")
    chips = parts // 2
    chip, core = me // 2, me % 2
    rows = y_cells // parts

    def swap(array, k):
        return lax.ppermute(array, "filt", [(i, i ^ k) for i in range(parts)])

    same_core = [[2 * g + c for g in range(chips)] for c in range(2)]
    pairs = [[2 * g, 2 * g + 1] for g in range(chips)]
    taps = lax.all_gather(kernel, "filt", axis=0, axis_index_groups=same_core)
    taps = lax.all_gather(taps, "filt", axis=0, axis_index_groups=pairs)
    if out_chan % 16:
        taps = taps.transpose(2, 3, 4, 1, 0, 5, 6).reshape(1, 1, 3, 3, 3, parts * out_chan, -1)

    def exchange(piece):
        count = piece.shape[0]
        by_row = jnp.pad(piece.transpose(0, 2, 1, 3), ((0, 0), (1, 1), (0, 0), (0, 0)))
        span = (parts - 2) * rows + rows + 2

        def windows(which):
            cut = lax.dynamic_slice_in_dim(by_row, which * rows, span, 1)
            return jnp.stack([cut[:, 2 * h * rows : 2 * h * rows + rows + 2] for h in range(chips)])

        mine = windows(core)
        theirs = swap(windows(1 - core), 1)
        both = jnp.concatenate(
            [jnp.where(core == 0, mine, theirs), jnp.where(core == 0, theirs, mine)], axis=3
        )
        blocks = [lax.dynamic_index_in_dim(both, chip ^ k, 0, keepdims=False) for k in range(chips)]
        return [block if k == 0 else swap(block, 2 * k) for k, block in enumerate(blocks)]

    outer = exchange(jnp.concatenate([features[:1], features[-1:]]))
    inner = exchange(features[1:-1])
    up = [(i, i + 1) for i in range(slabs - 1)]
    down = [(i + 1, i) for i in range(slabs - 1)]
    before = lax.ppermute(jnp.stack([block[1] for block in outer]), "slab", up)
    after = lax.ppermute(jnp.stack([block[0] for block in outer]), "slab", down)

    chip_array = jnp.full((1,), chip, jnp.int32)
    middle = tuple(range(1, planes - 1))
    ends = (0, planes - 1)

    def send_back(result):
        count = result.shape[1]
        result = result.reshape(chips, count, rows, 2, out_chan, cols)
        final = jnp.zeros((count, y_cells, out_chan, cols), jnp.bfloat16)
        for k in range(parts):
            other = me ^ k
            block = lax.dynamic_slice(
                result, (other // 2, 0, 0, other % 2, 0, 0), (1, count, rows, 1, out_chan, cols)
            ).reshape(count, rows, out_chan, cols)
            if k:
                block = swap(block, k)
            final = lax.dynamic_update_slice_in_dim(final, block, other * rows, 1)
        return final.transpose(0, 2, 1, 3)

    inside = send_back(convolve(middle, planes, chip_array, outer, inner, [], taps, bias_vector))
    outside = send_back(convolve(ends, planes, chip_array, outer, inner, [before, after], taps, bias_vector))
    return jnp.concatenate([outside[:1], inside, outside[1:]])


def solution(mesh):
    placed = (P("slab", "filt", None, None), P(None, None, None, "filt", None), P())
    return jax.shard_map(
        body, mesh=mesh, in_specs=placed, out_specs=P("slab", "filt", None, None), check_vma=False
    )
```

```python
import functools

import jax
import jax.numpy as jnp
from jax import lax
from jax.experimental import pallas as pl
from jax.experimental.pallas import tpu as pltpu
from jax.sharding import PartitionSpec as P

slope = 0.3
PAIR = 2


def conv_kernel(first, stride, count, plan, tap_count, *refs):
    refs = list(refs)
    pieces = [refs.pop(0) for _ in plan]
    tap_parts = [refs.pop(0) for _ in range(tap_count)]
    bias_ref = refs.pop(0)
    outs = refs[:-4]
    vol, taps, vol_sem, taps_sem = refs[-4:]
    rows_in, total_in, cols = vol.shape[1:]
    total_out = taps.shape[3]
    rows = rows_in - 2
    copies = []
    start = 0
    for n, part in enumerate(tap_parts):
        size = part.shape[3]
        copies.append(pltpu.make_async_copy(part, taps.at[:, :, :, pl.ds(start, size), :], taps_sem.at[n]))
        start += size
    for n, (piece, (slot, plane_count)) in enumerate(zip(pieces, plan)):
        chan = piece.shape[3]
        for s in range(piece.shape[0]):
            copies.append(
                pltpu.make_async_copy(
                    piece.at[s], vol.at[pl.ds(slot, plane_count), :, pl.ds(s * chan, chan), :], vol_sem.at[n, s]
                )
            )
    for copy in copies:
        copy.start()
    for copy in copies:
        copy.wait()

    lane = lax.broadcasted_iota(jnp.int32, (total_out, cols), 1)
    per_plane = rows // PAIR
    block = total_out // len(outs)

    def tile(step, carry):
        slot = step // per_plane
        plane = first + slot * stride
        row = (step % per_plane) * PAIR
        total = jnp.zeros((3 * total_out, PAIR * cols), jnp.float32)
        for a in range(3):
            for b in range(3):
                piece = jnp.concatenate([vol[plane + a, row + b + r] for r in range(PAIR)], axis=1)
                total = total + jnp.dot(
                    taps[a, b].reshape(3 * total_out, -1), piece, preferred_element_type=jnp.float32
                )
        for r in range(PAIR):
            part = total[:, r * cols : (r + 1) * cols].reshape(3, total_out, cols)
            left = jnp.where(lane == 0, 0.0, pltpu.roll(part[0], 1, 1))
            right = jnp.where(lane == cols - 1, 0.0, pltpu.roll(part[2], cols - 1, 1))
            shifted = part[1] + left + right + bias_ref[...]
            done = jnp.where(shifted > 0, shifted, slope * shifted).astype(jnp.bfloat16)
            for n, out_ref in enumerate(outs):
                out_ref[slot, row + r] = done[n * block : (n + 1) * block]
        return carry

    lax.fori_loop(0, count * per_plane, tile, 0)


def convolve(first, stride, count, pieces, plan, tap_parts, bias, blocks):
    sources, _, rows_in, chan, cols = pieces[0].shape
    in_chan = tap_parts[0].shape[4]
    total_out = sum(part.shape[3] for part in tap_parts)
    rows = rows_in - 2
    depth = max(slot + n for slot, n in plan)
    wide_bias = jnp.broadcast_to(bias[:, None], (total_out, cols))
    macs = 27 * total_out * in_chan * count * rows * cols
    any_space = pl.BlockSpec(memory_space=pl.ANY)
    in_vmem = pl.BlockSpec(memory_space=pltpu.VMEM)
    return pl.pallas_call(
        functools.partial(conv_kernel, first, stride, count, plan, len(tap_parts)),
        out_shape=[jax.ShapeDtypeStruct((count, rows, total_out // blocks, cols), jnp.bfloat16)] * blocks,
        in_specs=[any_space] * (len(pieces) + len(tap_parts)) + [in_vmem],
        out_specs=[in_vmem] * blocks,
        scratch_shapes=[
            pltpu.VMEM((depth, rows_in, sources * chan, cols), jnp.bfloat16),
            pltpu.VMEM((3, 3, 3, total_out, in_chan), jnp.bfloat16),
            pltpu.SemaphoreType.DMA((len(pieces), sources)),
            pltpu.SemaphoreType.DMA((len(tap_parts),)),
        ],
        cost_estimate=pl.CostEstimate(flops=2 * macs, bytes_accessed=10_000_000, transcendentals=0),
        compiler_params=pltpu.CompilerParams(vmem_limit_bytes=32 * 2**20),
    )(*pieces, *tap_parts, wide_bias)


def body(features, kernel, bias_vector):
    planes, chan, y_cells, cols = features.shape
    out_chan = kernel.shape[3]
    parts = lax.axis_size("filt")
    slabs = lax.axis_size("slab")
    me = lax.axis_index("filt")
    rows = y_cells // parts
    aligned = chan % 16 == 0 and out_chan % 16 == 0
    across = list(range(0, parts, 2))

    def swap(array, k):
        if k == 0:
            return array
        return lax.ppermute(array, "filt", [(i, i ^ k) for i in range(parts)])

    same = [swap(kernel, k) for k in across]
    other = swap(jnp.concatenate(same, axis=0), 1)
    tap_parts = []
    for n, part in enumerate(same):
        tap_parts += [part, other[3 * n : 3 * n + 3]]
    if not aligned:
        tap_parts = [jnp.concatenate(tap_parts, axis=3)]
    order = jnp.stack([me ^ k ^ c for k in across for c in range(2)])
    bias = jnp.take(bias_vector.reshape(parts, out_chan), order, axis=0).reshape(-1)

    def gather_rows(piece):
        by_row = jnp.pad(piece.transpose(0, 2, 1, 3), ((0, 0), (1, 1), (0, 0), (0, 0)))
        blocks = jnp.stack([by_row[:, j * rows : (j + 1) * rows + 2] for j in range(parts)])
        got = lax.all_to_all(blocks, "filt", 0, 0)
        if not aligned:
            got = got.transpose(1, 2, 0, 3, 4).reshape(1, piece.shape[0], rows + 2, parts * chan, cols)
        return got

    def send_back(results):
        count = results[0].shape[0]
        got = [swap(result, k) for result, k in zip(results, across)]
        mine = [block[:, :, :out_chan] for block in got]
        theirs = swap(jnp.stack([block[:, :, out_chan:] for block in got]), 1)
        final = jnp.zeros((count, y_cells, out_chan, cols), jnp.bfloat16)
        for n, k in enumerate(across):
            final = lax.dynamic_update_slice_in_dim(final, mine[n], (me ^ k) * rows, 1)
            final = lax.dynamic_update_slice_in_dim(final, theirs[n], (me ^ k ^ 1) * rows, 1)
        return final.transpose(0, 2, 1, 3)

    up = [(i, i + 1) for i in range(slabs - 1)]
    down = [(i + 1, i) for i in range(slabs - 1)]
    outer = gather_rows(jnp.concatenate([features[:1], features[-1:]]))
    first, last = outer[:, :1], outer[:, 1:]
    after = lax.ppermute(first, "slab", down)
    before = lax.ppermute(last, "slab", up)
    inner = gather_rows(features[1:-1])

    conv = functools.partial(convolve, tap_parts=tap_parts, bias=bias, blocks=len(across))
    middle = conv(0, 1, planes - 2, [first, inner, last], ((0, 1), (1, planes - 2), (planes - 1, 1)))
    inside = send_back(middle)
    ends = conv(
        0, planes - 1, 2, [first, inner, last, before, after],
        ((1, 1), (2, planes - 2), (planes, 1), (0, 1), (planes + 1, 1)),
    )
    outside = send_back(ends)
    return jnp.concatenate([outside[:1], inside, outside[1:]])


def solution(mesh):
    placed = (P("slab", "filt", None, None), P(None, None, None, "filt", None), P())
    return jax.shard_map(
        body, mesh=mesh, in_specs=placed, out_specs=P("slab", "filt", None, None), check_vma=False
    )
```

```python
import functools

import jax
import jax.numpy as jnp
from jax import lax
from jax.experimental import pallas as pl
from jax.experimental.pallas import tpu as pltpu
from jax.sharding import PartitionSpec as P

slope = 0.3
PAIR = 2


def conv_kernel(first, stride, count, plan, piece_count, tap_count, *refs):
    refs = list(refs)
    pieces = [refs.pop(0) for _ in range(piece_count)]
    tap_parts = [refs.pop(0) for _ in range(tap_count)]
    bias_ref = refs.pop(0)
    outs = refs[:-4]
    vol, taps, vol_sem, taps_sem = refs[-4:]
    rows_in, total_in, cols = vol.shape[1:]
    total_out = taps.shape[3]
    rows = rows_in - 2
    copies = []
    for n, part in enumerate(tap_parts):
        groups, size = part.shape[0], part.shape[4]
        for g in range(groups):
            where = pl.ds((g * tap_count + n) * size, size)
            copies.append(pltpu.make_async_copy(part.at[g], taps.at[:, :, :, where, :], taps_sem.at[n, g]))
    for n, (source, begin, slot, plane_count) in enumerate(plan):
        piece = pieces[source]
        chan = piece.shape[3]
        for s in range(piece.shape[0]):
            copies.append(
                pltpu.make_async_copy(
                    piece.at[s, pl.ds(begin, plane_count)],
                    vol.at[pl.ds(slot, plane_count), :, pl.ds(s * chan, chan), :],
                    vol_sem.at[n, s],
                )
            )
    for copy in copies:
        copy.start()
    for copy in copies:
        copy.wait()

    lane = lax.broadcasted_iota(jnp.int32, (total_out, cols), 1)
    per_plane = rows // PAIR
    block = total_out // len(outs)

    def tile(step, carry):
        slot = step // per_plane
        plane = first + slot * stride
        row = (step % per_plane) * PAIR
        total = jnp.zeros((3 * total_out, PAIR * cols), jnp.float32)
        for a in range(3):
            for b in range(3):
                piece = jnp.concatenate([vol[plane + a, row + b + r] for r in range(PAIR)], axis=1)
                total = total + jnp.dot(
                    taps[a, b].reshape(3 * total_out, -1), piece, preferred_element_type=jnp.float32
                )
        for r in range(PAIR):
            part = total[:, r * cols : (r + 1) * cols].reshape(3, total_out, cols)
            left = jnp.where(lane == 0, 0.0, pltpu.roll(part[0], 1, 1))
            right = jnp.where(lane == cols - 1, 0.0, pltpu.roll(part[2], cols - 1, 1))
            shifted = part[1] + left + right + bias_ref[...]
            done = jnp.where(shifted > 0, shifted, slope * shifted).astype(jnp.bfloat16)
            for n, out_ref in enumerate(outs):
                out_ref[slot, row + r] = done[n * block : (n + 1) * block]
        return carry

    lax.fori_loop(0, count * per_plane, tile, 0)


def convolve(first, stride, count, pieces, plan, tap_parts, bias, blocks):
    sources, _, rows_in, chan, cols = pieces[0].shape
    groups, in_chan = tap_parts[0].shape[0], tap_parts[0].shape[5]
    total_out = bias.shape[0]
    rows = rows_in - 2
    depth = max(slot + n for _, _, slot, n in plan)
    wide_bias = jnp.broadcast_to(bias[:, None], (total_out, cols))
    macs = 27 * total_out * in_chan * count * rows * cols
    any_space = pl.BlockSpec(memory_space=pl.ANY)
    in_vmem = pl.BlockSpec(memory_space=pltpu.VMEM)
    return pl.pallas_call(
        functools.partial(conv_kernel, first, stride, count, plan, len(pieces), len(tap_parts)),
        out_shape=[jax.ShapeDtypeStruct((count, rows, total_out // blocks, cols), jnp.bfloat16)] * blocks,
        in_specs=[any_space] * (len(pieces) + len(tap_parts)) + [in_vmem],
        out_specs=[in_vmem] * blocks,
        scratch_shapes=[
            pltpu.VMEM((depth, rows_in, sources * chan, cols), jnp.bfloat16),
            pltpu.VMEM((3, 3, 3, total_out, in_chan), jnp.bfloat16),
            pltpu.SemaphoreType.DMA((len(plan), sources)),
            pltpu.SemaphoreType.DMA((len(tap_parts), groups)),
        ],
        cost_estimate=pl.CostEstimate(flops=2 * macs, bytes_accessed=10_000_000, transcendentals=0),
        compiler_params=pltpu.CompilerParams(vmem_limit_bytes=16 * 2**20),
    )(*pieces, *tap_parts, wide_bias)


def body(features, kernel, bias_vector):
    planes, chan, y_cells, cols = features.shape
    out_chan = kernel.shape[3]
    parts = lax.axis_size("filt")
    slabs = lax.axis_size("slab")
    me = lax.axis_index("filt")
    rows = y_cells // parts
    aligned = chan % 16 == 0 and out_chan % 16 == 0
    across = list(range(0, parts, 2))

    def swap(array, k, axis="filt"):
        if k == 0:
            return array
        return lax.ppermute(array, axis, [(i, i ^ k) for i in range(lax.axis_size(axis))])

    half = out_chan // 2
    odd = lax.axis_index("slab") % 2
    mine = lax.dynamic_slice_in_dim(kernel, odd * half, half, 3)
    mine = jnp.stack([swap(mine, k) for k in across[1:]])
    theirs = swap(mine, 1, "slab")
    rest = jnp.concatenate([jnp.where(odd == 0, mine, theirs), jnp.where(odd == 0, theirs, mine)], axis=4)
    same = jnp.concatenate([kernel[None], rest])
    other = swap(same, 1)
    tap_parts = [same, other]
    if not aligned:
        joined = jnp.stack(tap_parts, axis=1).transpose(2, 3, 4, 0, 1, 5, 6)
        tap_parts = [joined.reshape(1, 3, 3, 3, parts * out_chan, -1)]
    order = jnp.stack([me ^ k ^ c for k in across for c in range(2)])
    bias = jnp.take(bias_vector.reshape(parts, out_chan), order, axis=0).reshape(-1)

    def gather_rows(piece):
        count = piece.shape[0]
        by_row = piece.transpose(0, 2, 1, 3).reshape(count, parts, rows, chan, cols).transpose(1, 0, 2, 3, 4)
        nothing = jnp.zeros((1, count, 1, chan, cols), piece.dtype)
        above = jnp.concatenate([nothing, by_row[:-1, :, -1:]])
        below = jnp.concatenate([by_row[1:, :, :1], nothing])
        got = lax.all_to_all(jnp.concatenate([above, by_row, below], axis=2), "filt", 0, 0)
        if not aligned:
            got = got.transpose(1, 2, 0, 3, 4).reshape(1, count, rows + 2, parts * chan, cols)
        return got

    def send_back(results):
        count = results[0].shape[0]
        got = [swap(result, k) for result, k in zip(results, across)]
        mine = [block[:, :, :out_chan] for block in got]
        theirs = swap(jnp.stack([block[:, :, out_chan:] for block in got]), 1)
        final = jnp.zeros((count, y_cells, out_chan, cols), jnp.bfloat16)
        for n, k in enumerate(across):
            final = lax.dynamic_update_slice_in_dim(final, mine[n], (me ^ k) * rows, 1)
            final = lax.dynamic_update_slice_in_dim(final, theirs[n], (me ^ k ^ 1) * rows, 1)
        return final.transpose(0, 2, 1, 3)

    up = [(i, i + 1) for i in range(slabs - 1)]
    down = [(i + 1, i) for i in range(slabs - 1)]
    outer = gather_rows(jnp.concatenate([features[:1], features[-1:]]))
    inner = gather_rows(features[1:-1])

    after = lax.ppermute(outer[:, :1], "slab", down)
    before = lax.ppermute(outer[:, 1:], "slab", up)

    conv = functools.partial(convolve, tap_parts=tap_parts, bias=bias, blocks=len(across))
    middle = conv(0, 1, planes - 2, [outer, inner], ((0, 0, 0, 1), (1, 0, 1, planes - 2), (0, 1, planes - 1, 1)))
    inside = send_back(middle)
    ends = conv(
        0, planes - 1, 2, [outer, inner, before, after],
        ((0, 0, 1, 1), (1, 0, 2, planes - 2), (0, 1, planes, 1), (2, 0, 0, 1), (3, 0, planes + 1, 1)),
    )
    outside = send_back(ends)
    return jnp.concatenate([outside[:1], inside, outside[1:]])


def solution(mesh):
    placed = (P("slab", "filt", None, None), P(None, None, None, "filt", None), P())
    return jax.shard_map(
        body, mesh=mesh, in_specs=placed, out_specs=P("slab", "filt", None, None), check_vma=False
    )
```

```python
import functools

import jax
import jax.numpy as jnp
from jax import lax
from jax.experimental import pallas as pl
from jax.experimental.pallas import tpu as pltpu
from jax.sharding import PartitionSpec as P

slope = 0.3
PAIR = 2


def conv_kernel(first, stride, count, plan, piece_count, *refs):
    refs = list(refs)
    place_ref = refs.pop(0)
    pieces = [refs.pop(0) for _ in range(piece_count)]
    taps = refs.pop(0)
    bias_ref = refs.pop(0)
    outs = refs[:-2]
    vol, vol_sem = refs[-2:]
    rows_in, total_in, cols = vol.shape[1:]
    total_out = bias_ref.shape[0]
    rows = rows_in - 2
    copies = []
    for n, (source, begin, slot, plane_count) in enumerate(plan):
        piece = pieces[source]
        chan = piece.shape[3]
        for s in range(piece.shape[0]):
            part = pl.ds(s * chan, chan)
            copies.append(
                pltpu.make_async_copy(
                    piece.at[s, pl.ds(begin, plane_count)],
                    vol.at[pl.ds(slot, plane_count), :, part, :],
                    vol_sem.at[n, s],
                )
            )
    for copy in copies:
        copy.start()
    for copy in copies:
        copy.wait()

    lane = lax.broadcasted_iota(jnp.int32, (total_out, cols), 1)
    per_plane = rows // PAIR
    block = total_out // len(outs)
    groups, size = taps.shape[0], taps.shape[4]
    places = [place_ref[g] for g in range(groups)]

    def tile(step, carry):
        slot = step // per_plane
        plane = first + slot * stride
        row = (step % per_plane) * PAIR
        cells = []
        weights = []
        for a in range(3):
            for b in range(3):
                cells.append(jnp.concatenate([vol[plane + a, row + b + r] for r in range(PAIR)], axis=1))
                weights.append(
                    jnp.concatenate(
                        [taps[place, a, b].reshape(3 * size, -1) for place in places], axis=0
                    )
                )
        total = jnp.dot(
            jnp.concatenate(weights, axis=1), jnp.concatenate(cells, axis=0), preferred_element_type=jnp.float32
        )
        for r in range(PAIR):
            part = total[:, r * cols : (r + 1) * cols].reshape(groups, 3, size, cols)
            side = [part[:, c].reshape(total_out, cols) for c in range(3)]
            left = jnp.where(lane == 0, 0.0, pltpu.roll(side[0], 1, 1))
            right = jnp.where(lane == cols - 1, 0.0, pltpu.roll(side[2], cols - 1, 1))
            shifted = side[1] + left + right + bias_ref[...]
            done = jnp.where(shifted > 0, shifted, slope * shifted).astype(jnp.bfloat16)
            for n, out_ref in enumerate(outs):
                out_ref[slot, row + r] = done[n * block : (n + 1) * block]
        return carry

    lax.fori_loop(0, count * per_plane, tile, 0)


def convolve(first, stride, count, places, pieces, plan, taps, bias, blocks):
    rows_in, cols = pieces[0].shape[2], pieces[0].shape[4]
    in_chan = taps.shape[5]
    total_out = bias.shape[0]
    rows = rows_in - 2
    depth = max(slot + n for _, _, slot, n in plan)
    wide_bias = jnp.broadcast_to(bias[:, None], (total_out, cols))
    macs = 27 * total_out * in_chan * count * rows * cols
    any_space = pl.BlockSpec(memory_space=pl.ANY)
    in_vmem = pl.BlockSpec(memory_space=pltpu.VMEM)
    in_smem = pl.BlockSpec(memory_space=pltpu.SMEM)
    return pl.pallas_call(
        functools.partial(conv_kernel, first, stride, count, plan, len(pieces)),
        out_shape=[jax.ShapeDtypeStruct((count, rows, total_out // blocks, cols), jnp.bfloat16)] * blocks,
        in_specs=[in_smem] + [any_space] * len(pieces) + [in_vmem] * 2,
        out_specs=[in_vmem] * blocks,
        scratch_shapes=[
            pltpu.VMEM((depth, rows_in, in_chan, cols), jnp.bfloat16),
            pltpu.SemaphoreType.DMA((len(plan), max(piece.shape[0] for piece in pieces))),
        ],
        cost_estimate=pl.CostEstimate(flops=2 * macs, bytes_accessed=10_000_000, transcendentals=0),
        compiler_params=pltpu.CompilerParams(vmem_limit_bytes=20 * 2**20),
    )(places, *pieces, taps, wide_bias)


def body(features, kernel, bias_vector):
    planes, chan, y_cells, cols = features.shape
    out_chan = kernel.shape[3]
    parts = lax.axis_size("filt")
    slabs = lax.axis_size("slab")
    me = lax.axis_index("filt")
    rows = y_cells // parts
    aligned = chan % 16 == 0 and out_chan % 16 == 0
    across = list(range(0, parts, 2))

    def swap(array, k):
        if k == 0:
            return array
        return lax.ppermute(array, "filt", [(i, i ^ k) for i in range(parts)])

    taps = lax.all_gather(kernel, "filt", axis=0)
    order = jnp.stack([me ^ k ^ c for k in across for c in range(2)])
    bias = jnp.take(bias_vector.reshape(parts, out_chan), order, axis=0).reshape(-1)
    if not aligned:
        taps = jnp.take(taps, order, axis=0).transpose(1, 2, 3, 0, 4, 5)
        taps = taps.reshape(1, 3, 3, 3, parts * out_chan, -1)
        order = jnp.zeros((1,), jnp.int32)

    def gather_rows(piece):
        count = piece.shape[0]
        by_row = piece.transpose(0, 2, 1, 3).reshape(count, parts, rows, chan, cols).transpose(1, 0, 2, 3, 4)
        nothing = jnp.zeros((1, count, 1, chan, cols), piece.dtype)
        above = jnp.concatenate([nothing, by_row[:-1, :, -1:]])
        below = jnp.concatenate([by_row[1:, :, :1], nothing])
        got = lax.all_to_all(jnp.concatenate([above, by_row, below], axis=2), "filt", 0, 0)
        if not aligned:
            got = got.transpose(1, 2, 0, 3, 4).reshape(1, count, rows + 2, parts * chan, cols)
        return got

    def send_back(results):
        count = results[0].shape[0]
        got = [swap(result, k) for result, k in zip(results, across)]
        mine = [block[:, :, :out_chan] for block in got]
        theirs = swap(jnp.stack([block[:, :, out_chan:] for block in got]), 1)
        final = jnp.zeros((count, y_cells, out_chan, cols), jnp.bfloat16)
        for n, k in enumerate(across):
            final = lax.dynamic_update_slice_in_dim(final, mine[n], (me ^ k) * rows, 1)
            final = lax.dynamic_update_slice_in_dim(final, theirs[n], (me ^ k ^ 1) * rows, 1)
        return final.transpose(0, 2, 1, 3)

    up = [(i, i + 1) for i in range(slabs - 1)]
    down = [(i + 1, i) for i in range(slabs - 1)]
    outer = gather_rows(jnp.concatenate([features[:1], features[-1:]]))
    inner = gather_rows(features[1:-1])
    after = lax.ppermute(outer[:, :1], "slab", down)
    before = lax.ppermute(outer[:, 1:], "slab", up)

    def conv(first, stride, count, edges, shift):
        plan = [(0, 0, shift, 1), (1, 0, 1 + shift, planes - 2), (0, 1, planes - 1 + shift, 1)]
        plan += [(2 + n, 0, n * (planes + 1), 1) for n in range(len(edges))]
        return convolve(first, stride, count, order, [outer, inner, *edges], tuple(plan), taps, bias, len(across))

    inside = send_back(conv(0, 1, planes - 2, [], 0))
    outside = send_back(conv(0, planes - 1, 2, [before, after], 1))
    return jnp.concatenate([outside[:1], inside, outside[1:]])


def solution(mesh):
    placed = (P("slab", "filt", None, None), P(None, None, None, "filt", None), P())
    return jax.shard_map(
        body, mesh=mesh, in_specs=placed, out_specs=P("slab", "filt", None, None), check_vma=False
    )
```

```python
import functools

import jax
import jax.numpy as jnp
from jax import lax
from jax.experimental import pallas as pl
from jax.experimental.pallas import tpu as pltpu
from jax.sharding import PartitionSpec as P

slope = 0.3
PAIR = 2


def conv_kernel(first, stride, count, plan, piece_count, tap_count, *refs):
    refs = list(refs)
    chip_ref = refs.pop(0)
    pieces = [refs.pop(0) for _ in range(piece_count)]
    tap_parts = [refs.pop(0) for _ in range(tap_count)]
    bias_ref = refs.pop(0)
    outs = refs[:-2]
    vol, vol_sem = refs[-2:]
    rows_in, total_in, cols = vol.shape[1:]
    total_out = bias_ref.shape[0]
    rows = rows_in - 2
    copies = []
    for n, (source, index, begin, slot, plane_count) in enumerate(plan):
        piece = pieces[source]
        chan = piece.shape[3]
        for s in range(piece.shape[0]):
            place = s if index is None else chip_ref[0] ^ index
            part = pl.ds(pl.multiple_of(place * chan, chan), chan)
            copies.append(
                pltpu.make_async_copy(
                    piece.at[s, pl.ds(begin, plane_count)],
                    vol.at[pl.ds(slot, plane_count), :, part, :],
                    vol_sem.at[n, s],
                )
            )
    for copy in copies:
        copy.start()
    for copy in copies:
        copy.wait()

    lane = lax.broadcasted_iota(jnp.int32, (total_out, cols), 1)
    per_plane = rows // PAIR
    block = total_out // len(outs)
    groups, size = tap_parts[0].shape[0], tap_parts[0].shape[4]

    def tile(step, carry):
        slot = step // per_plane
        plane = first + slot * stride
        row = (step % per_plane) * PAIR
        cells = []
        weights = []
        for a in range(3):
            for b in range(3):
                cells.append(jnp.concatenate([vol[plane + a, row + b + r] for r in range(PAIR)], axis=1))
                weights.append(
                    jnp.concatenate(
                        [part[g, a, b].reshape(3 * size, -1) for g in range(groups) for part in tap_parts], axis=0
                    )
                )
        total = jnp.dot(
            jnp.concatenate(weights, axis=1), jnp.concatenate(cells, axis=0), preferred_element_type=jnp.float32
        )
        for r in range(PAIR):
            part = total[:, r * cols : (r + 1) * cols].reshape(groups * tap_count, 3, size, cols)
            side = [part[:, c].reshape(total_out, cols) for c in range(3)]
            left = jnp.where(lane == 0, 0.0, pltpu.roll(side[0], 1, 1))
            right = jnp.where(lane == cols - 1, 0.0, pltpu.roll(side[2], cols - 1, 1))
            shifted = side[1] + left + right + bias_ref[...]
            done = jnp.where(shifted > 0, shifted, slope * shifted).astype(jnp.bfloat16)
            for n, out_ref in enumerate(outs):
                out_ref[slot, row + r] = done[n * block : (n + 1) * block]
        return carry

    lax.fori_loop(0, count * per_plane, tile, 0)


def convolve(first, stride, count, chip, pieces, plan, tap_parts, bias, blocks):
    rows_in, cols = pieces[0].shape[2], pieces[0].shape[4]
    in_chan = tap_parts[0].shape[5]
    total_out = bias.shape[0]
    rows = rows_in - 2
    depth = max(slot + n for _, _, _, slot, n in plan)
    wide_bias = jnp.broadcast_to(bias[:, None], (total_out, cols))
    macs = 27 * total_out * in_chan * count * rows * cols
    any_space = pl.BlockSpec(memory_space=pl.ANY)
    in_vmem = pl.BlockSpec(memory_space=pltpu.VMEM)
    in_smem = pl.BlockSpec(memory_space=pltpu.SMEM)
    return pl.pallas_call(
        functools.partial(conv_kernel, first, stride, count, plan, len(pieces), len(tap_parts)),
        out_shape=[jax.ShapeDtypeStruct((count, rows, total_out // blocks, cols), jnp.bfloat16)] * blocks,
        in_specs=[in_smem] + [any_space] * len(pieces) + [in_vmem] * (len(tap_parts) + 1),
        out_specs=[in_vmem] * blocks,
        scratch_shapes=[
            pltpu.VMEM((depth, rows_in, in_chan, cols), jnp.bfloat16),
            pltpu.SemaphoreType.DMA((len(plan), max(piece.shape[0] for piece in pieces))),
        ],
        cost_estimate=pl.CostEstimate(flops=2 * macs, bytes_accessed=10_000_000, transcendentals=0),
        compiler_params=pltpu.CompilerParams(vmem_limit_bytes=20 * 2**20),
    )(chip, *pieces, *tap_parts, wide_bias)


def body(features, kernel, bias_vector):
    planes, chan, y_cells, cols = features.shape
    out_chan = kernel.shape[3]
    parts = lax.axis_size("filt")
    slabs = lax.axis_size("slab")
    me = lax.axis_index("filt")
    core = me % 2
    rows = y_cells // parts
    chips = parts // 2
    aligned = chan % 16 == 0 and out_chan % 16 == 0
    across = list(range(0, parts, 2))

    def swap(array, k, axis="filt"):
        if k == 0:
            return array
        return lax.ppermute(array, axis, [(i, i ^ k) for i in range(lax.axis_size(axis))])

    def pack(piece):
        count = piece.shape[0]
        by_row = piece.transpose(0, 2, 1, 3).reshape(count, parts, rows, chan, cols).transpose(1, 0, 2, 3, 4)
        nothing = jnp.zeros((1, count, 1, chan, cols), piece.dtype)
        above = jnp.concatenate([nothing, by_row[:-1, :, -1:]])
        below = jnp.concatenate([by_row[1:, :, :1], nothing])
        return jnp.concatenate([above, by_row, below], axis=2)

    outer_rows = pack(jnp.concatenate([features[:1], features[-1:]]))
    inner_rows = pack(features[1:-1]).reshape(chips, 2, planes - 2, rows + 2, chan, cols)

    fetched = [swap(kernel, k) for k in across]
    outer_rows, inner_rows = lax.optimization_barrier((outer_rows, inner_rows))
    outer = lax.all_to_all(outer_rows, "filt", 0, 0)
    if not aligned:
        outer = outer.transpose(1, 2, 0, 3, 4).reshape(1, 2, rows + 2, parts * chan, cols)

    kept = lax.dynamic_index_in_dim(inner_rows, core, 1, keepdims=False)
    given = swap(lax.dynamic_index_in_dim(inner_rows, 1 - core, 1, keepdims=False), 1)
    both = jnp.concatenate([jnp.where(core == 0, kept, given), jnp.where(core == 0, given, kept)], axis=3)
    outer, both, fetched = lax.optimization_barrier((outer, both, fetched))
    inner = [swap(lax.dynamic_slice_in_dim(both, (me ^ k) // 2, 1, 0), k) for k in across]

    same = jnp.stack(fetched)
    tap_parts = [same, swap(same, 1)]
    if not aligned:
        joined = jnp.stack(tap_parts, axis=1).transpose(2, 3, 4, 0, 1, 5, 6)
        tap_parts = [joined.reshape(1, 3, 3, 3, parts * out_chan, -1)]
    order = jnp.stack([me ^ k ^ c for k in across for c in range(2)])
    bias = jnp.take(bias_vector.reshape(parts, out_chan), order, axis=0).reshape(-1)

    def send_back(results):
        count = results[0].shape[0]
        got = [swap(result, k) for result, k in zip(results, across)]
        mine = [block[:, :, :out_chan] for block in got]
        theirs = swap(jnp.stack([block[:, :, out_chan:] for block in got]), 1)
        final = jnp.zeros((count, y_cells, out_chan, cols), jnp.bfloat16)
        for n, k in enumerate(across):
            final = lax.dynamic_update_slice_in_dim(final, mine[n], (me ^ k) * rows, 1)
            final = lax.dynamic_update_slice_in_dim(final, theirs[n], (me ^ k ^ 1) * rows, 1)
        return final.transpose(0, 2, 1, 3)

    up = [(i, i + 1) for i in range(slabs - 1)]
    down = [(i + 1, i) for i in range(slabs - 1)]
    after = lax.ppermute(outer[:, :1], "slab", down)
    before = lax.ppermute(outer[:, 1:], "slab", up)

    chip = jnp.full((1,), me // 2, jnp.int32)

    def conv(first, stride, count, edges, shift):
        pieces = [outer, *inner, *edges]
        plan = [(0, None, 0, shift, 1), (0, None, 1, planes - 1 + shift, 1)]
        plan += [(1 + k, k, 0, 1 + shift, planes - 2) for k in range(chips)]
        plan += [(1 + chips + n, None, 0, n * (planes + 1), 1) for n in range(len(edges))]
        return convolve(first, stride, count, chip, pieces, tuple(plan), tap_parts, bias, chips)

    inside = send_back(conv(0, 1, planes - 2, [], 0))
    outside = send_back(conv(0, planes - 1, 2, [before, after], 1))
    return jnp.concatenate([outside[:1], inside, outside[1:]])


def solution(mesh):
    placed = (P("slab", "filt", None, None), P(None, None, None, "filt", None), P())
    return jax.shard_map(
        body, mesh=mesh, in_specs=placed, out_specs=P("slab", "filt", None, None), check_vma=False
    )
```

```python
import functools

import jax
import jax.numpy as jnp
from jax import lax
from jax.experimental import pallas as pl
from jax.experimental.pallas import tpu as pltpu
from jax.sharding import PartitionSpec as P

slope = 0.3
PAIR = 2


def cut_kernel(rows, me_ref, vol_ref, nothing_ref, *refs):
    outs, sems = refs[:-2], refs[-2:]
    planes, y_cells = vol_ref.shape[:2]
    parts = y_cells // rows
    main, edge = sems
    me = me_ref[0]

    def moves(out, n, block, source):
        top = block * rows
        return [
            (None, vol_ref.at[source, pl.ds(top, rows)], out.at[:, pl.ds(1, rows)], main.at[n]),
            (block > 0, vol_ref.at[source, pl.ds(jnp.maximum(top - 1, 0), 1)], out.at[:, pl.ds(0, 1)], edge.at[n, 0]),
            (block == 0, nothing_ref, out.at[:, pl.ds(0, 1)], edge.at[n, 0]),
            (
                block < parts - 1,
                vol_ref.at[source, pl.ds(jnp.minimum(top + rows, y_cells - 1), 1)],
                out.at[:, pl.ds(rows + 1, 1)],
                edge.at[n, 1],
            ),
            (block == parts - 1, nothing_ref, out.at[:, pl.ds(rows + 1, 1)], edge.at[n, 1]),
        ]

    work = []
    n = 0
    for source, (kept, given) in ((pl.ds(0, 2), outs[:2]), (pl.ds(2, planes - 2), outs[2:])):
        for k in range(parts // 2):
            for core, out in enumerate((kept, given)):
                work += moves(out.at[k], n, me ^ (2 * k + core), source)
                n += 1
    for act in ("start", "wait"):
        for condition, src, dst, sem in work:
            copy = pltpu.make_async_copy(src, dst, sem)
            if condition is None:
                getattr(copy, act)()
            else:
                pl.when(condition)(getattr(copy, act))


def cut(me, volume, parts):
    planes, y_cells, chan, cols = volume.shape
    rows = y_cells // parts
    count = planes - 2
    any_space = pl.BlockSpec(memory_space=pl.ANY)
    assert count == 2
    shape = jax.ShapeDtypeStruct((parts // 2, 2, rows + 2, chan, cols), volume.dtype)
    return pl.pallas_call(
        functools.partial(cut_kernel, rows),
        out_shape=[shape] * 4,
        in_specs=[pl.BlockSpec(memory_space=pltpu.SMEM), any_space, any_space],
        out_specs=[any_space] * 4,
        scratch_shapes=[pltpu.SemaphoreType.DMA((2 * parts,)), pltpu.SemaphoreType.DMA((2 * parts, 2))],
    )(jnp.full((1,), me, jnp.int32), volume, jnp.zeros((2, 1, chan, cols), volume.dtype))


def conv_kernel(first, stride, count, plan, piece_count, tap_count, *refs):
    refs = list(refs)
    place_ref = refs.pop(0)
    pieces = [refs.pop(0) for _ in range(piece_count)]
    tap_parts = [refs.pop(0) for _ in range(tap_count)]
    bias_ref = refs.pop(0)
    outs = refs[:-2]
    vol, vol_sem = refs[-2:]
    rows_in, total_in, cols = vol.shape[1:]
    total_out = bias_ref.shape[0]
    rows = rows_in - 2
    copies = []
    for n, (source, index, begin, slot, plane_count) in enumerate(plan):
        piece = pieces[source].at[pl.ds(begin, plane_count)]
        into = vol.at[pl.ds(slot, plane_count)]
        chan = piece.shape[2] // (1 if index is None else 2)
        for c in range(piece.shape[2] // chan):
            place = 0 if index is None else place_ref[2 * index + c]
            part = pl.ds(pl.multiple_of(place * chan, chan), chan)
            copies.append(
                pltpu.make_async_copy(piece.at[:, :, pl.ds(c * chan, chan)], into.at[:, :, part], vol_sem.at[n, c])
            )
    for copy in copies:
        copy.start()
    for copy in copies:
        copy.wait()

    lane = lax.broadcasted_iota(jnp.int32, (total_out, cols), 1)
    per_plane = rows // PAIR
    block = total_out // len(outs)
    groups, size = tap_parts[0].shape[0], tap_parts[0].shape[4]

    def tile(step, carry):
        slot = step // per_plane
        plane = first + slot * stride
        row = (step % per_plane) * PAIR
        cells = []
        weights = []
        for a in range(3):
            for b in range(3):
                cells.append(jnp.concatenate([vol[plane + a, row + b + r] for r in range(PAIR)], axis=1))
                weights.append(
                    jnp.concatenate(
                        [part[g, a, b].reshape(3 * size, -1) for g in range(groups) for part in tap_parts], axis=0
                    )
                )
        total = jnp.dot(
            jnp.concatenate(weights, axis=1), jnp.concatenate(cells, axis=0), preferred_element_type=jnp.float32
        )
        for r in range(PAIR):
            part = total[:, r * cols : (r + 1) * cols].reshape(groups * tap_count, 3, size, cols)
            side = [part[:, c].reshape(total_out, cols) for c in range(3)]
            left = jnp.where(lane == 0, 0.0, pltpu.roll(side[0], 1, 1))
            right = jnp.where(lane == cols - 1, 0.0, pltpu.roll(side[2], cols - 1, 1))
            shifted = side[1] + left + right + bias_ref[...]
            done = jnp.where(shifted > 0, shifted, slope * shifted).astype(jnp.bfloat16)
            for n, out_ref in enumerate(outs):
                out_ref[slot, row + r] = done[n * block : (n + 1) * block]
        return carry

    lax.fori_loop(0, count * per_plane, tile, 0)


def convolve(first, stride, count, places, pieces, plan, tap_parts, bias, blocks):
    rows_in, cols = pieces[0].shape[1], pieces[0].shape[3]
    in_chan = tap_parts[0].shape[5]
    total_out = bias.shape[0]
    rows = rows_in - 2
    depth = max(slot + n for _, _, _, slot, n in plan)
    wide_bias = jnp.broadcast_to(bias[:, None], (total_out, cols))
    macs = 27 * total_out * in_chan * count * rows * cols
    any_space = pl.BlockSpec(memory_space=pl.ANY)
    in_vmem = pl.BlockSpec(memory_space=pltpu.VMEM)
    in_smem = pl.BlockSpec(memory_space=pltpu.SMEM)
    return pl.pallas_call(
        functools.partial(conv_kernel, first, stride, count, plan, len(pieces), len(tap_parts)),
        out_shape=[jax.ShapeDtypeStruct((count, rows, total_out // blocks, cols), jnp.bfloat16)] * blocks,
        in_specs=[in_smem] + [any_space] * len(pieces) + [in_vmem] * (len(tap_parts) + 1),
        out_specs=[in_vmem] * blocks,
        scratch_shapes=[
            pltpu.VMEM((depth, rows_in, in_chan, cols), jnp.bfloat16),
            pltpu.SemaphoreType.DMA((len(plan), 2)),
        ],
        cost_estimate=pl.CostEstimate(flops=2 * macs, bytes_accessed=10_000_000, transcendentals=0),
        compiler_params=pltpu.CompilerParams(vmem_limit_bytes=20 * 2**20),
    )(places, *pieces, *tap_parts, wide_bias)


def tie(value, *others):
    return lax.optimization_barrier((value, others))[0]


def body(features, kernel, bias_vector):
    planes, chan, y_cells, cols = features.shape
    out_chan = kernel.shape[3]
    parts = lax.axis_size("filt")
    slabs = lax.axis_size("slab")
    me = lax.axis_index("filt")
    rows = y_cells // parts
    aligned = chan % 16 == 0 and out_chan % 16 == 0
    across = list(range(0, parts, 2))

    def swap(array, k, axis="filt"):
        if k == 0:
            return array
        return lax.ppermute(array, axis, [(i, i ^ k) for i in range(lax.axis_size(axis))])

    half = out_chan // 2
    odd = lax.axis_index("slab") % 2
    mine = lax.dynamic_slice_in_dim(kernel, odd * half, half, 3)
    mine = [swap(mine, k) for k in across[1:]]

    ordered = jnp.concatenate([features[:1], features[-1:], features[1:-1]])
    outer_kept, outer_given, inner_kept, inner_given = cut(me, ordered.transpose(0, 2, 1, 3), parts)
    outer_given = swap(outer_given, 1)
    outer_out = [jnp.concatenate([outer_kept[n], outer_given[n]], axis=2) for n in range(len(across))]
    inner_given = swap(tie(inner_given, outer_given), 1)
    inner_out = [jnp.concatenate([inner_kept[n], inner_given[n]], axis=2) for n in range(len(across))]

    mine = jnp.stack(tie(mine, outer_out))
    theirs = swap(mine, 1, "slab")
    rest = jnp.concatenate([jnp.where(odd == 0, mine, theirs), jnp.where(odd == 0, theirs, mine)], axis=4)
    same = jnp.concatenate([kernel[None], rest])
    other = swap(same, 1)
    tap_parts = [same, other]

    outer = [swap(block, k) for block, k in zip(outer_out, across)]
    inner = [swap(tie(block, got) if k else block, k) for block, got, k in zip(inner_out, outer, across)]
    up = [(i, i + 1) for i in range(slabs - 1)]
    down = [(i + 1, i) for i in range(slabs - 1)]
    after = lax.ppermute(jnp.stack([block[:1] for block in outer]), "slab", down)
    before = lax.ppermute(jnp.stack([block[1:] for block in outer]), "slab", up)
    after = [after[n] for n in range(len(across))]
    before = [before[n] for n in range(len(across))]

    order = jnp.stack([me ^ k ^ c for k in across for c in range(2)])
    bias = jnp.take(bias_vector.reshape(parts, out_chan), order, axis=0).reshape(-1)
    if not aligned:
        joined = jnp.stack(tap_parts, axis=1).transpose(2, 3, 4, 0, 1, 5, 6)
        tap_parts = [joined.reshape(1, 3, 3, 3, parts * out_chan, -1)]

        def settle(blocks):
            count = blocks[0].shape[0]
            found = jnp.stack(blocks).reshape(-1, count, rows + 2, 2, chan, cols).transpose(0, 3, 1, 2, 4, 5)
            found = jnp.take(found.reshape(parts, count, rows + 2, chan, cols), me ^ jnp.arange(parts), axis=0)
            return [found.transpose(1, 2, 0, 3, 4).reshape(count, rows + 2, parts * chan, cols)]

        outer, inner, before, after = settle(outer), settle(inner), settle(before), settle(after)

    def send_back(results):
        count = results[0].shape[0]
        got = [swap(result, k) for result, k in zip(results, across)]
        mine = [block[:, :, :out_chan] for block in got]
        theirs = swap(jnp.stack([block[:, :, out_chan:] for block in got]), 1)
        final = jnp.zeros((count, y_cells, out_chan, cols), jnp.bfloat16)
        for n, k in enumerate(across):
            final = lax.dynamic_update_slice_in_dim(final, mine[n], (me ^ k) * rows, 1)
            final = lax.dynamic_update_slice_in_dim(final, theirs[n], (me ^ k ^ 1) * rows, 1)
        return final.transpose(0, 2, 1, 3)

    def conv(first, stride, count, edges, shift):
        pieces, plan = [], []
        for blocks, moves in [(outer, ((0, shift, 1), (1, planes - 1 + shift, 1))), (inner, ((0, 1 + shift, planes - 2),))] + [
            (edge, ((0, n * (planes + 1), 1),)) for n, edge in enumerate(edges)
        ]:
            for n, block in enumerate(blocks):
                plan += [(len(pieces), n if aligned else None, *move) for move in moves]
                pieces.append(block)
        return convolve(first, stride, count, order, pieces, tuple(plan), tap_parts, bias, len(across))

    inside = send_back(conv(0, 1, planes - 2, [], 0))
    outside = send_back(conv(0, planes - 1, 2, [before, after], 1))
    return jnp.concatenate([outside[:1], inside, outside[1:]])


def solution(mesh):
    placed = (P("slab", "filt", None, None), P(None, None, None, "filt", None), P())
    return jax.shard_map(
        body, mesh=mesh, in_specs=placed, out_specs=P("slab", "filt", None, None), check_vma=False
    )
```

```python
import functools

import jax
import jax.numpy as jnp
from jax import lax
from jax.experimental import pallas as pl
from jax.experimental.pallas import tpu as pltpu
from jax.sharding import PartitionSpec as P

slope = 0.3
PAIR = 2


def cut_kernel(parts, me_ref, vol_ref, *outs):
    planes, y_cells = vol_ref.shape[:2]
    rows = y_cells // parts
    me = me_ref[0]
    for k in range(parts // 2):
        for core in range(2):
            block = me ^ (2 * k + core)
            for plane in range(planes):
                inside = 0 < plane < planes - 1
                out, slot = outs[2 * inside + core], (plane - 1 if inside else min(plane, 1))
                for r in range(rows + 2):
                    row = jnp.clip(block * rows + r - 1, 0, y_cells - 1)
                    line = vol_ref[plane, row]
                    if r == 0:
                        line = jnp.where(block > 0, line, jnp.zeros_like(line))
                    if r == rows + 1:
                        line = jnp.where(block < parts - 1, line, jnp.zeros_like(line))
                    out[k, slot, r] = line


def cut(me, volume, parts):
    planes, y_cells, chan, cols = volume.shape
    rows = y_cells // parts
    shapes = [
        jax.ShapeDtypeStruct((parts // 2, count, rows + 2, chan, cols), volume.dtype) for count in (2, 2, planes - 2, planes - 2)
    ]
    in_vmem = pl.BlockSpec(memory_space=pltpu.VMEM)
    return pl.pallas_call(
        functools.partial(cut_kernel, parts),
        out_shape=shapes,
        in_specs=[pl.BlockSpec(memory_space=pltpu.SMEM), in_vmem],
        out_specs=[in_vmem] * 4,
        compiler_params=pltpu.CompilerParams(vmem_limit_bytes=16 * 2**20),
    )(jnp.full((1,), me, jnp.int32), volume)


def join_kernel(kept_ref, given_ref, *outs):
    chan = kept_ref.shape[3]
    for k, out in enumerate(outs):
        out[:, :, :chan] = kept_ref[k]
        out[:, :, chan:] = given_ref[k]


def join(kept, given):
    chips, count, rows_in, chan, cols = kept.shape
    if chan % 16:
        return [jnp.concatenate([kept[k], given[k]], axis=2) for k in range(chips)]
    in_vmem = pl.BlockSpec(memory_space=pltpu.VMEM)
    return pl.pallas_call(
        join_kernel,
        out_shape=[jax.ShapeDtypeStruct((count, rows_in, 2 * chan, cols), kept.dtype)] * chips,
        in_specs=[in_vmem] * 2,
        out_specs=[in_vmem] * chips,
    )(kept, given)


def edges_kernel(*refs):
    blocks, (first, last) = refs[:-2], refs[-2:]
    for k, block in enumerate(blocks):
        first[k] = block[0]
        last[k] = block[1]


def edges_of(blocks):
    _, rows_in, chan, cols = blocks[0].shape
    in_vmem = pl.BlockSpec(memory_space=pltpu.VMEM)
    return pl.pallas_call(
        edges_kernel,
        out_shape=[jax.ShapeDtypeStruct((len(blocks), rows_in, chan, cols), blocks[0].dtype)] * 2,
        in_specs=[in_vmem] * len(blocks),
        out_specs=[in_vmem] * 2,
    )(*blocks)


def conv_kernel(first, stride, count, plan, piece_count, tap_count, *refs):
    refs = list(refs)
    place_ref = refs.pop(0)
    pieces = [refs.pop(0) for _ in range(piece_count)]
    tap_parts = [refs.pop(0) for _ in range(tap_count)]
    bias_ref = refs.pop(0)
    outs, vol = refs[:-1], refs[-1]
    rows_in, total_in, cols = vol.shape[1:]
    total_out = bias_ref.shape[0]
    rows = rows_in - 2

    def fill(row, carry):
        for source, index, begin, slot, plane_count in plan:
            piece = pieces[source]
            chan = piece.shape[2] // (1 if index is None else 2)
            for c in range(piece.shape[2] // chan):
                place = 0 if index is None else place_ref[2 * index + c]
                part = pl.ds(pl.multiple_of(place * chan, chan), chan)
                for p in range(plane_count):
                    vol[slot + p, row, part, :] = piece[begin + p, row, c * chan : (c + 1) * chan, :]
        return carry

    lax.fori_loop(0, rows_in, fill, 0)

    lane = lax.broadcasted_iota(jnp.int32, (total_out, cols), 1)
    per_plane = rows // PAIR
    block = total_out // len(outs)
    groups, size = tap_parts[0].shape[0], tap_parts[0].shape[4]

    def tile(step, carry):
        slot = step // per_plane
        plane = first + slot * stride
        row = (step % per_plane) * PAIR
        cells = []
        weights = []
        for a in range(3):
            for b in range(3):
                cells.append(jnp.concatenate([vol[plane + a, row + b + r] for r in range(PAIR)], axis=1))
                weights.append(
                    jnp.concatenate(
                        [part[g, a, b].reshape(3 * size, -1) for g in range(groups) for part in tap_parts], axis=0
                    )
                )
        total = jnp.dot(
            jnp.concatenate(weights, axis=1), jnp.concatenate(cells, axis=0), preferred_element_type=jnp.float32
        )
        for r in range(PAIR):
            part = total[:, r * cols : (r + 1) * cols].reshape(groups * tap_count, 3, size, cols)
            side = [part[:, c].reshape(total_out, cols) for c in range(3)]
            left = jnp.where(lane == 0, 0.0, pltpu.roll(side[0], 1, 1))
            right = jnp.where(lane == cols - 1, 0.0, pltpu.roll(side[2], cols - 1, 1))
            shifted = side[1] + left + right + bias_ref[...]
            done = jnp.where(shifted > 0, shifted, slope * shifted).astype(jnp.bfloat16)
            for n, out_ref in enumerate(outs):
                out_ref[slot, row + r] = done[n * block : (n + 1) * block]
        return carry

    lax.fori_loop(0, count * per_plane, tile, 0)


def convolve(first, stride, count, places, pieces, plan, tap_parts, bias, blocks):
    rows_in, cols = pieces[0].shape[1], pieces[0].shape[3]
    in_chan = tap_parts[0].shape[5]
    total_out = bias.shape[0]
    rows = rows_in - 2
    depth = max(slot + n for _, _, _, slot, n in plan)
    wide_bias = jnp.broadcast_to(bias[:, None], (total_out, cols))
    macs = 27 * total_out * in_chan * count * rows * cols
    in_vmem = pl.BlockSpec(memory_space=pltpu.VMEM)
    in_smem = pl.BlockSpec(memory_space=pltpu.SMEM)
    return pl.pallas_call(
        functools.partial(conv_kernel, first, stride, count, plan, len(pieces), len(tap_parts)),
        out_shape=[jax.ShapeDtypeStruct((count, rows, total_out // blocks, cols), jnp.bfloat16)] * blocks,
        in_specs=[in_smem] + [in_vmem] * (len(pieces) + len(tap_parts) + 1),
        out_specs=[in_vmem] * blocks,
        scratch_shapes=[pltpu.VMEM((depth, rows_in, in_chan, cols), jnp.bfloat16)],
        cost_estimate=pl.CostEstimate(flops=2 * macs, bytes_accessed=10_000_000, transcendentals=0),
        compiler_params=pltpu.CompilerParams(vmem_limit_bytes=20 * 2**20),
    )(places, *pieces, *tap_parts, wide_bias)


def tie(value, *others):
    return lax.optimization_barrier((value, others))[0]


def body(features, kernel, bias_vector):
    planes, chan, y_cells, cols = features.shape
    out_chan = kernel.shape[3]
    parts = lax.axis_size("filt")
    slabs = lax.axis_size("slab")
    me = lax.axis_index("filt")
    rows = y_cells // parts
    aligned = chan % 16 == 0 and out_chan % 16 == 0
    across = list(range(0, parts, 2))

    def swap(array, k, axis="filt"):
        if k == 0:
            return array
        return lax.ppermute(array, axis, [(i, i ^ k) for i in range(lax.axis_size(axis))])

    fetched = [swap(kernel, k) for k in (across[:3] if len(across) == 4 else across)]
    outer_kept, outer_given, inner_kept, inner_given = cut(me, features.transpose(0, 2, 1, 3), parts)
    outer_out = join(outer_kept, swap(outer_given, 1))
    inner_out = join(inner_kept, swap(tie(inner_given, outer_out), 1))

    if len(across) == 4:
        half = out_chan // 2
        across_x, across_y = tie(fetched[1:], outer_out)
        far = [swap(across_x[:, :, :, :half], across[2]), swap(across_y[:, :, :, half:], across[1])]
        fetched = [kernel, across_x, across_y, jnp.concatenate(far, axis=3)]
    same = jnp.stack(fetched)
    other = swap(same, 1)
    tap_parts = [same, other]

    outer = [swap(block, k) for block, k in zip(outer_out, across)]
    inner = [swap(tie(block, got, other) if k else block, k) for block, got, k in zip(inner_out, outer, across)]
    up = [(i, i + 1) for i in range(slabs - 1)]
    down = [(i + 1, i) for i in range(slabs - 1)]
    first, last = edges_of(outer)
    after = lax.ppermute(first, "slab", down)
    before = lax.ppermute(last, "slab", up)
    after = [after[n : n + 1] for n in range(len(across))]
    before = [before[n : n + 1] for n in range(len(across))]

    order = jnp.stack([me ^ k ^ c for k in across for c in range(2)])
    bias = jnp.take(bias_vector.reshape(parts, out_chan), order, axis=0).reshape(-1)
    if not aligned:
        joined = jnp.stack(tap_parts, axis=1).transpose(2, 3, 4, 0, 1, 5, 6)
        tap_parts = [joined.reshape(1, 3, 3, 3, parts * out_chan, -1)]

        def settle(blocks):
            count = blocks[0].shape[0]
            found = jnp.stack(blocks).reshape(-1, count, rows + 2, 2, chan, cols).transpose(0, 3, 1, 2, 4, 5)
            found = jnp.take(found.reshape(parts, count, rows + 2, chan, cols), me ^ jnp.arange(parts), axis=0)
            return [found.transpose(1, 2, 0, 3, 4).reshape(count, rows + 2, parts * chan, cols)]

        outer, inner, before, after = settle(outer), settle(inner), settle(before), settle(after)

    def send_back(results):
        count = results[0].shape[0]
        got = [swap(result, k) for result, k in zip(results, across)]
        mine = [block[:, :, :out_chan] for block in got]
        theirs = swap(jnp.stack([block[:, :, out_chan:] for block in got]), 1)
        final = jnp.zeros((count, y_cells, out_chan, cols), jnp.bfloat16)
        for n, k in enumerate(across):
            final = lax.dynamic_update_slice_in_dim(final, mine[n], (me ^ k) * rows, 1)
            final = lax.dynamic_update_slice_in_dim(final, theirs[n], (me ^ k ^ 1) * rows, 1)
        return final.transpose(0, 2, 1, 3)

    def conv(first, stride, count, edges, shift):
        pieces, plan = [], []
        for blocks, moves in [(outer, ((0, shift, 1), (1, planes - 1 + shift, 1))), (inner, ((0, 1 + shift, planes - 2),))] + [
            (edge, ((0, n * (planes + 1), 1),)) for n, edge in enumerate(edges)
        ]:
            for n, block in enumerate(blocks):
                plan += [(len(pieces), n if aligned else None, *move) for move in moves]
                pieces.append(block)
        return convolve(first, stride, count, order, pieces, tuple(plan), tap_parts, bias, len(across))

    inside = send_back(conv(0, 1, planes - 2, [], 0))
    outside = send_back(conv(0, planes - 1, 2, [before, after], 1))
    return jnp.concatenate([outside[:1], inside, outside[1:]])


def solution(mesh):
    placed = (P("slab", "filt", None, None), P(None, None, None, "filt", None), P())
    return jax.shard_map(
        body, mesh=mesh, in_specs=placed, out_specs=P("slab", "filt", None, None), check_vma=False
    )
```

```python
import functools

import jax
import jax.numpy as jnp
from jax import lax
from jax.experimental import pallas as pl
from jax.experimental.pallas import tpu as pltpu
from jax.sharding import PartitionSpec as P

slope = 0.3
ROWS = 4


def cut_kernel(parts, vol_ref, outer, inner):
    planes, y_cells = vol_ref.shape[:2]
    rows = y_cells // parts
    for block in range(parts):
        for r in range(rows + 2):
            row = block * rows + r - 1
            for plane in range(planes):
                line = vol_ref[plane, min(max(row, 0), y_cells - 1)]
                line = line if 0 <= row < y_cells else jnp.zeros_like(line)
                if 0 < plane < planes - 1:
                    inner[block, plane - 1, r] = line
                else:
                    outer[block, min(plane, 1), r] = line


def cut(volume, parts):
    planes, y_cells, chan, cols = volume.shape
    in_vmem = pl.BlockSpec(memory_space=pltpu.VMEM)
    return pl.pallas_call(
        functools.partial(cut_kernel, parts),
        out_shape=[
            jax.ShapeDtypeStruct((parts, count, y_cells // parts + 2, chan, cols), volume.dtype)
            for count in (2, planes - 2)
        ],
        in_specs=[in_vmem],
        out_specs=[in_vmem] * 2,
        compiler_params=pltpu.CompilerParams(vmem_limit_bytes=8 * 2**20),
    )(volume)


def edges_kernel(vol_ref, first, last):
    for s in range(vol_ref.shape[0]):
        for r in range(vol_ref.shape[2]):
            first[s, 0, r] = vol_ref[s, 0, r]
            last[s, 0, r] = vol_ref[s, 1, r]


def edges_of(volume):
    sources, _, rows_in, chan, cols = volume.shape
    in_vmem = pl.BlockSpec(memory_space=pltpu.VMEM)
    return pl.pallas_call(
        edges_kernel,
        out_shape=[jax.ShapeDtypeStruct((sources, 1, rows_in, chan, cols), volume.dtype)] * 2,
        in_specs=[in_vmem],
        out_specs=[in_vmem] * 2,
        compiler_params=pltpu.CompilerParams(vmem_limit_bytes=4 * 2**20),
    )(volume)


def conv_kernel(plan, rows_at_once, pieces_count, tap_count, *refs):
    refs = list(refs)
    pieces = [refs.pop(0) for _ in range(pieces_count)]
    tap_parts = [refs.pop(0) for _ in range(tap_count)]
    bias_ref, outs = refs[0], refs[1:]
    rows_in, cols = pieces[0].shape[2], pieces[0].shape[4]
    rows = rows_in - 2
    total_out = bias_ref.shape[0]
    block = total_out // len(outs)
    groups, size = tap_parts[0].shape[0], tap_parts[0].shape[4]
    lane = lax.broadcasted_iota(jnp.int32, (total_out, cols), 1)

    def tile(slot, row):
        cells = []
        weights = []
        for a, (source, plane) in enumerate(plan[slot]):
            piece = pieces[source]
            lines = [
                jnp.concatenate([piece[s, plane, row + r] for s in range(piece.shape[0])], axis=0)
                for r in range(rows_at_once + 2)
            ]
            for b in range(3):
                cells.append(jnp.concatenate(lines[b : b + rows_at_once], axis=1))
                weights.append(
                    jnp.concatenate(
                        [part[g, a, b].reshape(3 * size, -1) for g in range(groups) for part in tap_parts], axis=0
                    )
                )
        total = jnp.dot(
            jnp.concatenate(weights, axis=1), jnp.concatenate(cells, axis=0), preferred_element_type=jnp.float32
        )
        for r in range(rows_at_once):
            part = total[:, r * cols : (r + 1) * cols].reshape(groups * tap_count, 3, size, cols)
            side = [part[:, c].reshape(total_out, cols) for c in range(3)]
            left = jnp.where(lane == 0, 0.0, pltpu.roll(side[0], 1, 1))
            right = jnp.where(lane == cols - 1, 0.0, pltpu.roll(side[2], cols - 1, 1))
            shifted = side[1] + left + right + bias_ref[...]
            done = jnp.where(shifted > 0, shifted, slope * shifted).astype(jnp.bfloat16)
            for n, out_ref in enumerate(outs):
                out_ref[slot, row + r] = done[n * block : (n + 1) * block]

    for slot in range(len(plan)):

        @pl.loop(0, rows // rows_at_once)
        def _(step):
            tile(slot, step * rows_at_once)


def convolve(plan, pieces, tap_parts, bias, blocks):
    rows, cols = pieces[0].shape[2] - 2, pieces[0].shape[4]
    in_chan = tap_parts[0].shape[5]
    total_out = bias.shape[0]
    wide_bias = jnp.broadcast_to(bias[:, None], (total_out, cols))
    macs = 27 * total_out * in_chan * len(plan) * rows * cols
    in_vmem = pl.BlockSpec(memory_space=pltpu.VMEM)
    shape = jax.ShapeDtypeStruct((len(plan), rows, total_out // blocks, cols), jnp.bfloat16)
    return pl.pallas_call(
        functools.partial(conv_kernel, plan, min(ROWS, rows), len(pieces), len(tap_parts)),
        out_shape=[shape] * blocks,
        in_specs=[in_vmem] * (len(pieces) + len(tap_parts) + 1),
        out_specs=[in_vmem] * blocks,
        cost_estimate=pl.CostEstimate(flops=2 * macs, bytes_accessed=10_000_000, transcendentals=0),
        compiler_params=pltpu.CompilerParams(vmem_limit_bytes=20 * 2**20),
    )(*pieces, *tap_parts, wide_bias)


def body(features, kernel, bias_vector):
    planes, chan, y_cells, cols = features.shape
    out_chan = kernel.shape[3]
    parts = lax.axis_size("filt")
    slabs = lax.axis_size("slab")
    me = lax.axis_index("filt")
    rows = y_cells // parts
    aligned = chan % 16 == 0 and out_chan % 16 == 0
    across = list(range(0, parts, 2))

    def swap(array, k, axis="filt"):
        if k == 0:
            return array
        return lax.ppermute(array, axis, [(i, i ^ k) for i in range(lax.axis_size(axis))])

    same = jnp.stack([swap(kernel, k) for k in across])
    tap_parts = [same, swap(same, 1)]

    outer_rows, inner_rows = cut(features.transpose(0, 2, 1, 3), parts)
    outer = lax.all_to_all(outer_rows, "filt", 0, 0)
    inner = lax.all_to_all(inner_rows, "filt", 0, 0)
    up = [(i, i + 1) for i in range(slabs - 1)]
    down = [(i + 1, i) for i in range(slabs - 1)]
    first, last = edges_of(outer)
    after = lax.ppermute(first, "slab", down)
    before = lax.ppermute(last, "slab", up)

    order = jnp.stack([me ^ k ^ c for k in across for c in range(2)])
    bias = jnp.take(bias_vector.reshape(parts, out_chan), order, axis=0).reshape(-1)
    if not aligned:
        joined = jnp.stack(tap_parts, axis=1).transpose(2, 3, 4, 0, 1, 5, 6)
        tap_parts = [joined.reshape(1, 3, 3, 3, parts * out_chan, -1)]
        outer, inner, before, after = (
            array.transpose(1, 2, 0, 3, 4).reshape(1, -1, rows + 2, parts * chan, cols)
            for array in (outer, inner, before, after)
        )

    def send_back(results):
        count = results[0].shape[0]
        got = [swap(result, k) for result, k in zip(results, across)]
        mine = [block[:, :, :out_chan] for block in got]
        theirs = swap(jnp.stack([block[:, :, out_chan:] for block in got]), 1)
        final = jnp.zeros((count, y_cells, out_chan, cols), jnp.bfloat16)
        for n, k in enumerate(across):
            final = lax.dynamic_update_slice_in_dim(final, mine[n], (me ^ k) * rows, 1)
            final = lax.dynamic_update_slice_in_dim(final, theirs[n], (me ^ k ^ 1) * rows, 1)
        return final.transpose(0, 2, 1, 3)

    blocks = len(across)
    where = [(0, 0)] + [(1, plane) for plane in range(planes - 2)] + [(0, 1)]
    middle = tuple(tuple(where[plane - 1 : plane + 2]) for plane in range(1, planes - 1))
    inside = send_back(convolve(middle, [outer, inner], tap_parts, bias, blocks))
    ends = (((2, 0), *where[:2]), (*where[-2:], (3, 0)))
    outside = send_back(convolve(ends, [outer, inner, before, after], tap_parts, bias, blocks))
    return jnp.concatenate([outside[:1], inside, outside[1:]])


def solution(mesh):
    placed = (P("slab", "filt", None, None), P(None, None, None, "filt", None), P())
    return jax.shard_map(
        body, mesh=mesh, in_specs=placed, out_specs=P("slab", "filt", None, None), check_vma=False
    )
```

```python
import functools

import jax
import jax.numpy as jnp
from jax import lax
from jax.experimental import pallas as pl
from jax.experimental.pallas import tpu as pltpu
from jax.sharding import PartitionSpec as P

slope = 0.3
ROWS = 4


def cut_kernel(parts, vol_ref, outer, inner):
    planes, y_cells = vol_ref.shape[:2]
    rows = y_cells // parts
    for block in range(parts):
        for r in range(rows + 2):
            row = block * rows + r - 1
            for plane in range(planes):
                line = vol_ref[plane, min(max(row, 0), y_cells - 1)]
                line = line if 0 <= row < y_cells else jnp.zeros_like(line)
                if 0 < plane < planes - 1:
                    inner[block, plane - 1, r] = line
                else:
                    outer[block, min(plane, 1), r] = line


def cut(volume, parts):
    planes, y_cells, chan, cols = volume.shape
    in_vmem = pl.BlockSpec(memory_space=pltpu.VMEM)
    return pl.pallas_call(
        functools.partial(cut_kernel, parts),
        out_shape=[
            jax.ShapeDtypeStruct((parts, count, y_cells // parts + 2, chan, cols), volume.dtype)
            for count in (2, planes - 2)
        ],
        in_specs=[in_vmem],
        out_specs=[in_vmem] * 2,
        compiler_params=pltpu.CompilerParams(vmem_limit_bytes=8 * 2**20),
    )(volume)


def edges_kernel(vol_ref, first, last):
    for s in range(vol_ref.shape[0]):
        for r in range(vol_ref.shape[2]):
            first[s, 0, r] = vol_ref[s, 0, r]
            last[s, 0, r] = vol_ref[s, 1, r]


def edges_of(volume):
    sources, _, rows_in, chan, cols = volume.shape
    in_vmem = pl.BlockSpec(memory_space=pltpu.VMEM)
    return pl.pallas_call(
        edges_kernel,
        out_shape=[jax.ShapeDtypeStruct((sources, 1, rows_in, chan, cols), volume.dtype)] * 2,
        in_specs=[in_vmem],
        out_specs=[in_vmem] * 2,
        compiler_params=pltpu.CompilerParams(vmem_limit_bytes=4 * 2**20),
    )(volume)


def conv_kernel(plan, rows_at_once, pieces_count, tap_count, *refs):
    refs = list(refs)
    pieces = [refs.pop(0) for _ in range(pieces_count)]
    tap_parts = [refs.pop(0) for _ in range(tap_count)]
    bias_ref, outs = refs[0], refs[1:]
    rows_in, cols = pieces[0].shape[2], pieces[0].shape[4]
    rows = rows_in - 2
    total_out = bias_ref.shape[0]
    block = total_out // len(outs)
    groups, size = tap_parts[0].shape[0], tap_parts[0].shape[4]
    lane = lax.broadcasted_iota(jnp.int32, (total_out, cols), 1)

    def tile(slot, row):
        cells = []
        weights = []
        for a, (source, plane) in enumerate(plan[slot]):
            piece = pieces[source]
            lines = [
                jnp.concatenate([piece[s, plane, row + r] for s in range(piece.shape[0])], axis=0)
                for r in range(rows_at_once + 2)
            ]
            for b in range(3):
                cells.append(jnp.concatenate(lines[b : b + rows_at_once], axis=1))
                weights.append(
                    jnp.concatenate(
                        [part[g, a, b].reshape(3 * size, -1) for g in range(groups) for part in tap_parts], axis=0
                    )
                )
        total = jnp.dot(
            jnp.concatenate(weights, axis=1), jnp.concatenate(cells, axis=0), preferred_element_type=jnp.float32
        )
        for r in range(rows_at_once):
            part = total[:, r * cols : (r + 1) * cols].reshape(groups * tap_count, 3, size, cols)
            side = [part[:, c].reshape(total_out, cols) for c in range(3)]
            left = jnp.where(lane == 0, 0.0, pltpu.roll(side[0], 1, 1))
            right = jnp.where(lane == cols - 1, 0.0, pltpu.roll(side[2], cols - 1, 1))
            shifted = side[1] + left + right + bias_ref[...]
            done = jnp.where(shifted > 0, shifted, slope * shifted).astype(jnp.bfloat16)
            for n, out_ref in enumerate(outs):
                out_ref[slot, row + r] = done[n * block : (n + 1) * block]

    for slot in range(len(plan)):

        @pl.loop(0, rows // rows_at_once)
        def _(step):
            tile(slot, step * rows_at_once)


def convolve(plan, pieces, tap_parts, bias, blocks):
    rows, cols = pieces[0].shape[2] - 2, pieces[0].shape[4]
    in_chan = tap_parts[0].shape[5]
    total_out = bias.shape[0]
    wide_bias = jnp.broadcast_to(bias[:, None], (total_out, cols))
    macs = 27 * total_out * in_chan * len(plan) * rows * cols
    in_vmem = pl.BlockSpec(memory_space=pltpu.VMEM)
    shape = jax.ShapeDtypeStruct((len(plan), rows, total_out // blocks, cols), jnp.bfloat16)
    return pl.pallas_call(
        functools.partial(conv_kernel, plan, min(ROWS, rows), len(pieces), len(tap_parts)),
        out_shape=[shape] * blocks,
        in_specs=[in_vmem] * (len(pieces) + len(tap_parts) + 1),
        out_specs=[in_vmem] * blocks,
        cost_estimate=pl.CostEstimate(flops=2 * macs, bytes_accessed=10_000_000, transcendentals=0),
        compiler_params=pltpu.CompilerParams(vmem_limit_bytes=20 * 2**20),
    )(*pieces, *tap_parts, wide_bias)


def body(features, kernel, bias_vector):
    planes, chan, y_cells, cols = features.shape
    out_chan = kernel.shape[3]
    parts = lax.axis_size("filt")
    slabs = lax.axis_size("slab")
    me = lax.axis_index("filt")
    rows = y_cells // parts
    aligned = chan % 16 == 0 and out_chan % 16 == 0
    across = list(range(0, parts, 2))

    def swap(array, k, axis="filt"):
        if k == 0:
            return array
        return lax.ppermute(array, axis, [(i, i ^ k) for i in range(lax.axis_size(axis))])

    if len(across) == 4:
        half = out_chan // 2
        by_x, by_y = swap(kernel, across[1]), swap(kernel, across[2])
        far = [swap(by_x[:, :, :, :half], across[2]), swap(by_y[:, :, :, half:], across[1])]
        fetched = [kernel, by_x, by_y, jnp.concatenate(far, axis=3)]
    else:
        fetched = [swap(kernel, k) for k in across]
    same = jnp.stack(fetched)
    tap_parts = [same, swap(same, 1)]

    outer_rows, inner_rows = cut(features.transpose(0, 2, 1, 3), parts)
    outer = lax.all_to_all(outer_rows, "filt", 0, 0)
    inner = lax.all_to_all(inner_rows, "filt", 0, 0)
    arrived = outer
    order = jnp.stack([me ^ k ^ c for k in across for c in range(2)])
    bias = jnp.take(bias_vector.reshape(parts, out_chan), order, axis=0).reshape(-1)
    def settle(array):
        if aligned:
            return array
        return array.transpose(1, 2, 0, 3, 4).reshape(1, -1, rows + 2, parts * chan, cols)

    if not aligned:
        joined = jnp.stack(tap_parts, axis=1).transpose(2, 3, 4, 0, 1, 5, 6)
        tap_parts = [joined.reshape(1, 3, 3, 3, parts * out_chan, -1)]
        outer, inner = settle(outer), settle(inner)

    def send_back(results):
        count = results[0].shape[0]
        got = [swap(result, k) for result, k in zip(results, across)]
        mine = [block[:, :, :out_chan] for block in got]
        theirs = swap(jnp.stack([block[:, :, out_chan:] for block in got]), 1)
        final = jnp.zeros((count, y_cells, out_chan, cols), jnp.bfloat16)
        for n, k in enumerate(across):
            final = lax.dynamic_update_slice_in_dim(final, mine[n], (me ^ k) * rows, 1)
            final = lax.dynamic_update_slice_in_dim(final, theirs[n], (me ^ k ^ 1) * rows, 1)
        return final.transpose(0, 2, 1, 3)

    blocks = len(across)
    where = [(0, 0)] + [(1, plane) for plane in range(planes - 2)] + [(0, 1)]
    middle = tuple(tuple(where[plane - 1 : plane + 2]) for plane in range(1, planes - 1))
    inside = send_back(convolve(middle, [outer, inner], tap_parts, bias, blocks))
    up = [(i, i + 1) for i in range(slabs - 1)]
    down = [(i + 1, i) for i in range(slabs - 1)]
    first, last = edges_of(arrived)
    after = lax.ppermute(first, "slab", down)
    before = lax.ppermute(last, "slab", up)

    ends = (((2, 0), *where[:2]), (*where[-2:], (3, 0)))
    outside = send_back(convolve(ends, [outer, inner, settle(before), settle(after)], tap_parts, bias, blocks))
    whole = jnp.pad(inside, ((1, 1), (0, 0), (0, 0), (0, 0)))
    whole = lax.dynamic_update_slice_in_dim(whole, outside[:1], 0, 0)
    return lax.dynamic_update_slice_in_dim(whole, outside[1:], planes - 1, 0)


def solution(mesh):
    placed = (P("slab", "filt", None, None), P(None, None, None, "filt", None), P())
    return jax.shard_map(
        body, mesh=mesh, in_specs=placed, out_specs=P("slab", "filt", None, None), check_vma=False
    )
```

```python
import functools

import jax
import jax.numpy as jnp
from jax import lax
from jax.experimental import pallas as pl
from jax.experimental.pallas import tpu as pltpu
from jax.sharding import PartitionSpec as P

slope = 0.3
ROWS = 4


def cut_kernel(parts, vol_ref, outer, inner):
    planes, y_cells = vol_ref.shape[:2]
    rows = y_cells // parts
    for block in range(parts):
        for r in range(rows + 2):
            row = block * rows + r - 1
            for plane in range(planes):
                line = vol_ref[plane, min(max(row, 0), y_cells - 1)]
                line = line if 0 <= row < y_cells else jnp.zeros_like(line)
                if 0 < plane < planes - 1:
                    inner[block, plane - 1, r] = line
                else:
                    outer[block, min(plane, 1), r] = line


def cut(volume, parts):
    planes, y_cells, chan, cols = volume.shape
    in_vmem = pl.BlockSpec(memory_space=pltpu.VMEM)
    return pl.pallas_call(
        functools.partial(cut_kernel, parts),
        out_shape=[
            jax.ShapeDtypeStruct((parts, count, y_cells // parts + 2, chan, cols), volume.dtype)
            for count in (2, planes - 2)
        ],
        in_specs=[in_vmem],
        out_specs=[in_vmem] * 2,
        compiler_params=pltpu.CompilerParams(vmem_limit_bytes=8 * 2**20),
    )(volume)


def edges_kernel(vol_ref, first, last):
    for s in range(vol_ref.shape[0]):
        for r in range(vol_ref.shape[2]):
            first[s, 0, r] = vol_ref[s, 0, r]
            last[s, 0, r] = vol_ref[s, 1, r]


def edges_of(volume):
    sources, _, rows_in, chan, cols = volume.shape
    in_vmem = pl.BlockSpec(memory_space=pltpu.VMEM)
    return pl.pallas_call(
        edges_kernel,
        out_shape=[jax.ShapeDtypeStruct((sources, 1, rows_in, chan, cols), volume.dtype)] * 2,
        in_specs=[in_vmem],
        out_specs=[in_vmem] * 2,
        compiler_params=pltpu.CompilerParams(vmem_limit_bytes=4 * 2**20),
    )(volume)


def conv_kernel(plan, rows_at_once, sums_count, pieces_count, tap_count, final, *refs):
    refs = list(refs)
    sums = [refs.pop(0) for _ in range(sums_count)]
    pieces = [refs.pop(0) for _ in range(pieces_count)]
    tap_parts = [refs.pop(0) for _ in range(tap_count)]
    bias_ref, outs = refs[0], refs[1:]
    rows_in, cols = pieces[0].shape[2], pieces[0].shape[4]
    rows = rows_in - 2
    total_out = bias_ref.shape[0]
    block = total_out // len(outs)
    groups, size = tap_parts[0].shape[0], tap_parts[0].shape[4]
    lane = lax.broadcasted_iota(jnp.int32, (total_out, cols), 1)

    def tile(slot, row):
        cells = []
        weights = []
        for a, source, plane in plan[slot]:
            piece = pieces[source]
            lines = [
                jnp.concatenate([piece[s, plane, row + r] for s in range(piece.shape[0])], axis=0)
                for r in range(rows_at_once + 2)
            ]
            for b in range(3):
                cells.append(jnp.concatenate(lines[b : b + rows_at_once], axis=1))
                weights.append(
                    jnp.concatenate(
                        [part[g, a, b].reshape(3 * size, -1) for g in range(groups) for part in tap_parts], axis=0
                    )
                )
        total = jnp.dot(
            jnp.concatenate(weights, axis=1), jnp.concatenate(cells, axis=0), preferred_element_type=jnp.float32
        )
        for r in range(rows_at_once):
            part = total[:, r * cols : (r + 1) * cols].reshape(groups * tap_count, 3, size, cols)
            side = [part[:, c].reshape(total_out, cols) for c in range(3)]
            left = jnp.where(lane == 0, 0.0, pltpu.roll(side[0], 1, 1))
            right = jnp.where(lane == cols - 1, 0.0, pltpu.roll(side[2], cols - 1, 1))
            found = side[1] + left + right
            if not final:
                outs[slot // 2][slot % 2, row + r] = found
                continue
            shifted = found + sums[0][slot, row + r] + bias_ref[...]
            done = jnp.where(shifted > 0, shifted, slope * shifted).astype(jnp.bfloat16)
            for n, out_ref in enumerate(outs):
                out_ref[slot, row + r] = done[n * block : (n + 1) * block]

    for slot in range(len(plan)):

        @pl.loop(0, rows // rows_at_once)
        def _(step):
            tile(slot, step * rows_at_once)


def convolve(plan, sums, pieces, tap_parts, bias, blocks):
    rows, cols = pieces[0].shape[2] - 2, pieces[0].shape[4]
    in_chan = tap_parts[0].shape[5]
    total_out = bias.shape[0]
    wide_bias = jnp.broadcast_to(bias[:, None], (total_out, cols))
    macs = 9 * total_out * in_chan * sum(len(terms) for terms in plan) * rows * cols
    in_vmem = pl.BlockSpec(memory_space=pltpu.VMEM)
    if blocks:
        shapes = [jax.ShapeDtypeStruct((len(plan), rows, total_out // blocks, cols), jnp.bfloat16)] * blocks
    else:
        shapes = [jax.ShapeDtypeStruct((2, rows, total_out, cols), jnp.float32)] * (len(plan) // 2)
    return pl.pallas_call(
        functools.partial(
            conv_kernel, plan, min(ROWS, rows), len(sums), len(pieces), len(tap_parts), bool(blocks)
        ),
        out_shape=shapes,
        in_specs=[in_vmem] * (len(sums) + len(pieces) + len(tap_parts) + 1),
        out_specs=[in_vmem] * len(shapes),
        cost_estimate=pl.CostEstimate(flops=2 * macs, bytes_accessed=10_000_000, transcendentals=0),
        compiler_params=pltpu.CompilerParams(vmem_limit_bytes=20 * 2**20),
    )(*sums, *pieces, *tap_parts, wide_bias)


def body(features, kernel, bias_vector):
    planes, chan, y_cells, cols = features.shape
    out_chan = kernel.shape[3]
    parts = lax.axis_size("filt")
    slabs = lax.axis_size("slab")
    me = lax.axis_index("filt")
    rows = y_cells // parts
    aligned = chan % 16 == 0 and out_chan % 16 == 0
    across = list(range(0, parts, 2))

    def swap(array, k, axis="filt"):
        if k == 0:
            return array
        return lax.ppermute(array, axis, [(i, i ^ k) for i in range(lax.axis_size(axis))])

    if len(across) == 4:
        half = out_chan // 2
        by_x, by_y = swap(kernel, across[1]), swap(kernel, across[2])
        far = [swap(by_x[:, :, :, :half], across[2]), swap(by_y[:, :, :, half:], across[1])]
        fetched = [kernel, by_x, by_y, jnp.concatenate(far, axis=3)]
    else:
        fetched = [swap(kernel, k) for k in across]
    same = jnp.stack(fetched)
    tap_parts = [same, swap(same, 1)]

    outer_rows, inner_rows = cut(features.transpose(0, 2, 1, 3), parts)
    outer = lax.all_to_all(outer_rows, "filt", 0, 0)
    inner = lax.all_to_all(inner_rows, "filt", 0, 0)
    arrived = outer
    order = jnp.stack([me ^ k ^ c for k in across for c in range(2)])
    bias = jnp.take(bias_vector.reshape(parts, out_chan), order, axis=0).reshape(-1)
    def settle(array):
        if aligned:
            return array
        return array.transpose(1, 2, 0, 3, 4).reshape(1, -1, rows + 2, parts * chan, cols)

    if not aligned:
        joined = jnp.stack(tap_parts, axis=1).transpose(2, 3, 4, 0, 1, 5, 6)
        tap_parts = [joined.reshape(1, 3, 3, 3, parts * out_chan, -1)]
        outer, inner = settle(outer), settle(inner)

    def send_back(results):
        count = results[0].shape[0]
        got = [swap(result, k) for result, k in zip(results, across)]
        mine = [block[:, :, :out_chan] for block in got]
        theirs = swap(jnp.stack([block[:, :, out_chan:] for block in got]), 1)
        final = jnp.zeros((count, y_cells, out_chan, cols), jnp.bfloat16)
        for n, k in enumerate(across):
            final = lax.dynamic_update_slice_in_dim(final, mine[n], (me ^ k) * rows, 1)
            final = lax.dynamic_update_slice_in_dim(final, theirs[n], (me ^ k ^ 1) * rows, 1)
        return final.transpose(0, 2, 1, 3)

    blocks = len(across)
    assert planes == 4
    begun = ((0, 0, 0),), ((2, 0, 1),), ((1, 0, 0),), ((1, 0, 1),)
    middle_sums, end_sums = convolve(begun, [], [outer], tap_parts, bias, 0)
    middle = ((1, 0, 0), (2, 0, 1)), ((0, 0, 0), (1, 0, 1))
    inside = send_back(convolve(middle, [middle_sums], [inner], tap_parts, bias, blocks))
    up = [(i, i + 1) for i in range(slabs - 1)]
    down = [(i + 1, i) for i in range(slabs - 1)]
    first, last = edges_of(arrived)
    after = lax.ppermute(first, "slab", down)
    before = lax.ppermute(last, "slab", up)
    ends = ((0, 1, 0), (2, 0, 0)), ((0, 0, 1), (2, 2, 0))
    outside = send_back(
        convolve(ends, [end_sums], [inner, settle(before), settle(after)], tap_parts, bias, blocks)
    )
    inside, outside = lax.optimization_barrier((inside, outside))
    return jnp.concatenate([outside[:1], inside, outside[1:]])


def solution(mesh):
    placed = (P("slab", "filt", None, None), P(None, None, None, "filt", None), P())
    return jax.shard_map(
        body, mesh=mesh, in_specs=placed, out_specs=P("slab", "filt", None, None), check_vma=False
    )
```

```python
import functools

import jax
import jax.numpy as jnp
from jax import lax
from jax.experimental import pallas as pl
from jax.experimental.pallas import tpu as pltpu
from jax.sharding import PartitionSpec as P

slope = 0.3
ROWS = 2


def cut_kernel(parts, vol_ref, outer, inner):
    planes, y_cells = vol_ref.shape[:2]
    rows = y_cells // parts
    for block in range(parts):
        for r in range(rows + 2):
            row = block * rows + r - 1
            for plane in range(planes):
                line = vol_ref[plane, min(max(row, 0), y_cells - 1)]
                line = line if 0 <= row < y_cells else jnp.zeros_like(line)
                if 0 < plane < planes - 1:
                    inner[block, plane - 1, r] = line
                else:
                    outer[block, min(plane, 1), r] = line


def cut(volume, parts):
    planes, y_cells, chan, cols = volume.shape
    in_vmem = pl.BlockSpec(memory_space=pltpu.VMEM)
    return pl.pallas_call(
        functools.partial(cut_kernel, parts),
        out_shape=[
            jax.ShapeDtypeStruct((parts, count, y_cells // parts + 2, chan, cols), volume.dtype)
            for count in (2, planes - 2)
        ],
        in_specs=[in_vmem],
        out_specs=[in_vmem] * 2,
        compiler_params=pltpu.CompilerParams(vmem_limit_bytes=8 * 2**20),
    )(volume)


def edges_kernel(vol_ref, first, last):
    for s in range(vol_ref.shape[0]):
        for r in range(vol_ref.shape[2]):
            first[s, 0, r] = vol_ref[s, 0, r]
            last[s, 0, r] = vol_ref[s, 1, r]


def edges_of(volume):
    sources, _, rows_in, chan, cols = volume.shape
    in_vmem = pl.BlockSpec(memory_space=pltpu.VMEM)
    return pl.pallas_call(
        edges_kernel,
        out_shape=[jax.ShapeDtypeStruct((sources, 1, rows_in, chan, cols), volume.dtype)] * 2,
        in_specs=[in_vmem],
        out_specs=[in_vmem] * 2,
        compiler_params=pltpu.CompilerParams(vmem_limit_bytes=4 * 2**20),
    )(volume)


def conv_kernel(plan, rows_at_once, pieces_count, tap_count, *refs):
    refs = list(refs)
    pieces = [refs.pop(0) for _ in range(pieces_count)]
    tap_parts = [refs.pop(0) for _ in range(tap_count)]
    bias_ref, outs = refs[0], refs[1:]
    rows_in, cols = pieces[0].shape[2], pieces[0].shape[4]
    rows = rows_in - 2
    total_out = bias_ref.shape[0]
    block = total_out // len(outs)
    groups, size = tap_parts[0].shape[0], tap_parts[0].shape[4]
    lane = lax.broadcasted_iota(jnp.int32, (total_out, cols), 1)

    def tile(slot, row):
        total = jnp.zeros((3 * total_out, rows_at_once * cols), jnp.float32)
        for a, (source, plane) in enumerate(plan[slot]):
            piece = pieces[source]
            lines = [
                jnp.concatenate([piece[s, plane, row + r] for s in range(piece.shape[0])], axis=0)
                for r in range(rows_at_once + 2)
            ]
            for b in range(3):
                cells = jnp.concatenate(lines[b : b + rows_at_once], axis=1)
                weights = jnp.concatenate(
                    [part[g, a, b].reshape(3 * size, -1) for g in range(groups) for part in tap_parts], axis=0
                )
                total = total + jnp.dot(weights, cells, preferred_element_type=jnp.float32)
        for r in range(rows_at_once):
            part = total[:, r * cols : (r + 1) * cols].reshape(groups * tap_count, 3, size, cols)
            side = [part[:, c].reshape(total_out, cols) for c in range(3)]
            left = jnp.where(lane == 0, 0.0, pltpu.roll(side[0], 1, 1))
            right = jnp.where(lane == cols - 1, 0.0, pltpu.roll(side[2], cols - 1, 1))
            shifted = side[1] + left + right + bias_ref[...]
            done = jnp.where(shifted > 0, shifted, slope * shifted).astype(jnp.bfloat16)
            for n, out_ref in enumerate(outs):
                out_ref[slot, row + r] = done[n * block : (n + 1) * block]

    for slot in range(len(plan)):

        @pl.loop(0, rows // rows_at_once)
        def _(step):
            tile(slot, step * rows_at_once)


def convolve(plan, pieces, tap_parts, bias, blocks):
    rows, cols = pieces[0].shape[2] - 2, pieces[0].shape[4]
    in_chan = tap_parts[0].shape[5]
    total_out = bias.shape[0]
    wide_bias = jnp.broadcast_to(bias[:, None], (total_out, cols))
    macs = 27 * total_out * in_chan * len(plan) * rows * cols
    in_vmem = pl.BlockSpec(memory_space=pltpu.VMEM)
    shape = jax.ShapeDtypeStruct((len(plan), rows, total_out // blocks, cols), jnp.bfloat16)
    return pl.pallas_call(
        functools.partial(conv_kernel, plan, min(ROWS, rows), len(pieces), len(tap_parts)),
        out_shape=[shape] * blocks,
        in_specs=[in_vmem] * (len(pieces) + len(tap_parts) + 1),
        out_specs=[in_vmem] * blocks,
        cost_estimate=pl.CostEstimate(flops=2 * macs, bytes_accessed=10_000_000, transcendentals=0),
        compiler_params=pltpu.CompilerParams(vmem_limit_bytes=12 * 2**20),
    )(*pieces, *tap_parts, wide_bias)


def body(features, kernel, bias_vector):
    planes, chan, y_cells, cols = features.shape
    out_chan = kernel.shape[3]
    parts = lax.axis_size("filt")
    slabs = lax.axis_size("slab")
    me = lax.axis_index("filt")
    rows = y_cells // parts
    aligned = chan % 16 == 0 and out_chan % 16 == 0
    across = list(range(0, parts, 2))

    def swap(array, k, axis="filt"):
        if k == 0:
            return array
        return lax.ppermute(array, axis, [(i, i ^ k) for i in range(lax.axis_size(axis))])

    if len(across) == 4:
        half = out_chan // 2
        by_x, by_y = swap(kernel, across[1]), swap(kernel, across[2])
        far = [swap(by_x[:, :, :, :half], across[2]), swap(by_y[:, :, :, half:], across[1])]
        fetched = [kernel, by_x, by_y, jnp.concatenate(far, axis=3)]
    else:
        fetched = [swap(kernel, k) for k in across]
    same = jnp.stack(fetched)
    tap_parts = [same, swap(same, 1)]

    outer_rows, inner_rows = cut(features.transpose(0, 2, 1, 3), parts)
    outer = lax.all_to_all(outer_rows, "filt", 0, 0)
    inner = lax.all_to_all(inner_rows, "filt", 0, 0)
    arrived = outer
    order = jnp.stack([me ^ k ^ c for k in across for c in range(2)])
    bias = jnp.take(bias_vector.reshape(parts, out_chan), order, axis=0).reshape(-1)
    def settle(array):
        if aligned:
            return array
        return array.transpose(1, 2, 0, 3, 4).reshape(1, -1, rows + 2, parts * chan, cols)

    if not aligned:
        joined = jnp.stack(tap_parts, axis=1).transpose(2, 3, 4, 0, 1, 5, 6)
        tap_parts = [joined.reshape(1, 3, 3, 3, parts * out_chan, -1)]
        outer, inner = settle(outer), settle(inner)

    def send_back(results):
        count = results[0].shape[0]
        got = [swap(result, k) for result, k in zip(results, across)]
        mine = [block[:, :, :out_chan] for block in got]
        theirs = swap(jnp.stack([block[:, :, out_chan:] for block in got]), 1)
        final = jnp.zeros((count, y_cells, out_chan, cols), jnp.bfloat16)
        for n, k in enumerate(across):
            final = lax.dynamic_update_slice_in_dim(final, mine[n], (me ^ k) * rows, 1)
            final = lax.dynamic_update_slice_in_dim(final, theirs[n], (me ^ k ^ 1) * rows, 1)
        return final.transpose(0, 2, 1, 3)

    blocks = len(across)
    where = [(0, 0)] + [(1, plane) for plane in range(planes - 2)] + [(0, 1)]
    middle = tuple(tuple(where[plane - 1 : plane + 2]) for plane in range(1, planes - 1))
    inside = send_back(convolve(middle, [outer, inner], tap_parts, bias, blocks))
    up = [(i, i + 1) for i in range(slabs - 1)]
    down = [(i + 1, i) for i in range(slabs - 1)]
    first, last = edges_of(arrived)
    after = lax.ppermute(first, "slab", down)
    before = lax.ppermute(last, "slab", up)

    ends = (((2, 0), *where[:2]), (*where[-2:], (3, 0)))
    outside = send_back(convolve(ends, [outer, inner, settle(before), settle(after)], tap_parts, bias, blocks))
    inside, outside = lax.optimization_barrier((inside, outside))
    return jnp.concatenate([outside[:1], inside, outside[1:]])


def solution(mesh):
    placed = (P("slab", "filt", None, None), P(None, None, None, "filt", None), P())
    return jax.shard_map(
        body, mesh=mesh, in_specs=placed, out_specs=P("slab", "filt", None, None), check_vma=False
    )
```

```python
import functools

import jax
import jax.numpy as jnp
from jax import lax
from jax.experimental import pallas as pl
from jax.experimental.pallas import tpu as pltpu
from jax.sharding import PartitionSpec as P

slope = 0.3
ROWS = 2


def cut_kernel(parts, vol_ref, outer, inner):
    planes, y_cells = vol_ref.shape[:2]
    rows = y_cells // parts
    for block in range(parts):
        for r in range(rows + 2):
            row = block * rows + r - 1
            for plane in range(planes):
                line = vol_ref[plane, min(max(row, 0), y_cells - 1)]
                line = line if 0 <= row < y_cells else jnp.zeros_like(line)
                if 0 < plane < planes - 1:
                    inner[block, plane - 1, r] = line
                else:
                    outer[block, min(plane, 1), r] = line


def cut(volume, parts):
    planes, y_cells, chan, cols = volume.shape
    in_vmem = pl.BlockSpec(memory_space=pltpu.VMEM)
    return pl.pallas_call(
        functools.partial(cut_kernel, parts),
        out_shape=[
            jax.ShapeDtypeStruct((parts, count, y_cells // parts + 2, chan, cols), volume.dtype)
            for count in (2, planes - 2)
        ],
        in_specs=[in_vmem],
        out_specs=[in_vmem] * 2,
        compiler_params=pltpu.CompilerParams(vmem_limit_bytes=8 * 2**20),
    )(volume)


def edges_kernel(vol_ref, first, last):
    for s in range(vol_ref.shape[0]):
        for r in range(vol_ref.shape[2]):
            first[s, 0, r] = vol_ref[s, 0, r]
            last[s, 0, r] = vol_ref[s, 1, r]


def edges_of(volume):
    sources, _, rows_in, chan, cols = volume.shape
    in_vmem = pl.BlockSpec(memory_space=pltpu.VMEM)
    return pl.pallas_call(
        edges_kernel,
        out_shape=[jax.ShapeDtypeStruct((sources, 1, rows_in, chan, cols), volume.dtype)] * 2,
        in_specs=[in_vmem],
        out_specs=[in_vmem] * 2,
        compiler_params=pltpu.CompilerParams(vmem_limit_bytes=4 * 2**20),
    )(volume)


def conv_kernel(plan, rows_at_once, sums_count, pieces_count, tap_count, final, *refs):
    refs = list(refs)
    sums = [refs.pop(0) for _ in range(sums_count)]
    pieces = [refs.pop(0) for _ in range(pieces_count)]
    tap_parts = [refs.pop(0) for _ in range(tap_count)]
    bias_ref, outs = refs[0], refs[1:]
    rows_in, cols = pieces[0].shape[2], pieces[0].shape[4]
    rows = rows_in - 2
    total_out = bias_ref.shape[0]
    block = total_out // len(outs)
    groups, size = tap_parts[0].shape[0], tap_parts[0].shape[4]
    lane = lax.broadcasted_iota(jnp.int32, (total_out, cols), 1)

    def tile(slot, row):
        cells = []
        weights = []
        for a, source, plane in plan[slot]:
            piece = pieces[source]
            lines = [
                jnp.concatenate([piece[s, plane, row + r] for s in range(piece.shape[0])], axis=0)
                for r in range(rows_at_once + 2)
            ]
            for b in range(3):
                cells.append(jnp.concatenate(lines[b : b + rows_at_once], axis=1))
                weights.append(
                    jnp.concatenate(
                        [part[g, a, b].reshape(3 * size, -1) for g in range(groups) for part in tap_parts], axis=0
                    )
                )
        total = jnp.dot(
            jnp.concatenate(weights, axis=1), jnp.concatenate(cells, axis=0), preferred_element_type=jnp.float32
        )
        for r in range(rows_at_once):
            part = total[:, r * cols : (r + 1) * cols].reshape(groups * tap_count, 3, size, cols)
            side = [part[:, c].reshape(total_out, cols) for c in range(3)]
            left = jnp.where(lane == 0, 0.0, pltpu.roll(side[0], 1, 1))
            right = jnp.where(lane == cols - 1, 0.0, pltpu.roll(side[2], cols - 1, 1))
            found = side[1] + left + right
            if not final:
                outs[slot // 2][slot % 2, row + r] = found
                continue
            shifted = found + sums[0][slot, row + r] + bias_ref[...]
            done = jnp.where(shifted > 0, shifted, slope * shifted).astype(jnp.bfloat16)
            for n, out_ref in enumerate(outs):
                out_ref[slot, row + r] = done[n * block : (n + 1) * block]

    for slot in range(len(plan)):

        @pl.loop(0, rows // rows_at_once)
        def _(step):
            tile(slot, step * rows_at_once)


def convolve(plan, sums, pieces, tap_parts, bias, blocks):
    rows, cols = pieces[0].shape[2] - 2, pieces[0].shape[4]
    in_chan = tap_parts[0].shape[5]
    total_out = bias.shape[0]
    wide_bias = jnp.broadcast_to(bias[:, None], (total_out, cols))
    macs = 9 * total_out * in_chan * sum(len(terms) for terms in plan) * rows * cols
    in_vmem = pl.BlockSpec(memory_space=pltpu.VMEM)
    if blocks:
        shapes = [jax.ShapeDtypeStruct((len(plan), rows, total_out // blocks, cols), jnp.bfloat16)] * blocks
    else:
        shapes = [jax.ShapeDtypeStruct((2, rows, total_out, cols), jnp.float32)] * (len(plan) // 2)
    return pl.pallas_call(
        functools.partial(
            conv_kernel, plan, min(ROWS, rows), len(sums), len(pieces), len(tap_parts), bool(blocks)
        ),
        out_shape=shapes,
        in_specs=[in_vmem] * (len(sums) + len(pieces) + len(tap_parts) + 1),
        out_specs=[in_vmem] * len(shapes),
        cost_estimate=pl.CostEstimate(flops=2 * macs, bytes_accessed=10_000_000, transcendentals=0),
        compiler_params=pltpu.CompilerParams(vmem_limit_bytes=12 * 2**20),
    )(*sums, *pieces, *tap_parts, wide_bias)


def body(features, kernel, bias_vector):
    planes, chan, y_cells, cols = features.shape
    out_chan = kernel.shape[3]
    parts = lax.axis_size("filt")
    slabs = lax.axis_size("slab")
    me = lax.axis_index("filt")
    rows = y_cells // parts
    aligned = chan % 16 == 0 and out_chan % 16 == 0
    across = list(range(0, parts, 2))

    def swap(array, k, axis="filt"):
        if k == 0:
            return array
        return lax.ppermute(array, axis, [(i, i ^ k) for i in range(lax.axis_size(axis))])


    outer_rows, inner_rows = cut(features.transpose(0, 2, 1, 3), parts)
    fetched = [swap(kernel, k) for k in across]
    fetched = lax.optimization_barrier((fetched, outer_rows))[0]
    same = jnp.stack(fetched)
    tap_parts = [same, swap(same, 1)]
    outer = lax.all_to_all(outer_rows, "filt", 0, 0)
    inner = lax.all_to_all(inner_rows, "filt", 0, 0)
    arrived = outer
    order = jnp.stack([me ^ k ^ c for k in across for c in range(2)])
    bias = jnp.take(bias_vector.reshape(parts, out_chan), order, axis=0).reshape(-1)
    def settle(array):
        if aligned:
            return array
        return array.transpose(1, 2, 0, 3, 4).reshape(1, -1, rows + 2, parts * chan, cols)

    if not aligned:
        joined = jnp.stack(tap_parts, axis=1).transpose(2, 3, 4, 0, 1, 5, 6)
        tap_parts = [joined.reshape(1, 3, 3, 3, parts * out_chan, -1)]
        outer, inner = settle(outer), settle(inner)

    def send_back(results):
        count = results[0].shape[0]
        got = [swap(result, k) for result, k in zip(results, across)]
        mine = [block[:, :, :out_chan] for block in got]
        theirs = swap(jnp.stack([block[:, :, out_chan:] for block in got]), 1)
        final = jnp.zeros((count, y_cells, out_chan, cols), jnp.bfloat16)
        for n, k in enumerate(across):
            final = lax.dynamic_update_slice_in_dim(final, mine[n], (me ^ k) * rows, 1)
            final = lax.dynamic_update_slice_in_dim(final, theirs[n], (me ^ k ^ 1) * rows, 1)
        return final.transpose(0, 2, 1, 3)

    blocks = len(across)
    assert planes == 4
    begun = ((0, 0, 0),), ((2, 0, 1),), ((1, 0, 0),), ((1, 0, 1),)
    middle_sums, end_sums = convolve(begun, [], [outer], tap_parts, bias, 0)
    middle = ((1, 0, 0), (2, 0, 1)), ((0, 0, 0), (1, 0, 1))
    inside = send_back(convolve(middle, [middle_sums], [inner], tap_parts, bias, blocks))
    up = [(i, i + 1) for i in range(slabs - 1)]
    down = [(i + 1, i) for i in range(slabs - 1)]
    first, last = edges_of(arrived)
    after = lax.ppermute(first, "slab", down)
    before = lax.ppermute(last, "slab", up)
    ends = ((0, 1, 0), (2, 0, 0)), ((0, 0, 1), (2, 2, 0))
    outside = send_back(
        convolve(ends, [end_sums], [inner, settle(before), settle(after)], tap_parts, bias, blocks)
    )
    inside, outside = lax.optimization_barrier((inside, outside))
    return jnp.concatenate([outside[:1], inside, outside[1:]])


def solution(mesh):
    placed = (P("slab", "filt", None, None), P(None, None, None, "filt", None), P())
    return jax.shard_map(
        body, mesh=mesh, in_specs=placed, out_specs=P("slab", "filt", None, None), check_vma=False
    )
```

```python
import functools

import jax
import jax.numpy as jnp
from jax import lax
from jax.experimental import pallas as pl
from jax.experimental.pallas import tpu as pltpu
from jax.sharding import PartitionSpec as P

slope = 0.3
ROWS = 4


def cut_kernel(parts, vol_ref, outer, inner):
    planes, y_cells = vol_ref.shape[:2]
    rows = y_cells // parts
    for block in range(parts):
        for r in range(rows + 2):
            row = block * rows + r - 1
            for plane in range(planes):
                line = vol_ref[plane, min(max(row, 0), y_cells - 1)]
                line = line if 0 <= row < y_cells else jnp.zeros_like(line)
                if 0 < plane < planes - 1:
                    inner[block, plane - 1, r] = line
                else:
                    outer[block, min(plane, 1), r] = line


def cut(volume, parts):
    planes, y_cells, chan, cols = volume.shape
    in_vmem = pl.BlockSpec(memory_space=pltpu.VMEM)
    return pl.pallas_call(
        functools.partial(cut_kernel, parts),
        out_shape=[
            jax.ShapeDtypeStruct((parts, count, y_cells // parts + 2, chan, cols), volume.dtype)
            for count in (2, planes - 2)
        ],
        in_specs=[in_vmem],
        out_specs=[in_vmem] * 2,
        compiler_params=pltpu.CompilerParams(vmem_limit_bytes=8 * 2**20),
    )(volume)


def edges_kernel(vol_ref, first, last):
    for s in range(vol_ref.shape[0]):
        for r in range(vol_ref.shape[2]):
            first[s, 0, r] = vol_ref[s, 0, r]
            last[s, 0, r] = vol_ref[s, 1, r]


def edges_of(volume):
    sources, _, rows_in, chan, cols = volume.shape
    in_vmem = pl.BlockSpec(memory_space=pltpu.VMEM)
    return pl.pallas_call(
        edges_kernel,
        out_shape=[jax.ShapeDtypeStruct((sources, 1, rows_in, chan, cols), volume.dtype)] * 2,
        in_specs=[in_vmem],
        out_specs=[in_vmem] * 2,
        compiler_params=pltpu.CompilerParams(vmem_limit_bytes=4 * 2**20),
    )(volume)


def conv_kernel(plan, rows_at_once, sums_count, pieces_count, tap_count, final, *refs):
    refs = list(refs)
    sums = [refs.pop(0) for _ in range(sums_count)]
    pieces = [refs.pop(0) for _ in range(pieces_count)]
    tap_parts = [refs.pop(0) for _ in range(tap_count)]
    bias_ref, outs, store, sems = refs[0], refs[1:-2], refs[-2], refs[-1]
    rows_in, cols = pieces[0].shape[2], pieces[0].shape[4]
    rows = rows_in - 2
    total_out = bias_ref.shape[0]
    block = total_out // len(outs)
    groups, size = tap_parts[0].shape[0], tap_parts[0].shape[4]
    lane = lax.broadcasted_iota(jnp.int32, (total_out, cols), 1)

    def fetch(slot):
        return pltpu.make_async_copy(sums[0].at[slot], store.at[slot], sems.at[slot, 0])

    def put(slot, step):
        part = pl.ds(step * rows_at_once, rows_at_once)
        return pltpu.make_async_copy(store.at[slot, part], outs[slot // 2].at[slot % 2, part], sems.at[slot, step])

    if final:
        for slot in range(len(plan)):
            fetch(slot).start()

    def tile(slot, step):
        row = step * rows_at_once
        cells = []
        weights = []
        for a, source, plane in plan[slot]:
            piece = pieces[source]
            lines = [
                jnp.concatenate([piece[s, plane, row + r] for s in range(piece.shape[0])], axis=0)
                for r in range(rows_at_once + 2)
            ]
            for b in range(3):
                cells.append(jnp.concatenate(lines[b : b + rows_at_once], axis=1))
                weights.append(
                    jnp.concatenate(
                        [part[g, a, b].reshape(3 * size, -1) for g in range(groups) for part in tap_parts], axis=0
                    )
                )
        total = jnp.dot(
            jnp.concatenate(weights, axis=1), jnp.concatenate(cells, axis=0), preferred_element_type=jnp.float32
        )
        if final:
            pl.when(step == 0)(fetch(slot).wait)
        for r in range(rows_at_once):
            part = total[:, r * cols : (r + 1) * cols].reshape(groups * tap_count, 3, size, cols)
            side = [part[:, c].reshape(total_out, cols) for c in range(3)]
            left = jnp.where(lane == 0, 0.0, pltpu.roll(side[0], 1, 1))
            right = jnp.where(lane == cols - 1, 0.0, pltpu.roll(side[2], cols - 1, 1))
            found = side[1] + left + right
            if not final:
                store[slot, row + r] = found
                continue
            shifted = found + store[slot, row + r] + bias_ref[...]
            done = jnp.where(shifted > 0, shifted, slope * shifted).astype(jnp.bfloat16)
            for n, out_ref in enumerate(outs):
                out_ref[slot, row + r] = done[n * block : (n + 1) * block]
        if not final:
            put(slot, step).start()

    for slot in range(len(plan)):

        @pl.loop(0, rows // rows_at_once)
        def _(step):
            tile(slot, step)

    if not final:
        for slot in range(len(plan)):
            for step in range(rows // rows_at_once):
                put(slot, step).wait()


def convolve(plan, sums, pieces, tap_parts, bias, blocks):
    rows, cols = pieces[0].shape[2] - 2, pieces[0].shape[4]
    in_chan = tap_parts[0].shape[5]
    total_out = bias.shape[0]
    wide_bias = jnp.broadcast_to(bias[:, None], (total_out, cols))
    macs = 9 * total_out * in_chan * sum(len(terms) for terms in plan) * rows * cols
    in_vmem = pl.BlockSpec(memory_space=pltpu.VMEM)
    in_hbm = pl.BlockSpec(memory_space=pltpu.HBM)
    steps = rows // min(ROWS, rows)
    if blocks:
        shapes = [jax.ShapeDtypeStruct((len(plan), rows, total_out // blocks, cols), jnp.bfloat16)] * blocks
    else:
        shapes = [jax.ShapeDtypeStruct((2, rows, total_out, cols), jnp.float32)] * (len(plan) // 2)
    return pl.pallas_call(
        functools.partial(
            conv_kernel, plan, min(ROWS, rows), len(sums), len(pieces), len(tap_parts), bool(blocks)
        ),
        out_shape=shapes,
        in_specs=[in_hbm] * len(sums) + [in_vmem] * (len(pieces) + len(tap_parts) + 1),
        out_specs=[in_vmem if blocks else in_hbm] * len(shapes),
        scratch_shapes=[
            pltpu.VMEM((len(plan), rows, total_out, cols), jnp.float32),
            pltpu.SemaphoreType.DMA((len(plan), steps)),
        ],
        cost_estimate=pl.CostEstimate(flops=2 * macs, bytes_accessed=10_000_000, transcendentals=0),
        compiler_params=pltpu.CompilerParams(vmem_limit_bytes=16 * 2**20),
    )(*sums, *pieces, *tap_parts, wide_bias)


def body(features, kernel, bias_vector):
    planes, chan, y_cells, cols = features.shape
    out_chan = kernel.shape[3]
    parts = lax.axis_size("filt")
    slabs = lax.axis_size("slab")
    me = lax.axis_index("filt")
    rows = y_cells // parts
    aligned = chan % 16 == 0 and out_chan % 16 == 0
    across = list(range(0, parts, 2))

    def swap(array, k, axis="filt"):
        if k == 0:
            return array
        return lax.ppermute(array, axis, [(i, i ^ k) for i in range(lax.axis_size(axis))])


    outer_rows, inner_rows = cut(features.transpose(0, 2, 1, 3), parts)
    fetched = [swap(kernel, k) for k in across]
    fetched = lax.optimization_barrier((fetched, outer_rows))[0]
    same = jnp.stack(fetched)
    tap_parts = [same, swap(same, 1)]
    outer = lax.all_to_all(outer_rows, "filt", 0, 0)
    inner = lax.all_to_all(inner_rows, "filt", 0, 0)
    arrived = outer
    order = jnp.stack([me ^ k ^ c for k in across for c in range(2)])
    bias = jnp.take(bias_vector.reshape(parts, out_chan), order, axis=0).reshape(-1)
    def settle(array):
        if aligned:
            return array
        return array.transpose(1, 2, 0, 3, 4).reshape(1, -1, rows + 2, parts * chan, cols)

    if not aligned:
        joined = jnp.stack(tap_parts, axis=1).transpose(2, 3, 4, 0, 1, 5, 6)
        tap_parts = [joined.reshape(1, 3, 3, 3, parts * out_chan, -1)]
        outer, inner = settle(outer), settle(inner)

    def send_back(results):
        count = results[0].shape[0]
        got = [swap(result, k) for result, k in zip(results, across)]
        mine = [block[:, :, :out_chan] for block in got]
        theirs = swap(jnp.stack([block[:, :, out_chan:] for block in got]), 1)
        final = jnp.zeros((count, y_cells, out_chan, cols), jnp.bfloat16)
        for n, k in enumerate(across):
            final = lax.dynamic_update_slice_in_dim(final, mine[n], (me ^ k) * rows, 1)
            final = lax.dynamic_update_slice_in_dim(final, theirs[n], (me ^ k ^ 1) * rows, 1)
        return final.transpose(0, 2, 1, 3)

    blocks = len(across)
    assert planes == 4
    begun = ((0, 0, 0),), ((2, 0, 1),), ((1, 0, 0),), ((1, 0, 1),)
    middle_sums, end_sums = convolve(begun, [], [outer], tap_parts, bias, 0)
    middle = ((1, 0, 0), (2, 0, 1)), ((0, 0, 0), (1, 0, 1))
    inside = send_back(convolve(middle, [middle_sums], [inner], tap_parts, bias, blocks))
    up = [(i, i + 1) for i in range(slabs - 1)]
    down = [(i + 1, i) for i in range(slabs - 1)]
    first, last = edges_of(arrived)
    after = lax.ppermute(first, "slab", down)
    before = lax.ppermute(last, "slab", up)
    ends = ((0, 1, 0), (2, 0, 0)), ((0, 0, 1), (2, 2, 0))
    outside = send_back(
        convolve(ends, [end_sums], [inner, settle(before), settle(after)], tap_parts, bias, blocks)
    )
    inside, outside = lax.optimization_barrier((inside, outside))
    return jnp.concatenate([outside[:1], inside, outside[1:]])


def solution(mesh):
    placed = (P("slab", "filt", None, None), P(None, None, None, "filt", None), P())
    return jax.shard_map(
        body, mesh=mesh, in_specs=placed, out_specs=P("slab", "filt", None, None), check_vma=False
    )
```

```python
import functools

import jax
import jax.numpy as jnp
from jax import lax
from jax.experimental import pallas as pl
from jax.experimental.pallas import tpu as pltpu
from jax.sharding import PartitionSpec as P

slope = 0.3
ROWS = 4


def cut_kernel(parts, vol_ref, outer, inner):
    planes, y_cells = vol_ref.shape[:2]
    rows = y_cells // parts
    for block in range(parts):
        for r in range(rows + 2):
            row = block * rows + r - 1
            for plane in range(planes):
                line = vol_ref[plane, min(max(row, 0), y_cells - 1)]
                line = line if 0 <= row < y_cells else jnp.zeros_like(line)
                if 0 < plane < planes - 1:
                    inner[block, plane - 1, r] = line
                else:
                    outer[block, min(plane, 1), r] = line


def cut(volume, parts):
    planes, y_cells, chan, cols = volume.shape
    in_vmem = pl.BlockSpec(memory_space=pltpu.VMEM)
    return pl.pallas_call(
        functools.partial(cut_kernel, parts),
        out_shape=[
            jax.ShapeDtypeStruct((parts, count, y_cells // parts + 2, chan, cols), volume.dtype)
            for count in (2, planes - 2)
        ],
        in_specs=[in_vmem],
        out_specs=[in_vmem] * 2,
        compiler_params=pltpu.CompilerParams(vmem_limit_bytes=8 * 2**20),
    )(volume)


def edges_kernel(vol_ref, first, last):
    for s in range(vol_ref.shape[0]):
        for r in range(vol_ref.shape[2]):
            first[s, 0, r] = vol_ref[s, 0, r]
            last[s, 0, r] = vol_ref[s, 1, r]


def edges_of(volume):
    sources, _, rows_in, chan, cols = volume.shape
    in_vmem = pl.BlockSpec(memory_space=pltpu.VMEM)
    return pl.pallas_call(
        edges_kernel,
        out_shape=[jax.ShapeDtypeStruct((sources, 1, rows_in, chan, cols), volume.dtype)] * 2,
        in_specs=[in_vmem],
        out_specs=[in_vmem] * 2,
        compiler_params=pltpu.CompilerParams(vmem_limit_bytes=4 * 2**20),
    )(volume)


def conv_kernel(plan, rows_at_once, pieces_count, tap_count, *refs):
    refs = list(refs)
    pieces = [refs.pop(0) for _ in range(pieces_count)]
    tap_parts = [refs.pop(0) for _ in range(tap_count)]
    bias_ref, outs = refs[0], refs[1:]
    rows_in, cols = pieces[0].shape[2], pieces[0].shape[4]
    rows = rows_in - 2
    total_out = bias_ref.shape[0]
    block = total_out // len(outs)
    groups, size = tap_parts[0].shape[0], tap_parts[0].shape[4]
    lane = lax.broadcasted_iota(jnp.int32, (total_out, cols), 1)

    def tile(slot, row):
        cells = []
        weights = []
        for a, (source, plane) in enumerate(plan[slot]):
            piece = pieces[source]
            lines = [
                jnp.concatenate([piece[s, plane, row + r] for s in range(piece.shape[0])], axis=0)
                for r in range(rows_at_once + 2)
            ]
            for b in range(3):
                cells.append(jnp.concatenate(lines[b : b + rows_at_once], axis=1))
                weights.append(
                    jnp.concatenate(
                        [part[g, a, b].reshape(3 * size, -1) for g in range(groups) for part in tap_parts], axis=0
                    )
                )
        total = jnp.dot(
            jnp.concatenate(weights, axis=1), jnp.concatenate(cells, axis=0), preferred_element_type=jnp.float32
        )
        for r in range(rows_at_once):
            part = total[:, r * cols : (r + 1) * cols].reshape(groups * tap_count, 3, size, cols)
            side = [part[:, c].reshape(total_out, cols) for c in range(3)]
            left = jnp.where(lane == 0, 0.0, pltpu.roll(side[0], 1, 1))
            right = jnp.where(lane == cols - 1, 0.0, pltpu.roll(side[2], cols - 1, 1))
            shifted = side[1] + left + right + bias_ref[...]
            done = jnp.where(shifted > 0, shifted, slope * shifted).astype(jnp.bfloat16)
            for n, out_ref in enumerate(outs):
                out_ref[slot, row + r] = done[n * block : (n + 1) * block]

    for slot in range(len(plan)):
        for row in range(0, rows, rows_at_once):
            tile(slot, row)


def convolve(plan, pieces, tap_parts, bias, blocks):
    rows, cols = pieces[0].shape[2] - 2, pieces[0].shape[4]
    in_chan = tap_parts[0].shape[5]
    total_out = bias.shape[0]
    wide_bias = jnp.broadcast_to(bias[:, None], (total_out, cols))
    macs = 27 * total_out * in_chan * len(plan) * rows * cols
    in_vmem = pl.BlockSpec(memory_space=pltpu.VMEM)
    shape = jax.ShapeDtypeStruct((len(plan), rows, total_out // blocks, cols), jnp.bfloat16)
    return pl.pallas_call(
        functools.partial(conv_kernel, plan, min(ROWS, rows), len(pieces), len(tap_parts)),
        out_shape=[shape] * blocks,
        in_specs=[in_vmem] * (len(pieces) + len(tap_parts) + 1),
        out_specs=[in_vmem] * blocks,
        cost_estimate=pl.CostEstimate(flops=2 * macs, bytes_accessed=10_000_000, transcendentals=0),
        compiler_params=pltpu.CompilerParams(vmem_limit_bytes=16 * 2**20),
    )(*pieces, *tap_parts, wide_bias)


def body(features, kernel, bias_vector):
    planes, chan, y_cells, cols = features.shape
    out_chan = kernel.shape[3]
    parts = lax.axis_size("filt")
    slabs = lax.axis_size("slab")
    me = lax.axis_index("filt")
    rows = y_cells // parts
    aligned = chan % 16 == 0 and out_chan % 16 == 0
    across = list(range(0, parts, 2))

    def swap(array, k, axis="filt"):
        if k == 0:
            return array
        return lax.ppermute(array, axis, [(i, i ^ k) for i in range(lax.axis_size(axis))])

    if len(across) == 4:
        half = out_chan // 2
        by_x, by_y = swap(kernel, across[1]), swap(kernel, across[2])
        far = [swap(by_x[:, :, :, :half], across[2]), swap(by_y[:, :, :, half:], across[1])]
        fetched = [kernel, by_x, by_y, jnp.concatenate(far, axis=3)]
    else:
        fetched = [swap(kernel, k) for k in across]
    same = jnp.stack(fetched)
    tap_parts = [same, swap(same, 1)]

    outer_rows, inner_rows = cut(features.transpose(0, 2, 1, 3), parts)
    outer = lax.all_to_all(outer_rows, "filt", 0, 0)
    inner = lax.all_to_all(inner_rows, "filt", 0, 0)
    arrived = outer
    order = jnp.stack([me ^ k ^ c for k in across for c in range(2)])
    bias = jnp.take(bias_vector.reshape(parts, out_chan), order, axis=0).reshape(-1)
    def settle(array):
        if aligned:
            return array
        return array.transpose(1, 2, 0, 3, 4).reshape(1, -1, rows + 2, parts * chan, cols)

    if not aligned:
        joined = jnp.stack(tap_parts, axis=1).transpose(2, 3, 4, 0, 1, 5, 6)
        tap_parts = [joined.reshape(1, 3, 3, 3, parts * out_chan, -1)]
        outer, inner = settle(outer), settle(inner)

    def send_back(results):
        count = results[0].shape[0]
        got = [swap(result, k) for result, k in zip(results, across)]
        mine = [block[:, :, :out_chan] for block in got]
        theirs = swap(jnp.stack([block[:, :, out_chan:] for block in got]), 1)
        final = jnp.zeros((count, y_cells, out_chan, cols), jnp.bfloat16)
        for n, k in enumerate(across):
            final = lax.dynamic_update_slice_in_dim(final, mine[n], (me ^ k) * rows, 1)
            final = lax.dynamic_update_slice_in_dim(final, theirs[n], (me ^ k ^ 1) * rows, 1)
        return final.transpose(0, 2, 1, 3)

    blocks = len(across)
    where = [(0, 0)] + [(1, plane) for plane in range(planes - 2)] + [(0, 1)]
    middle = tuple(tuple(where[plane - 1 : plane + 2]) for plane in range(1, planes - 1))
    inside = send_back(convolve(middle, [outer, inner], tap_parts, bias, blocks))
    up = [(i, i + 1) for i in range(slabs - 1)]
    down = [(i + 1, i) for i in range(slabs - 1)]
    first, last = edges_of(arrived)
    after = lax.ppermute(first, "slab", down)
    before = lax.ppermute(last, "slab", up)

    ends = (((2, 0), *where[:2]), (*where[-2:], (3, 0)))
    outside = send_back(convolve(ends, [outer, inner, settle(before), settle(after)], tap_parts, bias, blocks))
    inside, outside = lax.optimization_barrier((inside, outside))
    return jnp.concatenate([outside[:1], inside, outside[1:]])


def solution(mesh):
    placed = (P("slab", "filt", None, None), P(None, None, None, "filt", None), P())
    return jax.shard_map(
        body, mesh=mesh, in_specs=placed, out_specs=P("slab", "filt", None, None), check_vma=False
    )
```

```python
import functools

import jax
import jax.numpy as jnp
from jax import lax
from jax.experimental import pallas as pl
from jax.experimental.pallas import tpu as pltpu
from jax.sharding import PartitionSpec as P

slope = 0.3
ROWS = 4


def cut_kernel(parts, vol_ref, out):
    planes, y_cells = vol_ref.shape[:2]
    rows = y_cells // parts
    for block in range(parts):
        for r in range(rows + 2):
            row = block * rows + r - 1
            for plane in range(planes):
                line = vol_ref[plane, min(max(row, 0), y_cells - 1)]
                out[block, plane, r] = line if 0 <= row < y_cells else jnp.zeros_like(line)


def cut(planes, parts):
    volume = planes.transpose(0, 2, 1, 3)
    count, y_cells, chan, cols = volume.shape
    in_vmem = pl.BlockSpec(memory_space=pltpu.VMEM)
    return pl.pallas_call(
        functools.partial(cut_kernel, parts),
        out_shape=jax.ShapeDtypeStruct((parts, count, y_cells // parts + 2, chan, cols), volume.dtype),
        in_specs=[in_vmem],
        out_specs=in_vmem,
        compiler_params=pltpu.CompilerParams(vmem_limit_bytes=6 * 2**20),
    )(volume)


def edges_kernel(vol_ref, first, last):
    for s in range(vol_ref.shape[0]):
        for r in range(vol_ref.shape[2]):
            first[s, 0, r] = vol_ref[s, 0, r]
            last[s, 0, r] = vol_ref[s, 1, r]


def edges_of(volume):
    sources, _, rows_in, chan, cols = volume.shape
    in_vmem = pl.BlockSpec(memory_space=pltpu.VMEM)
    return pl.pallas_call(
        edges_kernel,
        out_shape=[jax.ShapeDtypeStruct((sources, 1, rows_in, chan, cols), volume.dtype)] * 2,
        in_specs=[in_vmem],
        out_specs=[in_vmem] * 2,
        compiler_params=pltpu.CompilerParams(vmem_limit_bytes=4 * 2**20),
    )(volume)


def conv_kernel(plan, rows_at_once, pieces_count, tap_count, *refs):
    refs = list(refs)
    pieces = [refs.pop(0) for _ in range(pieces_count)]
    tap_parts = [refs.pop(0) for _ in range(tap_count)]
    bias_ref, outs = refs[0], refs[1:]
    rows_in, cols = pieces[0].shape[2], pieces[0].shape[4]
    rows = rows_in - 2
    total_out = bias_ref.shape[0]
    block = total_out // len(outs)
    groups, size = tap_parts[0].shape[0], tap_parts[0].shape[4]
    lane = lax.broadcasted_iota(jnp.int32, (total_out, cols), 1)

    def tile(slot, row):
        cells = []
        weights = []
        for a, (source, plane) in enumerate(plan[slot]):
            piece = pieces[source]
            lines = [
                jnp.concatenate([piece[s, plane, row + r] for s in range(piece.shape[0])], axis=0)
                for r in range(rows_at_once + 2)
            ]
            for b in range(3):
                cells.append(jnp.concatenate(lines[b : b + rows_at_once], axis=1))
                weights.append(
                    jnp.concatenate(
                        [part[g, a, b].reshape(3 * size, -1) for g in range(groups) for part in tap_parts], axis=0
                    )
                )
        total = jnp.dot(
            jnp.concatenate(weights, axis=1), jnp.concatenate(cells, axis=0), preferred_element_type=jnp.float32
        )
        for r in range(rows_at_once):
            part = total[:, r * cols : (r + 1) * cols].reshape(groups * tap_count, 3, size, cols)
            side = [part[:, c].reshape(total_out, cols) for c in range(3)]
            left = jnp.where(lane == 0, 0.0, pltpu.roll(side[0], 1, 1))
            right = jnp.where(lane == cols - 1, 0.0, pltpu.roll(side[2], cols - 1, 1))
            shifted = side[1] + left + right + bias_ref[...]
            done = jnp.where(shifted > 0, shifted, slope * shifted).astype(jnp.bfloat16)
            for n, out_ref in enumerate(outs):
                out_ref[slot, row + r] = done[n * block : (n + 1) * block]

    for slot in range(len(plan)):
        for row in range(0, rows, rows_at_once):
            tile(slot, row)


def convolve(plan, pieces, tap_parts, bias, blocks):
    rows, cols = pieces[0].shape[2] - 2, pieces[0].shape[4]
    in_chan = tap_parts[0].shape[5]
    total_out = bias.shape[0]
    wide_bias = jnp.broadcast_to(bias[:, None], (total_out, cols))
    macs = 27 * total_out * in_chan * len(plan) * rows * cols
    in_vmem = pl.BlockSpec(memory_space=pltpu.VMEM)
    shape = jax.ShapeDtypeStruct((len(plan), rows, total_out // blocks, cols), jnp.bfloat16)
    return pl.pallas_call(
        functools.partial(conv_kernel, plan, min(ROWS, rows), len(pieces), len(tap_parts)),
        out_shape=[shape] * blocks,
        in_specs=[in_vmem] * (len(pieces) + len(tap_parts) + 1),
        out_specs=[in_vmem] * blocks,
        cost_estimate=pl.CostEstimate(flops=2 * macs, bytes_accessed=10_000_000, transcendentals=0),
        compiler_params=pltpu.CompilerParams(vmem_limit_bytes=16 * 2**20),
    )(*pieces, *tap_parts, wide_bias)


def body(features, kernel, bias_vector):
    planes, chan, y_cells, cols = features.shape
    out_chan = kernel.shape[3]
    parts = lax.axis_size("filt")
    slabs = lax.axis_size("slab")
    me = lax.axis_index("filt")
    rows = y_cells // parts
    aligned = chan % 16 == 0 and out_chan % 16 == 0
    across = list(range(0, parts, 2))

    def swap(array, k, axis="filt"):
        if k == 0:
            return array
        return lax.ppermute(array, axis, [(i, i ^ k) for i in range(lax.axis_size(axis))])


    near = [swap(kernel, k) for k in across[1 : 3 if len(across) == 4 else None]]
    if len(across) == 4:
        half = out_chan // 2
        by_x, by_y = near
        far = [swap(by_x[:, :, :, :half], across[2]), swap(by_y[:, :, :, half:], across[1])]
        fetched = [kernel, by_x, by_y, jnp.concatenate(far, axis=3)]
    else:
        fetched = [kernel, *near]
    same = jnp.stack(fetched)
    tap_parts = [same, swap(same, 1)]

    outer = lax.all_to_all(cut(jnp.concatenate([features[:1], features[-1:]]), parts), "filt", 0, 0)
    between = lax.optimization_barrier((features[1:-1], near))[0]
    inner = lax.all_to_all(cut(between, parts), "filt", 0, 0)
    arrived = outer
    order = jnp.stack([me ^ k ^ c for k in across for c in range(2)])
    bias = jnp.take(bias_vector.reshape(parts, out_chan), order, axis=0).reshape(-1)
    def settle(array):
        if aligned:
            return array
        return array.transpose(1, 2, 0, 3, 4).reshape(1, -1, rows + 2, parts * chan, cols)

    if not aligned:
        joined = jnp.stack(tap_parts, axis=1).transpose(2, 3, 4, 0, 1, 5, 6)
        tap_parts = [joined.reshape(1, 3, 3, 3, parts * out_chan, -1)]
        outer, inner = settle(outer), settle(inner)

    def send_back(results):
        count = results[0].shape[0]
        got = [swap(result, k) for result, k in zip(results, across)]
        mine = [block[:, :, :out_chan] for block in got]
        theirs = swap(jnp.stack([block[:, :, out_chan:] for block in got]), 1)
        final = jnp.zeros((count, y_cells, out_chan, cols), jnp.bfloat16)
        for n, k in enumerate(across):
            final = lax.dynamic_update_slice_in_dim(final, mine[n], (me ^ k) * rows, 1)
            final = lax.dynamic_update_slice_in_dim(final, theirs[n], (me ^ k ^ 1) * rows, 1)
        return final.transpose(0, 2, 1, 3)

    blocks = len(across)
    where = [(0, 0)] + [(1, plane) for plane in range(planes - 2)] + [(0, 1)]
    middle = tuple(tuple(where[plane - 1 : plane + 2]) for plane in range(1, planes - 1))
    inside = send_back(convolve(middle, [outer, inner], tap_parts, bias, blocks))
    up = [(i, i + 1) for i in range(slabs - 1)]
    down = [(i + 1, i) for i in range(slabs - 1)]
    first, last = edges_of(arrived)
    after = lax.ppermute(first, "slab", down)
    before = lax.ppermute(last, "slab", up)

    ends = (((2, 0), *where[:2]), (*where[-2:], (3, 0)))
    outside = send_back(convolve(ends, [outer, inner, settle(before), settle(after)], tap_parts, bias, blocks))
    inside, outside = lax.optimization_barrier((inside, outside))
    return jnp.concatenate([outside[:1], inside, outside[1:]])


def solution(mesh):
    placed = (P("slab", "filt", None, None), P(None, None, None, "filt", None), P())
    return jax.shard_map(
        body, mesh=mesh, in_specs=placed, out_specs=P("slab", "filt", None, None), check_vma=False
    )
```

```python
import functools

import jax
import jax.numpy as jnp
from jax import lax
from jax.experimental import pallas as pl
from jax.experimental.pallas import tpu as pltpu
from jax.sharding import PartitionSpec as P

slope = 0.3
ROWS = 4


def cut_kernel(parts, vol_ref, out):
    planes, y_cells = vol_ref.shape[:2]
    rows = y_cells // parts
    for block in range(parts):
        for r in range(rows + 2):
            row = block * rows + r - 1
            for plane in range(planes):
                line = vol_ref[plane, min(max(row, 0), y_cells - 1)]
                out[block, plane, r] = line if 0 <= row < y_cells else jnp.zeros_like(line)


def cut(planes, parts):
    volume = planes.transpose(0, 2, 1, 3)
    count, y_cells, chan, cols = volume.shape
    in_vmem = pl.BlockSpec(memory_space=pltpu.VMEM)
    return pl.pallas_call(
        functools.partial(cut_kernel, parts),
        out_shape=jax.ShapeDtypeStruct((parts, count, y_cells // parts + 2, chan, cols), volume.dtype),
        in_specs=[in_vmem],
        out_specs=in_vmem,
        compiler_params=pltpu.CompilerParams(vmem_limit_bytes=6 * 2**20),
    )(volume)


def edges_kernel(vol_ref, first, last):
    for s in range(vol_ref.shape[0]):
        for r in range(vol_ref.shape[2]):
            first[s, 0, r] = vol_ref[s, 0, r]
            last[s, 0, r] = vol_ref[s, 1, r]


def edges_of(volume):
    sources, _, rows_in, chan, cols = volume.shape
    in_vmem = pl.BlockSpec(memory_space=pltpu.VMEM)
    return pl.pallas_call(
        edges_kernel,
        out_shape=[jax.ShapeDtypeStruct((sources, 1, rows_in, chan, cols), volume.dtype)] * 2,
        in_specs=[in_vmem],
        out_specs=[in_vmem] * 2,
        compiler_params=pltpu.CompilerParams(vmem_limit_bytes=4 * 2**20),
    )(volume)


def conv_kernel(plan, rows_at_once, pieces_count, tap_count, order, *refs):
    refs = list(refs)
    pieces = [refs.pop(0) for _ in range(pieces_count)]
    tap_parts = [refs.pop(0) for _ in range(tap_count)]
    bias_ref, outs = refs[0], refs[1:]
    rows_in, cols = pieces[0].shape[2], pieces[0].shape[4]
    rows = rows_in - 2
    total_out = bias_ref.shape[0]
    block = total_out // len(outs)
    size = tap_parts[0].shape[4]
    lane = lax.broadcasted_iota(jnp.int32, (total_out, cols), 1)

    def tile(slot, row):
        cells = []
        weights = []
        for a, (source, plane) in enumerate(plan[slot]):
            piece = pieces[source]
            lines = [
                jnp.concatenate([piece[s, plane, row + r] for s in range(piece.shape[0])], axis=0)
                for r in range(rows_at_once + 2)
            ]
            for b in range(3):
                cells.append(jnp.concatenate(lines[b : b + rows_at_once], axis=1))
                weights.append(
                    jnp.concatenate(
                        [tap_parts[n][g, a, b].reshape(3 * size, -1) for n, g in order], axis=0
                    )
                )
        total = jnp.dot(
            jnp.concatenate(weights, axis=1), jnp.concatenate(cells, axis=0), preferred_element_type=jnp.float32
        )
        for r in range(rows_at_once):
            part = total[:, r * cols : (r + 1) * cols].reshape(len(order), 3, size, cols)
            side = [part[:, c].reshape(total_out, cols) for c in range(3)]
            left = jnp.where(lane == 0, 0.0, pltpu.roll(side[0], 1, 1))
            right = jnp.where(lane == cols - 1, 0.0, pltpu.roll(side[2], cols - 1, 1))
            shifted = side[1] + left + right + bias_ref[...]
            done = jnp.where(shifted > 0, shifted, slope * shifted).astype(jnp.bfloat16)
            for n, out_ref in enumerate(outs):
                out_ref[slot, row + r] = done[n * block : (n + 1) * block]

    for slot in range(len(plan)):
        for row in range(0, rows, rows_at_once):
            tile(slot, row)


def convolve(plan, pieces, tap_parts, tap_order, bias, blocks):
    rows, cols = pieces[0].shape[2] - 2, pieces[0].shape[4]
    in_chan = tap_parts[0].shape[5]
    total_out = bias.shape[0]
    wide_bias = jnp.broadcast_to(bias[:, None], (total_out, cols))
    macs = 27 * total_out * in_chan * len(plan) * rows * cols
    in_vmem = pl.BlockSpec(memory_space=pltpu.VMEM)
    shape = jax.ShapeDtypeStruct((len(plan), rows, total_out // blocks, cols), jnp.bfloat16)
    return pl.pallas_call(
        functools.partial(conv_kernel, plan, min(ROWS, rows), len(pieces), len(tap_parts), tap_order),
        out_shape=[shape] * blocks,
        in_specs=[in_vmem] * (len(pieces) + len(tap_parts) + 1),
        out_specs=[in_vmem] * blocks,
        cost_estimate=pl.CostEstimate(flops=2 * macs, bytes_accessed=10_000_000, transcendentals=0),
        compiler_params=pltpu.CompilerParams(vmem_limit_bytes=16 * 2**20),
    )(*pieces, *tap_parts, wide_bias)


def body(features, kernel, bias_vector):
    planes, chan, y_cells, cols = features.shape
    out_chan = kernel.shape[3]
    parts = lax.axis_size("filt")
    slabs = lax.axis_size("slab")
    me = lax.axis_index("filt")
    rows = y_cells // parts
    aligned = chan % 16 == 0 and out_chan % 16 == 0
    across = list(range(0, parts, 2))

    def swap(array, k, axis="filt"):
        if k == 0:
            return array
        return lax.ppermute(array, axis, [(i, i ^ k) for i in range(lax.axis_size(axis))])


    half = out_chan // 2
    odd = lax.axis_index("slab") % 2
    mine = lax.dynamic_slice_in_dim(kernel, odd * half, half, 3)
    mine = [swap(mine, k) for k in across[1:]]
    outer = lax.all_to_all(cut(jnp.concatenate([features[:1], features[-1:]]), parts), "filt", 0, 0)
    between = lax.optimization_barrier((features[1:-1], mine))[0]
    inner = lax.all_to_all(cut(between, parts), "filt", 0, 0)
    mine = jnp.stack(mine)
    theirs = lax.optimization_barrier((swap(mine, 1, "slab"), outer))[0]
    rest = jnp.concatenate([jnp.where(odd == 0, mine, theirs), jnp.where(odd == 0, theirs, mine)], axis=4)
    same = jnp.concatenate([kernel[None], rest])
    tap_parts = [same, swap(same, 1)]
    tap_order = tuple((n, g) for g in range(len(across)) for n in range(2))
    arrived = outer
    order = jnp.stack([me ^ k ^ c for k in across for c in range(2)])
    bias = jnp.take(bias_vector.reshape(parts, out_chan), order, axis=0).reshape(-1)
    def settle(array):
        if aligned:
            return array
        return array.transpose(1, 2, 0, 3, 4).reshape(1, -1, rows + 2, parts * chan, cols)

    if not aligned:
        joined = jnp.stack([tap_parts[n][g] for n, g in tap_order]).transpose(1, 2, 3, 0, 4, 5)
        tap_parts = [joined.reshape(1, 3, 3, 3, parts * out_chan, -1)]
        tap_order = ((0, 0),)

    def send_back(results):
        count = results[0].shape[0]
        got = [swap(result, k) for result, k in zip(results, across)]
        mine = [block[:, :, :out_chan] for block in got]
        theirs = swap(jnp.stack([block[:, :, out_chan:] for block in got]), 1)
        final = jnp.zeros((count, y_cells, out_chan, cols), jnp.bfloat16)
        for n, k in enumerate(across):
            final = lax.dynamic_update_slice_in_dim(final, mine[n], (me ^ k) * rows, 1)
            final = lax.dynamic_update_slice_in_dim(final, theirs[n], (me ^ k ^ 1) * rows, 1)
        return final.transpose(0, 2, 1, 3)

    blocks = len(across)
    where = [(0, 0)] + [(1, plane) for plane in range(planes - 2)] + [(0, 1)]
    middle = tuple(tuple(where[plane - 1 : plane + 2]) for plane in range(1, planes - 1))
    results = convolve(middle, [outer, inner], tap_parts, tap_order, bias, blocks)
    inside = send_back(results)
    later_bias = lax.optimization_barrier((bias, results))[0]
    up = [(i, i + 1) for i in range(slabs - 1)]
    down = [(i + 1, i) for i in range(slabs - 1)]
    first, last = edges_of(arrived)
    after = lax.ppermute(first, "slab", down)
    before = lax.ppermute(last, "slab", up)

    ends = (((2, 0), *where[:2]), (*where[-2:], (3, 0)))
    outside = send_back(convolve(ends, [outer, inner, settle(before), settle(after)], tap_parts, tap_order, later_bias, blocks))
    inside, outside = lax.optimization_barrier((inside, outside))
    return jnp.concatenate([outside[:1], inside, outside[1:]])


def solution(mesh):
    placed = (P("slab", "filt", None, None), P(None, None, None, "filt", None), P())
    return jax.shard_map(
        body, mesh=mesh, in_specs=placed, out_specs=P("slab", "filt", None, None), check_vma=False
    )
```

```python
import functools

import jax
import jax.numpy as jnp
from jax import lax
from jax.experimental import pallas as pl
from jax.experimental.pallas import tpu as pltpu
from jax.sharding import PartitionSpec as P

slope = 0.3
ROWS = 4


def cut_kernel(parts, vol_ref, out):
    planes, y_cells = vol_ref.shape[:2]
    rows = y_cells // parts
    for block in range(parts):
        for r in range(rows + 2):
            row = block * rows + r - 1
            for plane in range(planes):
                line = vol_ref[plane, min(max(row, 0), y_cells - 1)]
                out[block, plane, r] = line if 0 <= row < y_cells else jnp.zeros_like(line)


def cut(planes, parts):
    volume = planes.transpose(0, 2, 1, 3)
    count, y_cells, chan, cols = volume.shape
    in_vmem = pl.BlockSpec(memory_space=pltpu.VMEM)
    return pl.pallas_call(
        functools.partial(cut_kernel, parts),
        out_shape=jax.ShapeDtypeStruct((parts, count, y_cells // parts + 2, chan, cols), volume.dtype),
        in_specs=[in_vmem],
        out_specs=in_vmem,
        compiler_params=pltpu.CompilerParams(vmem_limit_bytes=6 * 2**20),
    )(volume)


def edges_kernel(vol_ref, first, last):
    for s in range(vol_ref.shape[0]):
        for r in range(vol_ref.shape[2]):
            first[s, 0, r] = vol_ref[s, 0, r]
            last[s, 0, r] = vol_ref[s, 1, r]


def edges_of(volume):
    sources, _, rows_in, chan, cols = volume.shape
    in_vmem = pl.BlockSpec(memory_space=pltpu.VMEM)
    return pl.pallas_call(
        edges_kernel,
        out_shape=[jax.ShapeDtypeStruct((sources, 1, rows_in, chan, cols), volume.dtype)] * 2,
        in_specs=[in_vmem],
        out_specs=[in_vmem] * 2,
        compiler_params=pltpu.CompilerParams(vmem_limit_bytes=4 * 2**20),
    )(volume)


def conv_kernel(plan, rows_at_once, sums_count, pieces_count, tap_count, order, final, *refs):
    refs = list(refs)
    sums = [refs.pop(0) for _ in range(sums_count)]
    pieces = [refs.pop(0) for _ in range(pieces_count)]
    tap_parts = [refs.pop(0) for _ in range(tap_count)]
    bias_ref, outs = refs[0], refs[1:]
    rows_in, cols = pieces[0].shape[2], pieces[0].shape[4]
    rows = rows_in - 2
    total_out = bias_ref.shape[0]
    block = total_out // len(outs)
    size = tap_parts[0].shape[4]
    lane = lax.broadcasted_iota(jnp.int32, (total_out, cols), 1)

    def tile(slot, row):
        cells = []
        weights = []
        for a, source, plane in plan[slot]:
            piece = pieces[source]
            lines = [
                jnp.concatenate([piece[s, plane, row + r] for s in range(piece.shape[0])], axis=0)
                for r in range(rows_at_once + 2)
            ]
            for b in range(3):
                cells.append(jnp.concatenate(lines[b : b + rows_at_once], axis=1))
                weights.append(
                    jnp.concatenate(
                        [tap_parts[n][g, a, b].reshape(3 * size, -1) for n, g in order], axis=0
                    )
                )
        total = jnp.dot(
            jnp.concatenate(weights, axis=1), jnp.concatenate(cells, axis=0), preferred_element_type=jnp.float32
        )
        for r in range(rows_at_once):
            part = total[:, r * cols : (r + 1) * cols].reshape(len(order), 3, size, cols)
            side = [part[:, c].reshape(total_out, cols) for c in range(3)]
            left = jnp.where(lane == 0, 0.0, pltpu.roll(side[0], 1, 1))
            right = jnp.where(lane == cols - 1, 0.0, pltpu.roll(side[2], cols - 1, 1))
            found = side[1] + left + right
            if sums:
                found = found + sums[0][slot, row + r]
            if not final:
                outs[0][slot, row + r] = found
                continue
            shifted = found + bias_ref[...]
            done = jnp.where(shifted > 0, shifted, slope * shifted).astype(jnp.bfloat16)
            for n, out_ref in enumerate(outs):
                out_ref[slot, row + r] = done[n * block : (n + 1) * block]

    for slot in range(len(plan)):
        for row in range(0, rows, rows_at_once):
            tile(slot, row)


def convolve(plan, sums, pieces, tap_parts, tap_order, bias, blocks):
    rows, cols = pieces[0].shape[2] - 2, pieces[0].shape[4]
    in_chan = tap_parts[0].shape[5]
    total_out = bias.shape[0]
    wide_bias = jnp.broadcast_to(bias[:, None], (total_out, cols))
    macs = 9 * total_out * in_chan * sum(len(terms) for terms in plan) * rows * cols
    in_vmem = pl.BlockSpec(memory_space=pltpu.VMEM)
    if blocks:
        shapes = [jax.ShapeDtypeStruct((len(plan), rows, total_out // blocks, cols), jnp.bfloat16)] * blocks
    else:
        shapes = [jax.ShapeDtypeStruct((len(plan), rows, total_out, cols), jnp.float32)]
    return pl.pallas_call(
        functools.partial(
            conv_kernel, plan, min(ROWS, rows), len(sums), len(pieces), len(tap_parts), tap_order, bool(blocks)
        ),
        out_shape=shapes,
        in_specs=[in_vmem] * (len(sums) + len(pieces) + len(tap_parts) + 1),
        out_specs=[in_vmem] * len(shapes),
        cost_estimate=pl.CostEstimate(flops=2 * macs, bytes_accessed=10_000_000, transcendentals=0),
        compiler_params=pltpu.CompilerParams(vmem_limit_bytes=16 * 2**20),
    )(*sums, *pieces, *tap_parts, wide_bias)


def body(features, kernel, bias_vector):
    planes, chan, y_cells, cols = features.shape
    out_chan = kernel.shape[3]
    parts = lax.axis_size("filt")
    slabs = lax.axis_size("slab")
    me = lax.axis_index("filt")
    rows = y_cells // parts
    aligned = chan % 16 == 0 and out_chan % 16 == 0
    across = list(range(0, parts, 2))

    def swap(array, k, axis="filt"):
        if k == 0:
            return array
        return lax.ppermute(array, axis, [(i, i ^ k) for i in range(lax.axis_size(axis))])


    near = [swap(kernel, k) for k in across[1 : 3 if len(across) == 4 else None]]
    outer = lax.all_to_all(cut(jnp.concatenate([features[:1], features[-1:]]), parts), "filt", 0, 0)
    between = lax.optimization_barrier((features[1:-1], near))[0]
    inner_rows = cut(between, parts)
    inner = lax.all_to_all(inner_rows, "filt", 0, 0)
    same = jnp.stack([kernel, *near])
    tap_parts = [same, swap(same, 1)]
    tap_order = tuple((n, g) for g in range(len(near) + 1) for n in range(2))
    if len(across) == 4:
        half = out_chan // 2
        by_x, by_y = lax.optimization_barrier((near, inner_rows))[0]
        far = [swap(by_x[:, :, :, :half], across[2]), swap(by_y[:, :, :, half:], across[1])]
        far = jnp.concatenate(far, axis=3)[None]
        tap_parts += [far, swap(far, 1)]
        tap_order += ((2, 0), (3, 0))
    arrived = outer
    order = jnp.stack([me ^ k ^ c for k in across for c in range(2)])
    bias = jnp.take(bias_vector.reshape(parts, out_chan), order, axis=0).reshape(-1)
    def settle(array):
        if aligned:
            return array
        return array.transpose(1, 2, 0, 3, 4).reshape(1, -1, rows + 2, parts * chan, cols)

    if not aligned:
        joined = jnp.stack([tap_parts[n][g] for n, g in tap_order]).transpose(1, 2, 3, 0, 4, 5)
        tap_parts = [joined.reshape(1, 3, 3, 3, parts * out_chan, -1)]
        tap_order = ((0, 0),)

    def send_back(results):
        count = results[0].shape[0]
        got = [swap(result, k) for result, k in zip(results, across)]
        mine = [block[:, :, :out_chan] for block in got]
        theirs = swap(jnp.stack([block[:, :, out_chan:] for block in got]), 1)
        final = jnp.zeros((count, y_cells, out_chan, cols), jnp.bfloat16)
        for n, k in enumerate(across):
            final = lax.dynamic_update_slice_in_dim(final, mine[n], (me ^ k) * rows, 1)
            final = lax.dynamic_update_slice_in_dim(final, theirs[n], (me ^ k ^ 1) * rows, 1)
        return final.transpose(0, 2, 1, 3)

    blocks = len(across)
    where = [(0, 0)] + [(1, plane) for plane in range(planes - 2)] + [(0, 1)]

    def terms(plane, taps):
        return tuple((a, *where[plane + a - 1]) for a in taps)

    inside_planes = range(1, planes - 1)
    begun = tuple(terms(plane, [a for a in range(3) if plane + a - 1 in (0, planes - 1)]) for plane in inside_planes)
    rest = tuple(terms(plane, [a for a in range(3) if 0 < plane + a - 1 < planes - 1]) for plane in inside_planes)
    rest = tuple(tuple((a, n - 1, p) for a, n, p in found) for found in rest)
    early = convolve(begun, [], [outer], tap_parts, tap_order, bias, 0)
    results = convolve(rest, early, [inner], tap_parts, tap_order, bias, blocks)
    inside = send_back(results)
    later_bias = lax.optimization_barrier((bias, results))[0]
    up = [(i, i + 1) for i in range(slabs - 1)]
    down = [(i + 1, i) for i in range(slabs - 1)]
    first, last = edges_of(arrived)
    after = lax.ppermute(first, "slab", down)
    before = lax.ppermute(last, "slab", up)

    ends = ((0, 2, 0), *terms(0, [1, 2])), (*terms(planes - 1, [0, 1]), (2, 3, 0))
    outside = send_back(convolve(ends, [], [outer, inner, settle(before), settle(after)], tap_parts, tap_order, later_bias, blocks))
    inside, outside = lax.optimization_barrier((inside, outside))
    return jnp.concatenate([outside[:1], inside, outside[1:]])


def solution(mesh):
    placed = (P("slab", "filt", None, None), P(None, None, None, "filt", None), P())
    return jax.shard_map(
        body, mesh=mesh, in_specs=placed, out_specs=P("slab", "filt", None, None), check_vma=False
    )
```

```python
import functools

import jax
import jax.numpy as jnp
from jax import lax
from jax.experimental import pallas as pl
from jax.experimental.pallas import tpu as pltpu
from jax.sharding import PartitionSpec as P

slope = 0.3
ROWS = 4


def cut_kernel(parts, vol_ref, out):
    planes, y_cells = vol_ref.shape[:2]
    rows = y_cells // parts
    for block in range(parts):
        for r in range(rows + 2):
            row = block * rows + r - 1
            for plane in range(planes):
                line = vol_ref[plane, min(max(row, 0), y_cells - 1)]
                out[block, plane, r] = line if 0 <= row < y_cells else jnp.zeros_like(line)


def cut(planes, parts):
    volume = planes.transpose(0, 2, 1, 3)
    count, y_cells, chan, cols = volume.shape
    in_vmem = pl.BlockSpec(memory_space=pltpu.VMEM)
    return pl.pallas_call(
        functools.partial(cut_kernel, parts),
        out_shape=jax.ShapeDtypeStruct((parts, count, y_cells // parts + 2, chan, cols), volume.dtype),
        in_specs=[in_vmem],
        out_specs=in_vmem,
        compiler_params=pltpu.CompilerParams(vmem_limit_bytes=6 * 2**20),
    )(volume)


def edges_kernel(vol_ref, first, last):
    for s in range(vol_ref.shape[0]):
        for r in range(vol_ref.shape[2]):
            first[s, 0, r] = vol_ref[s, 0, r]
            last[s, 0, r] = vol_ref[s, 1, r]


def edges_of(volume):
    sources, _, rows_in, chan, cols = volume.shape
    in_vmem = pl.BlockSpec(memory_space=pltpu.VMEM)
    return pl.pallas_call(
        edges_kernel,
        out_shape=[jax.ShapeDtypeStruct((sources, 1, rows_in, chan, cols), volume.dtype)] * 2,
        in_specs=[in_vmem],
        out_specs=[in_vmem] * 2,
        compiler_params=pltpu.CompilerParams(vmem_limit_bytes=4 * 2**20),
    )(volume)


def conv_kernel(plan, rows_at_once, sums_count, pieces_count, tap_count, order, final, *refs):
    refs = list(refs)
    sums = [refs.pop(0) for _ in range(sums_count)]
    pieces = [refs.pop(0) for _ in range(pieces_count)]
    tap_parts = [refs.pop(0) for _ in range(tap_count)]
    bias_ref, outs = refs[0], refs[1:]
    rows_in, cols = pieces[0].shape[2], pieces[0].shape[4]
    rows = rows_in - 2
    total_out = bias_ref.shape[0]
    block = total_out // len(outs)
    size = tap_parts[0].shape[4]
    lane = lax.broadcasted_iota(jnp.int32, (total_out, cols), 1)

    def tile(slot, row):
        cells = []
        weights = []
        for a, source, plane in plan[slot]:
            piece = pieces[source]
            lines = [
                jnp.concatenate([piece[s, plane, row + r] for s in range(piece.shape[0])], axis=0)
                for r in range(rows_at_once + 2)
            ]
            for b in range(3):
                cells.append(jnp.concatenate(lines[b : b + rows_at_once], axis=1))
                weights.append(
                    jnp.concatenate(
                        [tap_parts[n][g, a, b].reshape(3 * size, -1) for n, g in order], axis=0
                    )
                )
        total = jnp.dot(
            jnp.concatenate(weights, axis=1), jnp.concatenate(cells, axis=0), preferred_element_type=jnp.float32
        )
        for r in range(rows_at_once):
            part = total[:, r * cols : (r + 1) * cols].reshape(len(order), 3, size, cols)
            side = [part[:, c].reshape(total_out, cols) for c in range(3)]
            left = jnp.where(lane == 0, 0.0, pltpu.roll(side[0], 1, 1))
            right = jnp.where(lane == cols - 1, 0.0, pltpu.roll(side[2], cols - 1, 1))
            found = side[1] + left + right
            if sums:
                found = found + sums[0][slot, row + r]
            if not final:
                outs[0][slot, row + r] = found
                continue
            shifted = found + bias_ref[...]
            done = jnp.where(shifted > 0, shifted, slope * shifted).astype(jnp.bfloat16)
            for n, out_ref in enumerate(outs):
                out_ref[slot, row + r] = done[n * block : (n + 1) * block]

    for slot in range(len(plan)):
        for row in range(0, rows, rows_at_once):
            tile(slot, row)


def convolve(plan, sums, pieces, tap_parts, tap_order, bias, blocks):
    rows, cols = pieces[0].shape[2] - 2, pieces[0].shape[4]
    in_chan = tap_parts[0].shape[5]
    total_out = bias.shape[0]
    wide_bias = jnp.broadcast_to(bias[:, None], (total_out, cols))
    macs = 9 * total_out * in_chan * sum(len(terms) for terms in plan) * rows * cols
    in_vmem = pl.BlockSpec(memory_space=pltpu.VMEM)
    if blocks:
        shapes = [jax.ShapeDtypeStruct((len(plan), rows, total_out // blocks, cols), jnp.bfloat16)] * blocks
    else:
        shapes = [jax.ShapeDtypeStruct((len(plan), rows, total_out, cols), jnp.float32)]
    return pl.pallas_call(
        functools.partial(
            conv_kernel, plan, min(ROWS, rows), len(sums), len(pieces), len(tap_parts), tap_order, bool(blocks)
        ),
        out_shape=shapes,
        in_specs=[in_vmem] * (len(sums) + len(pieces) + len(tap_parts) + 1),
        out_specs=[in_vmem] * len(shapes),
        cost_estimate=pl.CostEstimate(flops=2 * macs, bytes_accessed=10_000_000, transcendentals=0),
        compiler_params=pltpu.CompilerParams(vmem_limit_bytes=16 * 2**20),
    )(*sums, *pieces, *tap_parts, wide_bias)


def body(features, kernel, bias_vector):
    planes, chan, y_cells, cols = features.shape
    out_chan = kernel.shape[3]
    parts = lax.axis_size("filt")
    slabs = lax.axis_size("slab")
    me = lax.axis_index("filt")
    rows = y_cells // parts
    aligned = chan % 16 == 0 and out_chan % 16 == 0
    across = list(range(0, parts, 2))

    def swap(array, k, axis="filt"):
        if k == 0:
            return array
        return lax.ppermute(array, axis, [(i, i ^ k) for i in range(lax.axis_size(axis))])


    outer_rows = cut(jnp.concatenate([features[:1], features[-1:]]), parts)
    fetched = [swap(kernel, k) for k in across]
    fetched = lax.optimization_barrier((fetched, outer_rows))[0]
    same = jnp.stack(fetched)
    tap_parts = [same, swap(same, 1)]
    tap_order = tuple((n, g) for g in range(len(across)) for n in range(2))
    outer = lax.all_to_all(outer_rows, "filt", 0, 0)
    inner = lax.all_to_all(cut(features[1:-1], parts), "filt", 0, 0)
    arrived = outer
    order = jnp.stack([me ^ k ^ c for k in across for c in range(2)])
    bias = jnp.take(bias_vector.reshape(parts, out_chan), order, axis=0).reshape(-1)
    def settle(array):
        if aligned:
            return array
        return array.transpose(1, 2, 0, 3, 4).reshape(1, -1, rows + 2, parts * chan, cols)

    if not aligned:
        joined = jnp.stack([tap_parts[n][g] for n, g in tap_order]).transpose(1, 2, 3, 0, 4, 5)
        tap_parts = [joined.reshape(1, 3, 3, 3, parts * out_chan, -1)]
        tap_order = ((0, 0),)

    def send_back(results):
        count = results[0].shape[0]
        got = [swap(result, k) for result, k in zip(results, across)]
        mine = [block[:, :, :out_chan] for block in got]
        theirs = swap(jnp.stack([block[:, :, out_chan:] for block in got]), 1)
        final = jnp.zeros((count, y_cells, out_chan, cols), jnp.bfloat16)
        for n, k in enumerate(across):
            final = lax.dynamic_update_slice_in_dim(final, mine[n], (me ^ k) * rows, 1)
            final = lax.dynamic_update_slice_in_dim(final, theirs[n], (me ^ k ^ 1) * rows, 1)
        return final.transpose(0, 2, 1, 3)

    blocks = len(across)
    where = [(0, 0)] + [(1, plane) for plane in range(planes - 2)] + [(0, 1)]

    def terms(plane, taps):
        return tuple((a, *where[plane + a - 1]) for a in taps)

    inside_planes = range(1, planes - 1)
    begun = tuple(terms(plane, [a for a in range(3) if plane + a - 1 in (0, planes - 1)]) for plane in inside_planes)
    rest = tuple(terms(plane, [a for a in range(3) if 0 < plane + a - 1 < planes - 1]) for plane in inside_planes)
    rest = tuple(tuple((a, n - 1, p) for a, n, p in found) for found in rest)
    early = convolve(begun, [], [outer], tap_parts, tap_order, bias, 0)
    results = convolve(rest, early, [inner], tap_parts, tap_order, bias, blocks)
    inside = send_back(results)
    up = [(i, i + 1) for i in range(slabs - 1)]
    down = [(i + 1, i) for i in range(slabs - 1)]
    first, last = edges_of(arrived)
    after = lax.ppermute(first, "slab", down)
    before = lax.ppermute(last, "slab", up)

    ends = ((0, 2, 0), *terms(0, [1, 2])), (*terms(planes - 1, [0, 1]), (2, 3, 0))
    outside = send_back(convolve(ends, [], [outer, inner, settle(before), settle(after)], tap_parts, tap_order, bias, blocks))
    inside, outside = lax.optimization_barrier((inside, outside))
    return jnp.concatenate([outside[:1], inside, outside[1:]])


def solution(mesh):
    placed = (P("slab", "filt", None, None), P(None, None, None, "filt", None), P())
    return jax.shard_map(
        body, mesh=mesh, in_specs=placed, out_specs=P("slab", "filt", None, None), check_vma=False
    )
```

```python
import functools

import jax
import jax.numpy as jnp
from jax import lax
from jax.experimental import pallas as pl
from jax.experimental.pallas import tpu as pltpu
from jax.sharding import PartitionSpec as P

slope = 0.3
ROWS = 4


def cut_kernel(parts, vol_ref, out):
    planes, y_cells = vol_ref.shape[:2]
    rows = y_cells // parts
    for block in range(parts):
        for r in range(rows + 2):
            row = block * rows + r - 1
            for plane in range(planes):
                line = vol_ref[plane, min(max(row, 0), y_cells - 1)]
                out[block, plane, r] = line if 0 <= row < y_cells else jnp.zeros_like(line)


def cut(planes, parts):
    volume = planes.transpose(0, 2, 1, 3)
    count, y_cells, chan, cols = volume.shape
    in_vmem = pl.BlockSpec(memory_space=pltpu.VMEM)
    return pl.pallas_call(
        functools.partial(cut_kernel, parts),
        out_shape=jax.ShapeDtypeStruct((parts, count, y_cells // parts + 2, chan, cols), volume.dtype),
        in_specs=[in_vmem],
        out_specs=in_vmem,
        compiler_params=pltpu.CompilerParams(vmem_limit_bytes=6 * 2**20),
    )(volume)


def edges_kernel(vol_ref, first, last):
    for s in range(vol_ref.shape[0]):
        for r in range(vol_ref.shape[2]):
            first[s, 0, r] = vol_ref[s, 0, r]
            last[s, 0, r] = vol_ref[s, 1, r]


def edges_of(volume):
    sources, _, rows_in, chan, cols = volume.shape
    in_vmem = pl.BlockSpec(memory_space=pltpu.VMEM)
    return pl.pallas_call(
        edges_kernel,
        out_shape=[jax.ShapeDtypeStruct((sources, 1, rows_in, chan, cols), volume.dtype)] * 2,
        in_specs=[in_vmem],
        out_specs=[in_vmem] * 2,
        compiler_params=pltpu.CompilerParams(vmem_limit_bytes=4 * 2**20),
    )(volume)


def conv_kernel(plan, rows_at_once, pieces_count, tap_count, *refs):
    refs = list(refs)
    pieces = [refs.pop(0) for _ in range(pieces_count)]
    tap_parts = [refs.pop(0) for _ in range(tap_count)]
    bias_ref, outs = refs[0], refs[1:]
    rows_in, cols = pieces[0].shape[2], pieces[0].shape[4]
    rows = rows_in - 2
    total_out = bias_ref.shape[0]
    block = total_out // len(outs)
    groups, size = tap_parts[0].shape[0], tap_parts[0].shape[4]
    lane = lax.broadcasted_iota(jnp.int32, (total_out, cols), 1)

    def tile(slot, row):
        cells = []
        weights = []
        for a, (source, plane) in enumerate(plan[slot]):
            piece = pieces[source]
            lines = [
                jnp.concatenate([piece[s, plane, row + r] for s in range(piece.shape[0])], axis=0)
                for r in range(rows_at_once + 2)
            ]
            for b in range(3):
                cells.append(jnp.concatenate(lines[b : b + rows_at_once], axis=1))
                weights.append(
                    jnp.concatenate(
                        [part[g, a, b].reshape(3 * size, -1) for g in range(groups) for part in tap_parts], axis=0
                    )
                )
        total = jnp.dot(
            jnp.concatenate(weights, axis=1), jnp.concatenate(cells, axis=0), preferred_element_type=jnp.float32
        )
        for r in range(rows_at_once):
            part = total[:, r * cols : (r + 1) * cols].reshape(groups * tap_count, 3, size, cols)
            side = [part[:, c].reshape(total_out, cols) for c in range(3)]
            left = jnp.where(lane == 0, 0.0, pltpu.roll(side[0], 1, 1))
            right = jnp.where(lane == cols - 1, 0.0, pltpu.roll(side[2], cols - 1, 1))
            shifted = side[1] + left + right + bias_ref[...]
            done = jnp.where(shifted > 0, shifted, slope * shifted).astype(jnp.bfloat16)
            for n, out_ref in enumerate(outs):
                out_ref[slot, row + r] = done[n * block : (n + 1) * block]

    for slot in range(len(plan)):
        for row in range(0, rows, rows_at_once):
            tile(slot, row)


def convolve(plan, pieces, tap_parts, bias, blocks):
    rows, cols = pieces[0].shape[2] - 2, pieces[0].shape[4]
    in_chan = tap_parts[0].shape[5]
    total_out = bias.shape[0]
    wide_bias = jnp.broadcast_to(bias[:, None], (total_out, cols))
    macs = 27 * total_out * in_chan * len(plan) * rows * cols
    in_vmem = pl.BlockSpec(memory_space=pltpu.VMEM)
    shape = jax.ShapeDtypeStruct((len(plan), rows, total_out // blocks, cols), jnp.bfloat16)
    return pl.pallas_call(
        functools.partial(conv_kernel, plan, min(ROWS, rows), len(pieces), len(tap_parts)),
        out_shape=[shape] * blocks,
        in_specs=[in_vmem] * (len(pieces) + len(tap_parts) + 1),
        out_specs=[in_vmem] * blocks,
        cost_estimate=pl.CostEstimate(flops=2 * macs, bytes_accessed=10_000_000, transcendentals=0),
        compiler_params=pltpu.CompilerParams(vmem_limit_bytes=16 * 2**20),
    )(*pieces, *tap_parts, wide_bias)


def body(features, kernel, bias_vector):
    planes, chan, y_cells, cols = features.shape
    out_chan = kernel.shape[3]
    parts = lax.axis_size("filt")
    slabs = lax.axis_size("slab")
    me = lax.axis_index("filt")
    rows = y_cells // parts
    aligned = chan % 16 == 0 and out_chan % 16 == 0
    across = list(range(0, parts, 2))

    def swap(array, k, axis="filt"):
        if k == 0:
            return array
        return lax.ppermute(array, axis, [(i, i ^ k) for i in range(lax.axis_size(axis))])


    near = [swap(kernel, k) for k in across[1 : 3 if len(across) == 4 else None]]
    outer_rows = cut(jnp.concatenate([features[:1], features[-1:]]), parts)
    inner_rows = cut(features[1:-1], parts)
    if len(across) == 4:
        half = out_chan // 2
        by_x, by_y = near
        far = [swap(by_x[:, :, :, :half], across[2]), swap(by_y[:, :, :, half:], across[1])]
        far = lax.optimization_barrier((far, inner_rows))[0]
        near = [by_x, by_y, jnp.concatenate(far, axis=3)]
    same = jnp.stack([kernel, *near])
    tap_parts = [same, swap(same, 1)]
    outer = lax.all_to_all(outer_rows, "filt", 0, 0)
    inner = lax.all_to_all(inner_rows, "filt", 0, 0)
    arrived = outer
    order = jnp.stack([me ^ k ^ c for k in across for c in range(2)])
    bias = jnp.take(bias_vector.reshape(parts, out_chan), order, axis=0).reshape(-1)
    def settle(array):
        if aligned:
            return array
        return array.transpose(1, 2, 0, 3, 4).reshape(1, -1, rows + 2, parts * chan, cols)

    if not aligned:
        joined = jnp.stack(tap_parts, axis=1).transpose(2, 3, 4, 0, 1, 5, 6)
        tap_parts = [joined.reshape(1, 3, 3, 3, parts * out_chan, -1)]
        outer, inner = settle(outer), settle(inner)

    def send_back(results):
        count = results[0].shape[0]
        got = [swap(result, k) for result, k in zip(results, across)]
        mine = [block[:, :, :out_chan] for block in got]
        theirs = swap(jnp.stack([block[:, :, out_chan:] for block in got]), 1)
        final = jnp.zeros((count, y_cells, out_chan, cols), jnp.bfloat16)
        for n, k in enumerate(across):
            final = lax.dynamic_update_slice_in_dim(final, mine[n], (me ^ k) * rows, 1)
            final = lax.dynamic_update_slice_in_dim(final, theirs[n], (me ^ k ^ 1) * rows, 1)
        return final.transpose(0, 2, 1, 3)

    blocks = len(across)
    where = [(0, 0)] + [(1, plane) for plane in range(planes - 2)] + [(0, 1)]
    middle = tuple(tuple(where[plane - 1 : plane + 2]) for plane in range(1, planes - 1))
    inside = send_back(convolve(middle, [outer, inner], tap_parts, bias, blocks))
    up = [(i, i + 1) for i in range(slabs - 1)]
    down = [(i + 1, i) for i in range(slabs - 1)]
    first, last = edges_of(arrived)
    after = lax.ppermute(first, "slab", down)
    before = lax.ppermute(last, "slab", up)

    ends = (((2, 0), *where[:2]), (*where[-2:], (3, 0)))
    outside = send_back(convolve(ends, [outer, inner, settle(before), settle(after)], tap_parts, bias, blocks))
    inside, outside = lax.optimization_barrier((inside, outside))
    return jnp.concatenate([outside[:1], inside, outside[1:]])


def solution(mesh):
    placed = (P("slab", "filt", None, None), P(None, None, None, "filt", None), P())
    return jax.shard_map(
        body, mesh=mesh, in_specs=placed, out_specs=P("slab", "filt", None, None), check_vma=False
    )
```

```python
import functools

import jax
import jax.numpy as jnp
from jax import lax
from jax.experimental import pallas as pl
from jax.experimental.pallas import tpu as pltpu
from jax.sharding import PartitionSpec as P

slope = 0.3
ROWS = 8


def cut_kernel(parts, vol_ref, out):
    planes, y_cells = vol_ref.shape[:2]
    rows = y_cells // parts
    for block in range(parts):
        for r in range(rows + 2):
            row = block * rows + r - 1
            for plane in range(planes):
                line = vol_ref[plane, min(max(row, 0), y_cells - 1)]
                out[block, plane, r] = line if 0 <= row < y_cells else jnp.zeros_like(line)


def cut(planes, parts):
    volume = planes.transpose(0, 2, 1, 3)
    count, y_cells, chan, cols = volume.shape
    in_vmem = pl.BlockSpec(memory_space=pltpu.VMEM)
    return pl.pallas_call(
        functools.partial(cut_kernel, parts),
        out_shape=jax.ShapeDtypeStruct((parts, count, y_cells // parts + 2, chan, cols), volume.dtype),
        in_specs=[in_vmem],
        out_specs=in_vmem,
        compiler_params=pltpu.CompilerParams(vmem_limit_bytes=6 * 2**20),
    )(volume)


def edges_kernel(vol_ref, first, last):
    for s in range(vol_ref.shape[0]):
        for r in range(vol_ref.shape[2]):
            first[s, 0, r] = vol_ref[s, 0, r]
            last[s, 0, r] = vol_ref[s, 1, r]


def edges_of(volume):
    sources, _, rows_in, chan, cols = volume.shape
    in_vmem = pl.BlockSpec(memory_space=pltpu.VMEM)
    return pl.pallas_call(
        edges_kernel,
        out_shape=[jax.ShapeDtypeStruct((sources, 1, rows_in, chan, cols), volume.dtype)] * 2,
        in_specs=[in_vmem],
        out_specs=[in_vmem] * 2,
        compiler_params=pltpu.CompilerParams(vmem_limit_bytes=4 * 2**20),
    )(volume)


def conv_kernel(plan, rows_at_once, pieces_count, tap_count, *refs):
    refs = list(refs)
    pieces = [refs.pop(0) for _ in range(pieces_count)]
    tap_parts = [refs.pop(0) for _ in range(tap_count)]
    bias_ref, outs = refs[0], refs[1:]
    rows_in, cols = pieces[0].shape[2], pieces[0].shape[4]
    rows = rows_in - 2
    total_out = bias_ref.shape[0]
    block = total_out // len(outs)
    groups, size = tap_parts[0].shape[0], tap_parts[0].shape[4]
    lane = lax.broadcasted_iota(jnp.int32, (total_out, cols), 1)

    def tile(slot, row):
        cells = []
        weights = []
        for a, (source, plane) in enumerate(plan[slot]):
            piece = pieces[source]
            lines = [
                jnp.concatenate([piece[s, plane, row + r] for s in range(piece.shape[0])], axis=0)
                for r in range(rows_at_once + 2)
            ]
            for b in range(3):
                cells.append(jnp.concatenate(lines[b : b + rows_at_once], axis=1))
                weights.append(
                    jnp.concatenate(
                        [part[g, a, b].reshape(3 * size, -1) for g in range(groups) for part in tap_parts], axis=0
                    )
                )
        total = jnp.dot(
            jnp.concatenate(weights, axis=1), jnp.concatenate(cells, axis=0), preferred_element_type=jnp.float32
        )
        for r in range(rows_at_once):
            part = total[:, r * cols : (r + 1) * cols].reshape(groups * tap_count, 3, size, cols)
            side = [part[:, c].reshape(total_out, cols) for c in range(3)]
            left = jnp.where(lane == 0, 0.0, pltpu.roll(side[0], 1, 1))
            right = jnp.where(lane == cols - 1, 0.0, pltpu.roll(side[2], cols - 1, 1))
            shifted = side[1] + left + right + bias_ref[...]
            done = jnp.where(shifted > 0, shifted, slope * shifted).astype(jnp.bfloat16)
            for n, out_ref in enumerate(outs):
                out_ref[slot, row + r] = done[n * block : (n + 1) * block]

    for slot in range(len(plan)):
        for row in range(0, rows, rows_at_once):
            tile(slot, row)


def convolve(plan, pieces, tap_parts, bias, blocks):
    rows, cols = pieces[0].shape[2] - 2, pieces[0].shape[4]
    in_chan = tap_parts[0].shape[5]
    total_out = bias.shape[0]
    wide_bias = jnp.broadcast_to(bias[:, None], (total_out, cols))
    macs = 27 * total_out * in_chan * len(plan) * rows * cols
    in_vmem = pl.BlockSpec(memory_space=pltpu.VMEM)
    shape = jax.ShapeDtypeStruct((len(plan), rows, total_out // blocks, cols), jnp.bfloat16)
    return pl.pallas_call(
        functools.partial(conv_kernel, plan, min(ROWS, rows), len(pieces), len(tap_parts)),
        out_shape=[shape] * blocks,
        in_specs=[in_vmem] * (len(pieces) + len(tap_parts) + 1),
        out_specs=[in_vmem] * blocks,
        cost_estimate=pl.CostEstimate(flops=2 * macs, bytes_accessed=10_000_000, transcendentals=0),
        compiler_params=pltpu.CompilerParams(vmem_limit_bytes=16 * 2**20),
    )(*pieces, *tap_parts, wide_bias)


def body(features, kernel, bias_vector):
    planes, chan, y_cells, cols = features.shape
    out_chan = kernel.shape[3]
    parts = lax.axis_size("filt")
    slabs = lax.axis_size("slab")
    me = lax.axis_index("filt")
    rows = y_cells // parts
    aligned = chan % 16 == 0 and out_chan % 16 == 0
    across = list(range(0, parts, 2))

    def swap(array, k, axis="filt"):
        if k == 0:
            return array
        return lax.ppermute(array, axis, [(i, i ^ k) for i in range(lax.axis_size(axis))])


    near = [swap(kernel, k) for k in across[1 : 3 if len(across) == 4 else None]]
    outer_rows = cut(jnp.concatenate([features[:1], features[-1:]]), parts)
    inner_rows = cut(features[1:-1], parts)
    if len(across) == 4:
        half = out_chan // 2
        by_x, by_y = near
        far = [swap(by_x[:, :, :, :half], across[2]), swap(by_y[:, :, :, half:], across[1])]
        far = lax.optimization_barrier((far, inner_rows))[0]
        near = [by_x, by_y, jnp.concatenate(far, axis=3)]
    same = jnp.stack([kernel, *near])
    tap_parts = [same, swap(same, 1)]
    outer = lax.all_to_all(outer_rows, "filt", 0, 0)
    inner = lax.all_to_all(inner_rows, "filt", 0, 0)
    arrived = outer
    order = jnp.stack([me ^ k ^ c for k in across for c in range(2)])
    bias = jnp.take(bias_vector.reshape(parts, out_chan), order, axis=0).reshape(-1)
    def settle(array):
        if aligned:
            return array
        return array.transpose(1, 2, 0, 3, 4).reshape(1, -1, rows + 2, parts * chan, cols)

    if not aligned:
        joined = jnp.stack(tap_parts, axis=1).transpose(2, 3, 4, 0, 1, 5, 6)
        tap_parts = [joined.reshape(1, 3, 3, 3, parts * out_chan, -1)]
        outer, inner = settle(outer), settle(inner)

    def send_back(results):
        count = results[0].shape[0]
        got = [swap(result, k) for result, k in zip(results, across)]
        mine = [block[:, :, :out_chan] for block in got]
        theirs = swap(jnp.stack([block[:, :, out_chan:] for block in got]), 1)
        final = jnp.zeros((count, y_cells, out_chan, cols), jnp.bfloat16)
        for n, k in enumerate(across):
            final = lax.dynamic_update_slice_in_dim(final, mine[n], (me ^ k) * rows, 1)
            final = lax.dynamic_update_slice_in_dim(final, theirs[n], (me ^ k ^ 1) * rows, 1)
        return final.transpose(0, 2, 1, 3)

    blocks = len(across)
    where = [(0, 0)] + [(1, plane) for plane in range(planes - 2)] + [(0, 1)]
    middle = tuple(tuple(where[plane - 1 : plane + 2]) for plane in range(1, planes - 1))
    inside = send_back(convolve(middle, [outer, inner], tap_parts, bias, blocks))
    up = [(i, i + 1) for i in range(slabs - 1)]
    down = [(i + 1, i) for i in range(slabs - 1)]
    first, last = edges_of(arrived)
    after = lax.ppermute(first, "slab", down)
    before = lax.ppermute(last, "slab", up)

    ends = (((2, 0), *where[:2]), (*where[-2:], (3, 0)))
    outside = send_back(convolve(ends, [outer, inner, settle(before), settle(after)], tap_parts, bias, blocks))
    inside, outside = lax.optimization_barrier((inside, outside))
    return jnp.concatenate([outside[:1], inside, outside[1:]])


def solution(mesh):
    placed = (P("slab", "filt", None, None), P(None, None, None, "filt", None), P())
    return jax.shard_map(
        body, mesh=mesh, in_specs=placed, out_specs=P("slab", "filt", None, None), check_vma=False
    )
```

```python
import functools

import jax
import jax.numpy as jnp
from jax import lax
from jax.experimental import pallas as pl
from jax.experimental.pallas import tpu as pltpu
from jax.sharding import PartitionSpec as P

slope = 0.3
ROWS = 4


def cut_kernel(parts, vol_ref, out):
    planes, y_cells = vol_ref.shape[:2]
    rows = y_cells // parts
    for block in range(parts):
        for r in range(rows + 2):
            row = block * rows + r - 1
            for plane in range(planes):
                line = vol_ref[plane, min(max(row, 0), y_cells - 1)]
                out[block, plane, r] = line if 0 <= row < y_cells else jnp.zeros_like(line)


def cut(planes, parts):
    volume = planes.transpose(0, 2, 1, 3)
    count, y_cells, chan, cols = volume.shape
    in_vmem = pl.BlockSpec(memory_space=pltpu.VMEM)
    return pl.pallas_call(
        functools.partial(cut_kernel, parts),
        out_shape=jax.ShapeDtypeStruct((parts, count, y_cells // parts + 2, chan, cols), volume.dtype),
        in_specs=[in_vmem],
        out_specs=in_vmem,
        compiler_params=pltpu.CompilerParams(vmem_limit_bytes=6 * 2**20),
    )(volume)


def edges_kernel(vol_ref, first, last):
    for s in range(vol_ref.shape[0]):
        for r in range(vol_ref.shape[2]):
            first[s, 0, r] = vol_ref[s, 0, r]
            last[s, 0, r] = vol_ref[s, 1, r]


def edges_of(volume):
    sources, _, rows_in, chan, cols = volume.shape
    in_vmem = pl.BlockSpec(memory_space=pltpu.VMEM)
    return pl.pallas_call(
        edges_kernel,
        out_shape=[jax.ShapeDtypeStruct((sources, 1, rows_in, chan, cols), volume.dtype)] * 2,
        in_specs=[in_vmem],
        out_specs=[in_vmem] * 2,
        compiler_params=pltpu.CompilerParams(vmem_limit_bytes=4 * 2**20),
    )(volume)


def conv_kernel(plan, rows_at_once, sums_count, pieces_count, tap_count, order, final, *refs):
    refs = list(refs)
    sums = [refs.pop(0) for _ in range(sums_count)]
    pieces = [refs.pop(0) for _ in range(pieces_count)]
    tap_parts = [refs.pop(0) for _ in range(tap_count)]
    bias_ref, outs = refs[0], refs[1:]
    rows_in, cols = pieces[0].shape[2], pieces[0].shape[4]
    rows = rows_in - 2
    total_out = bias_ref.shape[0]
    block = total_out // len(outs)
    size = tap_parts[0].shape[4]
    lane = lax.broadcasted_iota(jnp.int32, (total_out, cols), 1)

    def tile(slot, row):
        cells = []
        weights = []
        for a, source, plane in plan[slot]:
            piece = pieces[source]
            lines = [
                jnp.concatenate([piece[s, plane, row + r] for s in range(piece.shape[0])], axis=0)
                for r in range(rows_at_once + 2)
            ]
            for b in range(3):
                cells.append(jnp.concatenate(lines[b : b + rows_at_once], axis=1))
                weights.append(
                    jnp.concatenate(
                        [tap_parts[n][g, a, b].reshape(3 * size, -1) for n, g in order], axis=0
                    )
                )
        total = jnp.dot(
            jnp.concatenate(weights, axis=1), jnp.concatenate(cells, axis=0), preferred_element_type=jnp.float32
        )
        for r in range(rows_at_once):
            part = total[:, r * cols : (r + 1) * cols].reshape(len(order), 3, size, cols)
            side = [part[:, c].reshape(total_out, cols) for c in range(3)]
            left = jnp.where(lane == 0, 0.0, pltpu.roll(side[0], 1, 1))
            right = jnp.where(lane == cols - 1, 0.0, pltpu.roll(side[2], cols - 1, 1))
            found = side[1] + left + right
            if sums:
                found = found + sums[0][slot, row + r]
            if not final:
                outs[0][slot, row + r] = found
                continue
            shifted = found + bias_ref[...]
            done = jnp.where(shifted > 0, shifted, slope * shifted).astype(jnp.bfloat16)
            for n, out_ref in enumerate(outs):
                out_ref[slot, row + r] = done[n * block : (n + 1) * block]

    for slot in range(len(plan)):
        for row in range(0, rows, rows_at_once):
            tile(slot, row)


def convolve(plan, sums, pieces, tap_parts, tap_order, bias, blocks):
    rows, cols = pieces[0].shape[2] - 2, pieces[0].shape[4]
    in_chan = tap_parts[0].shape[5]
    total_out = bias.shape[0]
    wide_bias = jnp.broadcast_to(bias[:, None], (total_out, cols))
    macs = 9 * total_out * in_chan * sum(len(terms) for terms in plan) * rows * cols
    in_vmem = pl.BlockSpec(memory_space=pltpu.VMEM)
    if blocks:
        shapes = [jax.ShapeDtypeStruct((len(plan), rows, total_out // blocks, cols), jnp.bfloat16)] * blocks
    else:
        shapes = [jax.ShapeDtypeStruct((len(plan), rows, total_out, cols), jnp.float32)]
    return pl.pallas_call(
        functools.partial(
            conv_kernel, plan, min(ROWS, rows), len(sums), len(pieces), len(tap_parts), tap_order, bool(blocks)
        ),
        out_shape=shapes,
        in_specs=[in_vmem] * (len(sums) + len(pieces) + len(tap_parts) + 1),
        out_specs=[in_vmem] * len(shapes),
        cost_estimate=pl.CostEstimate(flops=2 * macs, bytes_accessed=10_000_000, transcendentals=0),
        compiler_params=pltpu.CompilerParams(vmem_limit_bytes=16 * 2**20),
    )(*sums, *pieces, *tap_parts, wide_bias)


def body(features, kernel, bias_vector):
    planes, chan, y_cells, cols = features.shape
    out_chan = kernel.shape[3]
    parts = lax.axis_size("filt")
    slabs = lax.axis_size("slab")
    me = lax.axis_index("filt")
    rows = y_cells // parts
    aligned = chan % 16 == 0 and out_chan % 16 == 0
    across = list(range(0, parts, 2))

    def swap(array, k, axis="filt"):
        if k == 0:
            return array
        return lax.ppermute(array, axis, [(i, i ^ k) for i in range(lax.axis_size(axis))])


    near = [swap(kernel, k) for k in across[1 : 3 if len(across) == 4 else None]]
    outer_rows = cut(jnp.concatenate([features[:1], features[-1:]]), parts)
    inner_rows = cut(features[1:-1], parts)
    if len(across) == 4:
        half = out_chan // 2
        by_x, by_y = lax.optimization_barrier((near, outer_rows))[0]
        far = [swap(by_x[:, :, :, :half], across[2]), swap(by_y[:, :, :, half:], across[1])]
        far = lax.optimization_barrier((far, inner_rows))[0]
        near = [by_x, by_y, jnp.concatenate(far, axis=3)]
    same = jnp.stack([kernel, *near])
    tap_parts = [same, swap(same, 1)]
    tap_order = tuple((n, g) for g in range(len(across)) for n in range(2))
    outer = lax.all_to_all(outer_rows, "filt", 0, 0)
    inner = lax.all_to_all(inner_rows, "filt", 0, 0)
    arrived = outer
    order = jnp.stack([me ^ k ^ c for k in across for c in range(2)])
    bias = jnp.take(bias_vector.reshape(parts, out_chan), order, axis=0).reshape(-1)
    def settle(array):
        if aligned:
            return array
        return array.transpose(1, 2, 0, 3, 4).reshape(1, -1, rows + 2, parts * chan, cols)

    if not aligned:
        joined = jnp.stack([tap_parts[n][g] for n, g in tap_order]).transpose(1, 2, 3, 0, 4, 5)
        tap_parts = [joined.reshape(1, 3, 3, 3, parts * out_chan, -1)]
        tap_order = ((0, 0),)

    def send_back(results):
        count = results[0].shape[0]
        got = [swap(result, k) for result, k in zip(results, across)]
        mine = [block[:, :, :out_chan] for block in got]
        theirs = swap(jnp.stack([block[:, :, out_chan:] for block in got]), 1)
        final = jnp.zeros((count, y_cells, out_chan, cols), jnp.bfloat16)
        for n, k in enumerate(across):
            final = lax.dynamic_update_slice_in_dim(final, mine[n], (me ^ k) * rows, 1)
            final = lax.dynamic_update_slice_in_dim(final, theirs[n], (me ^ k ^ 1) * rows, 1)
        return final.transpose(0, 2, 1, 3)

    blocks = len(across)
    where = [(0, 0)] + [(1, plane) for plane in range(planes - 2)] + [(0, 1)]

    def terms(plane, taps):
        return tuple((a, *where[plane + a - 1]) for a in taps)

    inside_planes = range(1, planes - 1)
    begun = tuple(terms(plane, [a for a in range(3) if plane + a - 1 in (0, planes - 1)]) for plane in inside_planes)
    rest = tuple(terms(plane, [a for a in range(3) if 0 < plane + a - 1 < planes - 1]) for plane in inside_planes)
    rest = tuple(tuple((a, n - 1, p) for a, n, p in found) for found in rest)
    early = convolve(begun, [], [outer], tap_parts, tap_order, bias, 0)
    results = convolve(rest, early, [inner], tap_parts, tap_order, bias, blocks)
    inside = send_back(results)
    up = [(i, i + 1) for i in range(slabs - 1)]
    down = [(i + 1, i) for i in range(slabs - 1)]
    first, last = edges_of(arrived)
    after = lax.ppermute(first, "slab", down)
    before = lax.ppermute(last, "slab", up)

    ends = ((0, 2, 0), *terms(0, [1, 2])), (*terms(planes - 1, [0, 1]), (2, 3, 0))
    outside = send_back(convolve(ends, [], [outer, inner, settle(before), settle(after)], tap_parts, tap_order, bias, blocks))
    inside, outside = lax.optimization_barrier((inside, outside))
    return jnp.concatenate([outside[:1], inside, outside[1:]])


def solution(mesh):
    placed = (P("slab", "filt", None, None), P(None, None, None, "filt", None), P())
    return jax.shard_map(
        body, mesh=mesh, in_specs=placed, out_specs=P("slab", "filt", None, None), check_vma=False
    )
```
